32 devices in a mesh: fsdp: 16 (over z, y, core), tp: 2 (over x).
Axes of the slice: x: 2, y: 2, z: 4, core: 2. Of those that a mesh axis runs over, the one named last changes fastest.
Arguments:
- layer_in: bfloat16 [2, 8192, 2048], P(None, 'fsdp'), may hold values from -6 to 6
- out_grad: bfloat16 [2, 8192, 2048], P(None, 'fsdp'), may hold values from -6 to 6
- parents: int32 [2, 13], replicated, may hold values from 0 to 4, as said below
- seg_len: int32 [2, 13], replicated, may hold values from 1 to 1024, as said below
- attn_gain: bfloat16 [2048], P('fsdp'), may hold values from 0.5 to 1.5
- w_query: bfloat16 [2048, 2048], P('fsdp', 'tp'), may hold values from -0.25 to 0.25
- key_weight: bfloat16 [2048, 512], P('fsdp', 'tp'), may hold values from -0.125 to 0.125
- value_weight: bfloat16 [2048, 512], P('fsdp', 'tp'), may hold values from -0.125 to 0.125
- w_out: bfloat16 [2048, 2048], P('tp', 'fsdp'), may hold values from -0.75 to 0.75
- ffn_gain: bfloat16 [2048], P('fsdp'), may hold values from 0.5 to 1.5
- w_gate: bfloat16 [2048, 8192], P('fsdp', 'tp'), may hold values from -0.125 to 0.125
- w_up: bfloat16 [2048, 8192], P('fsdp', 'tp'), may hold values from -0.125 to 0.125
- w_down: bfloat16 [8192, 2048], P('tp', 'fsdp'), may hold values from -0.0625 to 0.0625
Outputs:
- output: bfloat16 [2, 8192, 2048], P(None, 'fsdp')
- input_grad: float32 [2, 8192, 2048], P(None, 'fsdp')
- attn_gain_grad: float32 [2048], P('fsdp')
- query_grad: float32 [2048, 2048], P('fsdp', 'tp')
- key_grad: float32 [2048, 512], P('fsdp', 'tp')
- value_grad: float32 [2048, 512], P('fsdp', 'tp')
- out_proj_grad: float32 [2048, 2048], P('tp', 'fsdp')
- ffn_gain_grad: float32 [2048], P('fsdp')
- gate_grad: float32 [2048, 8192], P('fsdp', 'tp')
- up_grad: float32 [2048, 8192], P('fsdp', 'tp')
- down_grad: float32 [8192, 2048], P('tp', 'fsdp')
The draws below stay inside these ranges and needn't reach their ends.
Inputs may be any that keep to these rules, and one draw needn't show every extreme that they name: Segment 0 is the trunk, its own parent; segments 1 to 4 are branches whose parent is 0; the 8 segments after them are leaves whose parents are branches, each branch the parent of one leaf or more. `seg_len`: the lengths of a tree's segments are positive and sum to 8192; the trunk's is the largest.
All inputs are finite; a program needn't handle non-finite values.
Results may differ from the reference program's by a relative error of at most 0.02.
Values may be sent and summed in bfloat16 or wider, within the bound.
A program may use at most 320 MiB of HBM per device.

```python
import math
import jax
import jax.numpy as jnp
from jax import lax

MODEL_DIMENSION = 2048
QUERY_HEADS = 32
KEY_VALUE_HEADS = 8
HEAD_SIZE = 64
FF = 8192
MB = 2
BRANCHES = 4
LEAVES = 8
LEVELS = 3
SEGMENTS = 13
TREE = 8192


def draw_parents(key, part):
    key = jax.random.fold_in(key, 11)
    result_rows = []
    for tree_index in range(MB):
        tree_key = jax.random.fold_in(key, tree_index)
        cover_key, spare_key, order_key = jax.random.split(tree_key, 3)
        covered = jax.random.permutation(cover_key, BRANCHES).astype(jnp.int32) + 1
        spare_rows = jax.random.randint(spare_key, (LEAVES - BRANCHES,), 1, BRANCHES + 1).astype(jnp.int32)
        leaf_parents = jnp.concatenate([covered, spare_rows])
        leaf_parents = leaf_parents[jax.random.permutation(order_key, LEAVES)]
        result_rows.append(jnp.concatenate([jnp.zeros((1 + BRANCHES,), jnp.int32), leaf_parents]))
    return jnp.stack(result_rows)


def draw_seg_len(key, part):
    key = jax.random.fold_in(key, 23)
    shares = jax.random.randint(key, (MB, SEGMENTS - 1), 8, 12).astype(jnp.int32)
    rest_total = TREE - TREE // 8
    share_sum = jnp.sum(shares, axis=1, keepdims=True).astype(jnp.int32)
    others = (shares * rest_total // share_sum).astype(jnp.int32)
    others = others.at[:, -1].add(rest_total - jnp.sum(others, axis=1).astype(jnp.int32))
    trunk_len = jnp.full((MB, 1), TREE // 8, jnp.int32)
    return jnp.concatenate([trunk_len, others.astype(jnp.int32)], axis=1)


def shard_levels(key, extent, cuts, smallest, largest):
    def one(axis_at, shards_of):
        steps = jax.random.uniform(jax.random.fold_in(jax.random.fold_in(key, 6), axis_at), (shards_of,), jnp.float32, smallest / len(cuts), largest / len(cuts))
        return jnp.repeat(jnp.exp(steps), extent[axis_at] // shards_of).reshape((-1,) + (1,) * (len(extent) - axis_at - 1))

    gain = one(*cuts[0])
    for cut in cuts[1:]:
        gain = gain * one(*cut)
    return gain


def bell_draw(stream_key, dims, scale, most, shards=(), held_as=jnp.bfloat16):
    drawn = scale * jax.random.normal(stream_key, dims, jnp.float32)
    if shards:
        drawn = drawn * shard_levels(stream_key, dims, shards, -0.22, 0.18)
    return jnp.clip(drawn, -most, most).astype(held_as)


def setup_inputs(seed: int = 0) -> dict:
    key_of = jax.random.split(jax.random.key(seed), 14)
    layer_in = bell_draw(key_of[0], (MB, TREE, MODEL_DIMENSION), 1.0, 6.0, ((1, 16),))
    out_grad = bell_draw(key_of[1], (MB, TREE, MODEL_DIMENSION), 1.0, 6.0, ((1, 16),))
    parents = draw_parents(jax.random.fold_in(key_of[13], 71), 0)
    seg_len = draw_seg_len(jax.random.fold_in(key_of[13], 71), 0)
    attn_gain = jnp.clip(1.0 + 0.1 * jax.random.normal(key_of[4], (MODEL_DIMENSION,), jnp.float32), 0.5, 1.5).astype(jnp.bfloat16)
    w_query = bell_draw(key_of[5], (MODEL_DIMENSION, QUERY_HEADS * HEAD_SIZE), (MODEL_DIMENSION // 4) ** -0.5, 0.25, ((0, 16), (1, 2)))
    key_weight = bell_draw(key_of[6], (MODEL_DIMENSION, KEY_VALUE_HEADS * HEAD_SIZE), MODEL_DIMENSION ** -0.5, 0.125, ((0, 16), (1, 2)))
    value_weight = bell_draw(key_of[7], (MODEL_DIMENSION, KEY_VALUE_HEADS * HEAD_SIZE), MODEL_DIMENSION ** -0.5, 0.125, ((0, 16), (1, 2)))
    w_out = bell_draw(key_of[8], (QUERY_HEADS * HEAD_SIZE, MODEL_DIMENSION), HEAD_SIZE ** -0.5, 0.75, ((0, 2), (1, 16)))
    ffn_gain = jnp.clip(1.0 + 0.1 * jax.random.normal(key_of[9], (MODEL_DIMENSION,), jnp.float32), 0.5, 1.5).astype(jnp.bfloat16)
    w_gate = bell_draw(key_of[10], (MODEL_DIMENSION, FF), MODEL_DIMENSION ** -0.5, 0.125, ((0, 16), (1, 2)))
    w_up = bell_draw(key_of[11], (MODEL_DIMENSION, FF), MODEL_DIMENSION ** -0.5, 0.125, ((0, 16), (1, 2)))
    w_down = bell_draw(key_of[12], (FF, MODEL_DIMENSION), FF ** -0.5, 0.0625, ((0, 2), (1, 16)))
    return dict(layer_in=layer_in, out_grad=out_grad, parents=parents, seg_len=seg_len, attn_gain=attn_gain, w_query=w_query, key_weight=key_weight, value_weight=value_weight, w_out=w_out, ffn_gain=ffn_gain, w_gate=w_gate, w_up=w_up, w_down=w_down)


EPS = 1e-05
THETA = 500000.0
NEG = -1e+30

@jax.custom_vjp
def lowered_copy(v):
    return lax.optimization_barrier(v.astype(jnp.bfloat16)).astype(jnp.float32)

@jax.custom_vjp
def lowered_backward(v):
    return v

def low_keep(v):
    return (lowered_copy(v), None)

def low_pass(kept, grad):
    return (grad,)

def back_keep(v):
    return (v, None)

def back_low(kept, grad):
    return (lowered_copy(grad),)
lowered_copy.defvjp(low_keep, low_pass)
lowered_backward.defvjp(back_keep, back_low)

def matrix_product_exact(left, right):
    return jnp.dot(left, right, precision=lax.Precision.HIGHEST)

def normalize(rows_in):
    return rows_in * lax.rsqrt(lax.optimization_barrier(jnp.mean(rows_in * rows_in, axis=-1, keepdims=True)) + EPS)

def rope_tables(position, head_dim):
    half_dim = head_dim // 2
    index_row = jnp.arange(half_dim, dtype=jnp.float32)
    inverse = THETA ** (-2.0 * index_row / head_dim)
    wavelen = 2.0 * math.pi / inverse
    smooth = jnp.clip((8192.0 / wavelen - 1.0) / 3.0, 0.0, 1.0)
    inverse = (1.0 - smooth) * inverse / 32.0 + smooth * inverse
    angles = position.astype(jnp.float32)[:, None] * inverse[None, :]
    return (jnp.cos(angles), jnp.sin(angles))

def rotary_apply(values_in, cosine_table, sine_table):
    half_dim = values_in.shape[-1] // 2
    first_half = values_in[..., :half_dim]
    second_half = values_in[..., half_dim:]
    cos_rows = cosine_table[:, None, :]
    sin_rows = sine_table[:, None, :]
    return jnp.concatenate([first_half * cos_rows - second_half * sin_rows, second_half * cos_rows + first_half * sin_rows], axis=-1)

def tree_tables(parents_row, lengths):
    seg_count = parents_row.shape[0]
    labels = jnp.arange(seg_count, dtype=jnp.int32)
    ends_at = jnp.cumsum(lengths).astype(jnp.int32)
    starts_at = (ends_at - lengths).astype(jnp.int32)
    reaches = labels[:, None] == labels[None, :]
    climber = labels
    for level_index in range(LEVELS - 1):
        climber = lax.optimization_barrier(jnp.sum(jnp.where(climber[:, None] == labels[None, :], parents_row[None, :], 0), axis=1)).astype(jnp.int32)
        reaches = reaches | (climber[:, None] == labels[None, :])
    before = lax.optimization_barrier(jnp.sum(jnp.where(reaches & (labels[:, None] != labels[None, :]), lengths[None, :], 0), axis=1)).astype(jnp.int32)
    return (reaches, starts_at, ends_at, before)

def place_tokens(tokens, starts_at, ends_at, before):
    labels = jnp.arange(starts_at.shape[0], dtype=jnp.int32)
    segment = lax.optimization_barrier(jnp.sum((tokens[:, None] >= ends_at[None, :]).astype(jnp.int32), axis=1)).astype(jnp.int32)
    member = segment[:, None] == labels[None, :]
    position = tokens - lax.optimization_barrier(jnp.sum(jnp.where(member, starts_at[None, :], 0), axis=1)) + lax.optimization_barrier(jnp.sum(jnp.where(member, before[None, :], 0), axis=1))
    return (segment, position.astype(jnp.int32))

def attention(query_rows, key_row_block, value_row_block, segment, reaches):
    tree_row_block = query_rows.shape[0]
    head_repeat_count = QUERY_HEADS // KEY_VALUE_HEADS
    key_full = jnp.repeat(key_row_block, head_repeat_count, axis=1)
    value_full = jnp.repeat(value_row_block, head_repeat_count, axis=1)
    block_rows = math.gcd(tree_row_block, 128)
    tokens = jnp.arange(tree_row_block, dtype=jnp.int32)

    def per_block(block_items):
        query_block, seg_block, token_block = block_items
        raw_scores = jnp.einsum('qhd,khd->hqk', query_block, key_full, precision=lax.Precision.HIGHEST)
        scores = lowered_backward(raw_scores) * HEAD_SIZE ** (-0.5)
        visible = reaches[seg_block][:, segment] & (tokens[None, :] <= token_block[:, None])
        scores = jnp.where(visible[None], scores, NEG)
        row_top = lax.optimization_barrier(jnp.max(scores, axis=-1, keepdims=True))
        exp_terms = jnp.exp(scores - row_top)
        probs = exp_terms / lax.optimization_barrier(jnp.sum(exp_terms, axis=-1, keepdims=True))
        return jnp.einsum('hqk,khd->qhd', lowered_copy(probs), value_full, precision=lax.Precision.HIGHEST)
    block_count = tree_row_block // block_rows
    mixed = lax.map(jax.checkpoint(per_block), (query_rows.reshape(block_count, block_rows, QUERY_HEADS, HEAD_SIZE), segment.reshape(block_count, block_rows), tokens.reshape(block_count, block_rows)))
    return mixed.reshape(tree_row_block, QUERY_HEADS * HEAD_SIZE)

def tree_forward(rows_in, gain_a, w_query, key_weight, value_weight, w_out, gain_f, w_gate, w_up, w_down, segment, reaches, cosine_table, sine_table):
    tree_row_block = rows_in.shape[0]
    attention_inner = lowered_copy(normalize(rows_in) * gain_a)
    query_rows = lowered_copy(rotary_apply(lowered_backward(matrix_product_exact(attention_inner, w_query)).reshape(tree_row_block, QUERY_HEADS, HEAD_SIZE), cosine_table, sine_table))
    key_row_block = lowered_copy(rotary_apply(lowered_backward(matrix_product_exact(attention_inner, key_weight)).reshape(tree_row_block, KEY_VALUE_HEADS, HEAD_SIZE), cosine_table, sine_table))
    value_row_block = lowered_copy(lowered_backward(matrix_product_exact(attention_inner, value_weight))).reshape(tree_row_block, KEY_VALUE_HEADS, HEAD_SIZE)
    attn_low = lowered_copy(lowered_backward(attention(query_rows, key_row_block, value_row_block, segment, reaches)))
    middle = rows_in + lowered_backward(matrix_product_exact(attn_low, w_out))
    inner_f = lowered_copy(normalize(middle) * gain_f)
    gate_rows = lowered_backward(matrix_product_exact(inner_f, w_gate))
    up_rows = lowered_backward(matrix_product_exact(inner_f, w_up))
    hidden = lowered_copy(gate_rows * jax.nn.sigmoid(gate_rows) * up_rows)
    return middle + lowered_backward(matrix_product_exact(hidden, w_down))

def reference(layer_in, out_grad, parents, seg_len, attn_gain, w_query, key_weight, value_weight, w_out, ffn_gain, w_gate, w_up, w_down):
    weights = tuple((w.astype(jnp.float32) for w in (attn_gain, w_query, key_weight, value_weight, w_out, ffn_gain, w_gate, w_up, w_down)))
    totals = tuple((jnp.zeros_like(w) for w in weights))
    outputs = []
    in_grads = []
    for tree_index in range(MB):
        reaches, starts_at, ends_at, before = tree_tables(parents[tree_index], seg_len[tree_index])
        tokens = jnp.arange(TREE, dtype=jnp.int32)
        segment, position = place_tokens(tokens, starts_at, ends_at, before)
        cosine_table, sine_table = rope_tables(position, HEAD_SIZE)

        def run_tree(rows_in, *params):
            return tree_forward(rows_in, *params, segment, reaches, cosine_table, sine_table)
        result, pullback = jax.vjp(run_tree, layer_in[tree_index].astype(jnp.float32), *weights)
        grads = pullback(out_grad[tree_index].astype(jnp.float32))
        outputs.append(result.astype(jnp.bfloat16))
        in_grads.append(grads[0])
        totals = tuple((a + b for a, b in zip(totals, grads[1:])))
    return (jnp.stack(outputs), jnp.stack(in_grads), totals[0], totals[1], totals[2], totals[3], totals[4], totals[5], totals[6], totals[7], totals[8])
```

```python
import functools
import math

import jax
import jax.numpy as jnp
from jax import lax
from jax.experimental import pallas as pl
from jax.experimental.pallas import tpu as pltpu
from jax.sharding import Mesh
from jax.sharding import PartitionSpec as P

QUERY_HEADS = 32
KEY_VALUE_HEADS = 8
HEAD_SIZE = 64
LEVELS = 3

EPS = 1e-05
THETA = 500000.0
NEG = -1e30
LN2 = math.log(2.0)
SWAP = [(0, 1), (1, 0)]
F32 = jnp.float32
BF16 = jnp.bfloat16


def dot(left, right, left_dim=1, right_dim=0):
    return lax.dot_general(
        left, right, (((left_dim,), (right_dim,)), ((), ())), preferred_element_type=F32
    )


def row_scale_of(rows_in):
    return lax.rsqrt(jnp.mean(rows_in * rows_in, axis=-1, keepdims=True) + EPS)


def norm_back(grad_normed, normed, row_scale):
    return row_scale * (
        grad_normed - normed * jnp.mean(grad_normed * normed, axis=-1, keepdims=True)
    )


def rope_angles(position, head_dim):
    half_dim = head_dim // 2
    index_row = jnp.arange(half_dim, dtype=F32)
    inverse = THETA ** (-2.0 * index_row / head_dim)
    wavelen = 2.0 * math.pi / inverse
    smooth = jnp.clip((8192.0 / wavelen - 1.0) / 3.0, 0.0, 1.0)
    inverse = (1.0 - smooth) * inverse / 32.0 + smooth * inverse
    return inverse[:, None] * position.astype(F32)[None, :]


def turn(first_half, second_half, cosine, sine):
    return first_half * cosine - second_half * sine, second_half * cosine + first_half * sine


def tree_tables(parents_row, lengths):
    seg_count = parents_row.shape[0]
    labels = jnp.arange(seg_count, dtype=jnp.int32)
    ends_at = jnp.cumsum(lengths)
    starts_at = ends_at - lengths
    reaches = labels[:, None] == labels[None, :]
    climber = labels
    for _ in range(LEVELS - 1):
        climber = jnp.sum(
            jnp.where(climber[:, None] == labels[None, :], parents_row[None, :], 0), axis=1
        )
        reaches = reaches | (climber[:, None] == labels[None, :])
    before = jnp.sum(
        jnp.where(reaches & (labels[:, None] != labels[None, :]), lengths[None, :], 0), axis=1
    )
    return reaches, starts_at, ends_at, before


def after(value, *others):
    return lax.optimization_barrier((value,) + others)[0]


class Ring:
    def __init__(self):
        self.count = lax.axis_size("zy")
        count = self.count
        place = [2 * i if i < count // 2 else 2 * (count - 1 - i) + 1 for i in range(count)]
        self.right = [(place[i], place[(i + 1) % count]) for i in range(count)]
        self.left = [(b, a) for a, b in self.right]
        me = lax.axis_index("zy")
        self.spot = jnp.where(me % 2 == 0, me // 2, count - 1 - me // 2)

    def chip(self, offset):
        spot = lax.rem(self.spot + offset + self.count, self.count)
        return jnp.where(spot < self.count // 2, 2 * spot, 2 * (self.count - 1 - spot) + 1)

    def go_right(self, value):
        return lax.ppermute(value, "zy", self.right)

    def go_left(self, value):
        return lax.ppermute(value, "zy", self.left)

    def gather(self, piece, line=None):
        count, half = self.count, self.count // 2
        cut = piece.shape[0] // 2
        if line is not None:
            piece = after(piece, *line)
        zeros = (0,) * (piece.ndim - 1)
        whole = jnp.zeros((count,) + piece.shape, piece.dtype)

        def put(whole, part, offset, row=0):
            return lax.dynamic_update_slice(whole, part[None], (self.chip(offset), row) + zeros)

        whole = put(whole, piece, 0)
        rightward = leftward = piece
        for step in range(1, half):
            rightward = self.go_right(rightward)
            leftward = self.go_left(leftward)
            whole = put(whole, rightward, -step)
            whole = put(whole, leftward, step)
        mark = (rightward, leftward)
        whole = put(whole, self.go_right(rightward[:cut]), half)
        whole = put(whole, self.go_left(leftward[cut:]), half, cut)
        return whole, mark

    def reduce(self, terms, line=None):
        half = self.count // 2
        cut = terms.shape[1] // 2
        if line is not None:
            terms = after(terms, *line)

        def term(offset):
            return lax.dynamic_index_in_dim(terms, self.chip(offset), 0, keepdims=False)

        far = term(half)
        rightward = self.go_right(far[:cut])
        leftward = self.go_left(far[cut:])
        for step in range(half - 1, 0, -1):
            mine, other = term(step), term(-step)
            if step == half - 1:
                rightward = jnp.concatenate([add_low(mine[:cut], rightward), mine[cut:]], axis=0)
                leftward = jnp.concatenate([other[:cut], add_low(other[cut:], leftward)], axis=0)
            else:
                rightward, leftward = add_low(mine, rightward), add_low(other, leftward)
            rightward, leftward = self.go_right(rightward), self.go_left(leftward)
        total = term(0).astype(F32) + rightward.astype(F32) + leftward.astype(F32)
        return total, (rightward, leftward)


def add_low(left, right):
    return (left.astype(F32) + right.astype(F32)).astype(BF16)


def other_core(value):
    return lax.ppermute(value, "core", SWAP)


def other_half(value):
    return lax.ppermute(value, "tp", SWAP)


def by_core(own, other, axis):
    first = lax.axis_index("core") == 0
    return jnp.concatenate(
        [jnp.where(first, own, other), jnp.where(first, other, own)], axis=axis
    )


def split_by_core(value, axis):
    core = lax.axis_index("core")
    size = value.shape[axis] // 2
    return (
        lax.dynamic_slice_in_dim(value, core * size, size, axis),
        lax.dynamic_slice_in_dim(value, (1 - core) * size, size, axis),
    )


def split3(value):
    high = value.astype(BF16)
    rest = value - high.astype(F32)
    middle = rest.astype(BF16)
    low = (rest - middle.astype(F32)).astype(BF16)
    return high, middle, low


def causal(scores, block):
    key_at = lax.broadcasted_iota(jnp.int32, scores.shape, 0)
    query_at = lax.rem(lax.broadcasted_iota(jnp.int32, scores.shape, 1), block)
    return jnp.where(key_at <= query_at, scores, NEG)


def block_of(ref, index, block, per_piece, lanes):
    piece = lax.div(index, per_piece)
    start = pl.multiple_of(lax.rem(index, per_piece) * block, block)
    return ref[piece, 0, pl.ds(start, block), lanes]


KEYS = slice(0, 128)
VALUES = slice(128, 256)


def attend_kernel(
    block, rep, per_piece, count_ref, list_ref, diag_ref, query_ref, mask_ref, kv_ref, hot_ref,
    out_ref, lse_ref, query_aug, value_turned,
):
    group, at = pl.program_id(0), pl.program_id(1)
    key_blocks = hot_ref.shape[0] // block - 1

    @pl.when((group == 0) & (at == 0))
    def _():
        rows = per_piece * block
        for piece in range(kv_ref.shape[0]):
            value_turned[:, piece * rows : (piece + 1) * rows] = kv_ref[piece, 0, :, VALUES].T

    query_aug[...] = jnp.zeros_like(query_aug)
    own = pl.ds(pl.multiple_of(group * HEAD_SIZE, HEAD_SIZE), HEAD_SIZE)
    for r in range(rep):
        columns = slice(r * block, (r + 1) * block)
        query_aug[own, columns] = query_ref[r * HEAD_SIZE : (r + 1) * HEAD_SIZE, :]
        query_aug[128:144, columns] = mask_ref[...]

    def scores_of(index):
        keys = block_of(kv_ref, jnp.minimum(index, key_blocks - 1), block, per_piece, KEYS)
        hot = hot_ref[pl.ds(pl.multiple_of(index * block, block), block), :]
        return jnp.dot(
            jnp.concatenate([keys, hot], axis=1), query_aug[...], preferred_element_type=F32
        )

    def values_of(index):
        index = jnp.minimum(index, key_blocks - 1)
        return value_turned[own, pl.ds(pl.multiple_of(index * block, block), block)]

    diagonal = diag_ref[at]
    scores = causal(scores_of(diagonal), block)
    top = jnp.max(scores, axis=0, keepdims=True)
    probs = jnp.exp2(scores - top)
    total = jnp.sum(probs, axis=0, keepdims=True)
    mixed = jnp.dot(values_of(diagonal), probs.astype(BF16), preferred_element_type=F32)

    def step(j, carry):
        top, total, mixed = carry
        one, two = list_ref[at, 2 * j], list_ref[at, 2 * j + 1]
        first, second = scores_of(one), scores_of(two)
        new = jnp.maximum(top, jnp.max(first, axis=0, keepdims=True))
        new = jnp.maximum(new, jnp.max(second, axis=0, keepdims=True))
        factor = jnp.exp2(top - new)
        first, second = jnp.exp2(first - new), jnp.exp2(second - new)
        total = (
            total * factor
            + jnp.sum(first, axis=0, keepdims=True)
            + jnp.sum(second, axis=0, keepdims=True)
        )
        values = jnp.concatenate([values_of(one), values_of(two)], axis=1)
        probs = jnp.concatenate([first.astype(BF16), second.astype(BF16)], axis=0)
        mixed = mixed * factor + jnp.dot(values, probs, preferred_element_type=F32)
        return new, total, mixed

    pairs = lax.div(count_ref[at] + 1, 2)
    top, total, mixed = lax.fori_loop(0, pairs, step, (top, total, mixed))
    mixed = mixed * (1.0 / total)
    lse = top + jnp.log2(total)
    for r in range(rep):
        columns = slice(r * block, (r + 1) * block)
        out_ref[r * HEAD_SIZE : (r + 1) * HEAD_SIZE, :] = mixed[:, columns].astype(BF16)
        lse_ref[0, r : r + 1, :] = lse[:, columns]


def attend(tree, tables, query, mask, kv, rep, block):
    counts, lists, diagonals, hot = tables
    heads = query.shape[0]
    pieces, _, rows, _ = kv.shape
    groups, query_blocks = heads // (rep * HEAD_SIZE), rows // block
    keys = pieces * rows
    grid_spec = pltpu.PrefetchScalarGridSpec(
        num_scalar_prefetch=3,
        grid=(groups, query_blocks),
        in_specs=[
            pl.BlockSpec(
                (rep * HEAD_SIZE, block), lambda g, q, *_: (g, tree * query_blocks + q)
            ),
            pl.BlockSpec((16, block), lambda g, q, *_: (0, q)),
            pl.BlockSpec((pieces, 1, rows, 256), lambda g, q, *_: (0, 0, 0, 0)),
            pl.BlockSpec((keys + block, 128), lambda g, q, *_: (0, 0)),
        ],
        out_specs=[
            pl.BlockSpec((rep * HEAD_SIZE, block), lambda g, q, *_: (g, q)),
            pl.BlockSpec((1, rep, block), lambda g, q, *_: (g, 0, q)),
        ],
        scratch_shapes=[
            pltpu.VMEM((256, rep * block), BF16),
            pltpu.VMEM((128, keys), BF16),
        ],
    )
    return pl.pallas_call(
        functools.partial(attend_kernel, block, rep, rows // block),
        grid_spec=grid_spec,
        out_shape=[
            jax.ShapeDtypeStruct((heads, rows), BF16),
            jax.ShapeDtypeStruct((groups, rep, rows), F32),
        ],
        compiler_params=pltpu.CompilerParams(vmem_limit_bytes=48 * 2**20),
        cost_estimate=pl.CostEstimate(
            flops=28 * 10**9, bytes_accessed=12 * 2**20, transcendentals=0
        ),
        name="tree_attention",
    )(counts, lists, diagonals, query, mask, kv, hot)


def attend_back_kernel(
    block, rep, per_piece, seen_ref, query_ref, mask_ref, mixed_ref, grad_ref, lse_ref, kv_ref,
    hot_ref, grad_query_ref, grad_kv_ref, query_aug, grad_aug, query_rows, grad_rows, key_turned,
    grad_query, grad_keys, grad_values,
):
    group = pl.program_id(0)
    rows = per_piece * block
    query_blocks = rows // block
    key_blocks = kv_ref.shape[0] * per_piece
    width = rep * block

    @pl.when(group == 0)
    def _():
        for piece in range(kv_ref.shape[0]):
            key_turned[:, piece * rows : (piece + 1) * rows] = kv_ref[piece, 0, :, KEYS].T
        grad_keys[...] = jnp.zeros_like(grad_keys)
        grad_values[...] = jnp.zeros_like(grad_values)

    query_aug[...] = jnp.zeros_like(query_aug)
    grad_aug[...] = jnp.zeros_like(grad_aug)
    grad_query[...] = jnp.zeros_like(grad_query)
    own = pl.ds(pl.multiple_of(group * HEAD_SIZE, HEAD_SIZE), HEAD_SIZE)
    none = jnp.zeros((HEAD_SIZE, block), BF16)
    for at in range(query_blocks):
        columns = slice(at * block, (at + 1) * block)
        for r in range(rep):
            here = slice(at * width + r * block, at * width + (r + 1) * block)
            head = slice(r * HEAD_SIZE, (r + 1) * HEAD_SIZE)
            query, grad = query_ref[head, columns], grad_ref[head, columns]
            query_aug[own, here] = query
            grad_aug[own, here] = grad
            delta = jnp.sum(
                grad.astype(F32) * mixed_ref[head, columns].astype(F32), axis=0, keepdims=True
            )
            empty = jnp.zeros((13, block), BF16)
            query_aug[128:160, here] = jnp.concatenate(
                [mask_ref[:, columns], *split3(-lse_ref[0, r : r + 1, columns]), empty], axis=0
            )
            grad_aug[128:160, here] = jnp.concatenate(
                [jnp.zeros((16, block), BF16), *split3(-delta), empty], axis=0
            )

            @pl.when(group == 0)
            def _():
                query_rows[here, :] = jnp.concatenate([query, none], axis=0).T
                grad_rows[here, :] = jnp.concatenate([grad, none], axis=0).T

            @pl.when(group == 1)
            def _():
                query_rows[here, :] = jnp.concatenate([none, query], axis=0).T
                grad_rows[here, :] = jnp.concatenate([none, grad], axis=0).T

    def over_keys(index, _):
        rows_at = pl.ds(pl.multiple_of(index * block, block), block)
        for at in range(query_blocks):
            columns = slice(at * width, (at + 1) * width)

            def work(on_diagonal):
                hot = hot_ref[rows_at, :]
                keys = block_of(kv_ref, index, block, per_piece, KEYS)
                values = block_of(kv_ref, index, block, per_piece, VALUES)
                scores = jnp.dot(
                    jnp.concatenate([keys, hot], axis=1),
                    query_aug[:, columns],
                    preferred_element_type=F32,
                )
                if on_diagonal:
                    scores = causal(scores, block)
                probs = jnp.exp2(scores)
                grad_probs = jnp.dot(
                    jnp.concatenate([values, hot], axis=1),
                    grad_aug[:, columns],
                    preferred_element_type=F32,
                )
                grad_scores = (probs * grad_probs).astype(BF16)
                grad_values[rows_at, :] += jnp.dot(
                    probs.astype(BF16), grad_rows[columns, :], preferred_element_type=F32
                )
                grad_keys[rows_at, :] += jnp.dot(
                    grad_scores, query_rows[columns, :], preferred_element_type=F32
                )
                grad_query[:, columns] += jnp.dot(
                    key_turned[own, rows_at], grad_scores, preferred_element_type=F32
                )

            seen = seen_ref[at, index]
            pl.when(seen == 1)(functools.partial(work, False))
            pl.when(seen == 2)(functools.partial(work, True))
        return 0

    lax.fori_loop(0, key_blocks, over_keys, 0)
    for at in range(query_blocks):
        for r in range(rep):
            here = slice(at * width + r * block, at * width + (r + 1) * block)
            grad_query_ref[
                r * HEAD_SIZE : (r + 1) * HEAD_SIZE, at * block : (at + 1) * block
            ] = grad_query[:, here]

    @pl.when(group == pl.num_programs(0) - 1)
    def _():
        for piece in range(kv_ref.shape[0]):
            at = slice(piece * rows, (piece + 1) * rows)
            grad_kv_ref[piece, :, KEYS] = (grad_keys[at, :] * LN2).astype(BF16)
            grad_kv_ref[piece, :, VALUES] = grad_values[at, :].astype(BF16)


def attend_back(tree, seen, hot, query, mask, mixed, grad, lse, kv, rep, block):
    heads = query.shape[0]
    pieces, _, rows, _ = kv.shape
    groups = heads // (rep * HEAD_SIZE)
    keys = pieces * rows
    head = pl.BlockSpec((rep * HEAD_SIZE, rows), lambda g, *_: (g, 0))
    grid_spec = pltpu.PrefetchScalarGridSpec(
        num_scalar_prefetch=1,
        grid=(groups,),
        in_specs=[
            pl.BlockSpec((rep * HEAD_SIZE, rows), lambda g, *_: (g, tree)),
            pl.BlockSpec((16, rows), lambda g, *_: (0, 0)),
            head,
            head,
            pl.BlockSpec((1, rep, rows), lambda g, *_: (g, 0, 0)),
            pl.BlockSpec((pieces, 1, rows, 256), lambda g, *_: (0, 0, 0, 0)),
            pl.BlockSpec((keys + block, 128), lambda g, *_: (0, 0)),
        ],
        out_specs=[
            head,
            pl.BlockSpec((pieces, rows, 256), lambda g, *_: (0, 0, 0)),
        ],
        scratch_shapes=[
            pltpu.VMEM((256, rep * rows), BF16),
            pltpu.VMEM((256, rep * rows), BF16),
            pltpu.VMEM((rep * rows, 128), BF16),
            pltpu.VMEM((rep * rows, 128), BF16),
            pltpu.VMEM((128, keys), BF16),
            pltpu.VMEM((HEAD_SIZE, rep * rows), F32),
            pltpu.VMEM((keys, 128), F32),
            pltpu.VMEM((keys, 128), F32),
        ],
    )
    return pl.pallas_call(
        functools.partial(attend_back_kernel, block, rep, rows // block),
        grid_spec=grid_spec,
        out_shape=[
            jax.ShapeDtypeStruct((heads, rows), F32),
            jax.ShapeDtypeStruct((pieces, rows, 256), BF16),
        ],
        compiler_params=pltpu.CompilerParams(vmem_limit_bytes=56 * 2**20),
        cost_estimate=pl.CostEstimate(
            flops=60 * 10**9, bytes_accessed=20 * 2**20, transcendentals=0
        ),
        name="tree_attention_back",
    )(seen, query, mask, mixed, grad, lse, kv, hot)


def shards(
    layer_in,
    out_grad,
    parents,
    seg_len,
    attn_gain,
    w_query,
    key_weight,
    value_weight,
    w_out,
    ffn_gain,
    w_gate,
    w_up,
    w_down,
):
    trees, rows, width = layer_in.shape
    ring = Ring()
    chips = ring.count
    here, core = lax.axis_index("zy"), lax.axis_index("core")
    chip_rows = 2 * rows
    keys = chips * chip_rows
    groups = KEY_VALUE_HEADS // (2 * lax.axis_size("tp"))
    rep = QUERY_HEADS // KEY_VALUE_HEADS
    heads = groups * rep
    head_cols, kv_cols = heads * HEAD_SIZE, groups * HEAD_SIZE
    block = math.gcd(rows, 256)
    per_half = rows // block
    query_blocks, key_blocks = chip_rows // block, keys // block

    def column_piece(weight):
        keep, give = split_by_core(weight, 1)
        return by_core(keep, other_core(give), 0)

    def row_piece(weight):
        keep, give = split_by_core(weight, 0)
        return by_core(keep.T, other_core(give).T, 0)

    qkv_piece = jnp.concatenate(
        [column_piece(w_query), column_piece(key_weight), column_piece(value_weight)], axis=1
    )
    gains = jnp.stack([attn_gain, ffn_gain])
    gain_piece = by_core(gains, other_core(gains), 1)
    gain_all, _ = ring.gather(gain_piece)
    gain_all = jnp.transpose(gain_all, (1, 0, 2)).reshape(2, width).astype(F32)
    gain_a, gain_f = gain_all[0], gain_all[1]
    w_qkv, line = ring.gather(qkv_piece)
    w_qkv = w_qkv.reshape(width, head_cols + 2 * kv_cols)
    w_q, w_kv = w_qkv[:, :head_cols], w_qkv[:, head_cols:]
    out_piece = row_piece(w_out)
    gate_piece, up_piece, down_piece = column_piece(w_gate), column_piece(w_up), row_piece(w_down)
    w_o, line = ring.gather(out_piece, line)
    w_o = w_o.reshape(width, head_cols)

    def token_order(chip):
        first = (chip * 2 + core) * rows
        second = (chip * 2 + 1 - core) * rows
        steps = jnp.arange(rows, dtype=jnp.int32)
        return jnp.concatenate(
            [first[..., None] + steps, second[..., None] + steps], axis=-1
        ).reshape(-1)

    own_tokens = token_order(here)
    key_tokens = token_order(jnp.arange(chips, dtype=jnp.int32))
    own_block = own_tokens[::block] // block
    key_block = key_tokens[::block] // block
    diagonals = here * query_blocks + jnp.arange(query_blocks, dtype=jnp.int32)
    labels = jnp.arange(16, dtype=jnp.int32)
    tables, positions, masks, seens = [], [], [], []
    for tree in range(trees):
        reaches, starts_at, ends_at, before = tree_tables(parents[tree], seg_len[tree])
        seg_count = ends_at.shape[0]
        extra = 16 - seg_count
        reach16 = jnp.pad(reaches, ((0, extra), (0, extra)))
        starts16 = jnp.pad(starts_at, (0, extra))
        before16 = jnp.pad(before, (0, extra))
        ends16 = jnp.pad(ends_at, (0, extra), constant_values=2**30)
        own_seg = jnp.sum((own_tokens[:, None] >= ends_at[None, :]).astype(jnp.int32), axis=1)
        key_seg = jnp.sum((key_tokens[:, None] >= ends_at[None, :]).astype(jnp.int32), axis=1)
        member = own_seg[None, :] == labels[:, None]
        positions.append(
            own_tokens + jnp.sum(jnp.where(member, (before16 - starts16)[:, None], 0), axis=0)
        )
        seen_by = jnp.sum(
            jnp.where(member[:, None, :], reach16.astype(jnp.int32)[:, :, None], 0), axis=0
        )
        masks.append(jnp.where(seen_by > 0, 0.0, NEG).astype(BF16))
        lanes = jnp.arange(128, dtype=jnp.int32)
        key_seg_all = jnp.concatenate([key_seg, jnp.full((block,), seg_count, jnp.int32)])
        hot = (lanes[None, :] == key_seg_all[:, None]) | ((lanes >= 16) & (lanes < 19))[None, :]
        hot = hot.astype(BF16)

        def holds(blocks):
            low = blocks[:, None] * block
            return ((starts_at[None, :] < low + block) & (ends_at[None, :] > low)).astype(F32)

        linked = dot(dot(holds(own_block), reaches.astype(F32)), holds(key_block), 1, 1) > 0.5
        seen = linked & (key_block[None, :] < own_block[:, None])
        rank = jnp.cumsum(seen.astype(jnp.int32), axis=1) - 1
        slots = jnp.arange(key_blocks + 2, dtype=jnp.int32)
        index = jnp.arange(key_blocks, dtype=jnp.int32)
        chosen = seen[:, :, None] & (rank[:, :, None] == slots[None, None, :])
        lists = key_blocks + jnp.sum(
            jnp.where(chosen, index[None, :, None] - key_blocks, 0), axis=1
        )
        counts = jnp.sum(seen.astype(jnp.int32), axis=1)
        tables.append((counts, lists, diagonals, hot))
        on_diagonal = index[None, :] == diagonals[:, None]
        seens.append(jnp.where(on_diagonal, 2, seen.astype(jnp.int32)))
    position = jnp.concatenate(positions)
    angles = rope_angles(position, HEAD_SIZE)
    cosine, sine = jnp.cos(angles), jnp.sin(angles)

    rows_in = layer_in.astype(F32)
    scale_a = row_scale_of(rows_in)
    normed_a = rows_in * scale_a

    def both_cores(own):
        return jnp.concatenate([own, other_core(own)], axis=1)

    inner_a = both_cores((normed_a * gain_a).astype(BF16)).reshape(trees * chip_rows, width)
    grad_low = both_cores(out_grad).reshape(trees * chip_rows, width)

    def by_head(value):
        return value.reshape(-1, 2, HEAD_SIZE // 2, value.shape[-1])

    def query_turn(value, cosine, sine):
        value = by_head(value)
        first, second = turn(value[:, 0], value[:, 1], cosine[None], sine[None])
        return jnp.stack([first, second], axis=1).reshape(-1, value.shape[-1])

    query = dot(w_q, inner_a, 0, 1)
    query = (query_turn(query, cosine, sine) * (HEAD_SIZE**-0.5 / LN2)).astype(BF16)
    key_value = dot(inner_a, w_kv)
    key_pre = key_value[:, :kv_cols].reshape(-1, groups, 2, HEAD_SIZE // 2)
    cosine_rows, sine_rows = cosine.T[:, None, :], sine.T[:, None, :]
    first, second = turn(key_pre[:, :, 0], key_pre[:, :, 1], cosine_rows, sine_rows)
    key_low = jnp.stack([first, second], axis=2).reshape(-1, kv_cols)
    key_value = jnp.concatenate([key_low, key_value[:, kv_cols:]], axis=1).astype(BF16)
    key_value = key_value.reshape(trees, 1, chip_rows, 2 * kv_cols)

    kvs = []
    for tree in range(trees):
        kv, line = ring.gather(key_value[tree].reshape(chip_rows, 2 * kv_cols), line)
        kvs.append(kv.reshape(chips, 1, chip_rows, 2 * kv_cols))

    w_g, line = ring.gather(gate_piece, line)
    w_u, line = ring.gather(up_piece, line)
    w_d, line = ring.gather(down_piece, line)
    w_g, w_u, w_d = (w.reshape(width, -1) for w in (w_g, w_u, w_d))

    def sum_parts(part):
        own = part[:rows] + other_core(part[rows:].astype(BF16)).astype(F32)
        low = own.astype(BF16)
        return low.astype(F32) + other_half(low).astype(F32), own

    mixes, lses, middles, inners, normeds_f, scales_f = [], [], [], [], [], []
    for tree in range(trees):
        mixed, lse = attend(tree, tables[tree], query, masks[tree], kvs[tree], rep, block)
        mixes.append(mixed)
        lses.append(lse)
        middle = rows_in[tree] + sum_parts(dot(mixed, w_o, 0, 1))[0]
        scale_f = row_scale_of(middle)
        normed_f = middle * scale_f
        inner = (normed_f * gain_f).astype(BF16)
        inners += [inner, other_core(inner)]
        middles.append(middle)
        scales_f.append(scale_f)
        normeds_f.append(normed_f)
    inner_f = jnp.concatenate(inners, axis=0)

    gate = dot(inner_f, w_g)
    up = dot(inner_f, w_u)
    sigmoid = jax.nn.sigmoid(gate)
    activated = gate * sigmoid
    hidden = (activated * up).astype(BF16)
    outputs = []
    for tree in range(trees):
        span = slice(tree * chip_rows, (tree + 1) * chip_rows)
        outputs.append((middles[tree] + sum_parts(dot(hidden[span], w_d, 1, 1))[0]).astype(BF16))

    def pieces(term):
        return term.astype(BF16).reshape(chips, width // chips, -1)

    grad_hidden = dot(grad_low, w_d)
    down_sum, line = ring.reduce(pieces(dot(grad_low, hidden, 0, 0)), line)
    grad_gate = (grad_hidden * up * sigmoid * (1.0 + gate * (1.0 - sigmoid))).astype(BF16)
    grad_up = (grad_hidden * activated).astype(BF16)
    grads_middle, grads_low, gain_f_terms = [], [], []
    for tree in range(trees):
        span = slice(tree * chip_rows, (tree + 1) * chip_rows)
        part = dot(grad_gate[span], w_g, 1, 1) + dot(grad_up[span], w_u, 1, 1)
        grad_inner, _ = sum_parts(part)
        gain_f_terms.append(jnp.sum(grad_inner * normeds_f[tree], axis=0))
        grad_middle = out_grad[tree].astype(F32) + norm_back(
            grad_inner * gain_f, normeds_f[tree], scales_f[tree]
        )
        low = grad_middle.astype(BF16)
        grads_middle.append(grad_middle)
        grads_low += [low, other_core(low)]
    gate_sum, line = ring.reduce(pieces(dot(inner_f, grad_gate, 0, 0)), line)
    up_sum, line = ring.reduce(pieces(dot(inner_f, grad_up, 0, 0)), line)

    grad_queries, kv_sums, line_kv = [], [], line
    for tree in range(trees):
        low = jnp.concatenate(grads_low[2 * tree : 2 * tree + 2], axis=0)
        grad_mixed = dot(w_o, low, 0, 1).astype(BF16)
        grad_query, grad_kv = attend_back(
            tree,
            seens[tree],
            tables[tree][3],
            query,
            masks[tree],
            mixes[tree],
            grad_mixed,
            lses[tree],
            kvs[tree],
            rep,
            block,
        )
        grad_queries.append(grad_query)
        kv_sum, line_kv = ring.reduce(grad_kv, line_kv)
        kv_sums.append(kv_sum)
    grad_mid_low = jnp.concatenate(grads_low, axis=0)
    mixed_all = jnp.concatenate(mixes, axis=1)
    out_sum, _ = ring.reduce(pieces(dot(grad_mid_low, mixed_all, 0, 1)), line)

    grads_q, grads_kv, in_grads, gain_a_terms = [], [], [], []
    for tree in range(trees):
        span = slice(tree * chip_rows, (tree + 1) * chip_rows)
        grad_q = query_turn(grad_queries[tree], cosine[:, span], -sine[:, span])
        grad_q = (grad_q * HEAD_SIZE**-0.5).astype(BF16)
        grad_k = kv_sums[tree][:, :kv_cols].reshape(-1, groups, 2, HEAD_SIZE // 2)
        first, second = turn(
            grad_k[:, :, 0], grad_k[:, :, 1], cosine_rows[span], -sine_rows[span]
        )
        grad_k = jnp.stack([first, second], axis=2).reshape(-1, kv_cols)
        grad_kv = jnp.concatenate([grad_k, kv_sums[tree][:, kv_cols:]], axis=1).astype(BF16)
        grads_q.append(grad_q)
        grads_kv.append(grad_kv)
        part = dot(grad_q, w_q, 0, 1) + dot(grad_kv, w_kv, 1, 1)
        grad_inner, core_sum = sum_parts(part)
        gain_a_terms.append(jnp.sum(core_sum * normed_a[tree], axis=0))
        in_grads.append(
            grads_middle[tree] + norm_back(grad_inner * gain_a, normed_a[tree], scale_a[tree])
        )
    term_q = dot(inner_a, jnp.concatenate(grads_q, axis=1), 0, 1)
    term_kv = dot(inner_a, jnp.concatenate(grads_kv, axis=0), 0, 0)
    qkv_sum, _ = ring.reduce(pieces(jnp.concatenate([term_q, term_kv], axis=1)), line_kv)

    def gain_sum(terms):
        keep, give = split_by_core(sum(terms).reshape(chips, 2, width // chips // 2), 1)
        both = (keep + other_core(give)).reshape(chips, 2, -1)
        total = both_ways(ring, both)
        return total.reshape(-1)

    gain_f_grad = gain_sum(gain_f_terms)
    gain_a_grad = gain_sum(gain_a_terms)
    gain_a_grad = gain_a_grad + other_half(gain_a_grad)

    def column_grad(total):
        keep, give = split_by_core(total, 0)
        return by_core(keep, other_core(give), 1)

    def row_grad(total):
        keep, give = split_by_core(total, 0)
        return by_core(keep, other_core(give), 1).T

    return (
        jnp.stack(outputs),
        jnp.stack(in_grads),
        gain_a_grad,
        column_grad(qkv_sum[:, :head_cols]),
        column_grad(qkv_sum[:, head_cols : head_cols + kv_cols]),
        column_grad(qkv_sum[:, head_cols + kv_cols :]),
        row_grad(out_sum),
        gain_f_grad,
        column_grad(gate_sum),
        column_grad(up_sum),
        row_grad(down_sum),
    )


def both_ways(ring, terms):
    half = ring.count // 2

    def term(offset):
        return lax.dynamic_index_in_dim(terms, ring.chip(offset), 0, keepdims=False)

    rightward, leftward = ring.go_right(term(half)), None
    for step in range(half - 1, 0, -1):
        rightward = ring.go_right(rightward + term(step))
        leftward = ring.go_left(term(-step) if leftward is None else leftward + term(-step))
    total = term(0) + rightward
    return total if leftward is None else total + leftward


def solution(mesh):
    devices = mesh.devices
    mesh = Mesh(devices.reshape(-1, 2, devices.shape[1]), ("zy", "core", "tp"))
    fsdp = ("zy", "core")
    specs = (
        P(fsdp),
        P(fsdp, "tp"),
        P(fsdp, "tp"),
        P(fsdp, "tp"),
        P("tp", fsdp),
        P(fsdp),
        P(fsdp, "tp"),
        P(fsdp, "tp"),
        P("tp", fsdp),
    )
    tokens = P(None, fsdp, None)
    return jax.shard_map(
        shards,
        mesh=mesh,
        in_specs=(tokens, tokens, P(), P()) + specs,
        out_specs=(tokens, tokens) + specs,
        check_vma=False,
    )
```

```python
import functools
import math

import jax
import jax.numpy as jnp
from jax import lax
from jax.experimental import pallas as pl
from jax.experimental.pallas import tpu as pltpu
from jax.sharding import Mesh
from jax.sharding import PartitionSpec as P

QUERY_HEADS = 32
KEY_VALUE_HEADS = 8
HEAD_SIZE = 64
LEVELS = 3

EPS = 1e-05
THETA = 500000.0
NEG = -1e30
LN2 = math.log(2.0)
SWAP = [(0, 1), (1, 0)]
F32 = jnp.float32
BF16 = jnp.bfloat16
SMALL = pl.CostEstimate(flops=2**20, bytes_accessed=2**10, transcendentals=0)


def dot(left, right, left_dim=1, right_dim=0):
    return lax.dot_general(
        left, right, (((left_dim,), (right_dim,)), ((), ())), preferred_element_type=F32
    )


def row_scale_of(rows_in):
    return lax.rsqrt(jnp.mean(rows_in * rows_in, axis=-1, keepdims=True) + EPS)


def norm_back(grad_normed, normed, row_scale):
    return row_scale * (
        grad_normed - normed * jnp.mean(grad_normed * normed, axis=-1, keepdims=True)
    )


def rope_angles(position, head_dim):
    half_dim = head_dim // 2
    index_row = jnp.arange(half_dim, dtype=F32)
    inverse = THETA ** (-2.0 * index_row / head_dim)
    wavelen = 2.0 * math.pi / inverse
    smooth = jnp.clip((8192.0 / wavelen - 1.0) / 3.0, 0.0, 1.0)
    inverse = (1.0 - smooth) * inverse / 32.0 + smooth * inverse
    return inverse[:, None] * position.astype(F32)[None, :]


def turn(first_half, second_half, cosine, sine):
    return first_half * cosine - second_half * sine, second_half * cosine + first_half * sine


def tree_tables(parents_row, lengths):
    seg_count = parents_row.shape[0]
    labels = jnp.arange(seg_count, dtype=jnp.int32)
    ends_at = jnp.cumsum(lengths)
    starts_at = ends_at - lengths
    reaches = labels[:, None] == labels[None, :]
    climber = labels
    for _ in range(LEVELS - 1):
        climber = jnp.sum(
            jnp.where(climber[:, None] == labels[None, :], parents_row[None, :], 0), axis=1
        )
        reaches = reaches | (climber[:, None] == labels[None, :])
    before = jnp.sum(
        jnp.where(reaches & (labels[:, None] != labels[None, :]), lengths[None, :], 0), axis=1
    )
    return reaches, starts_at, ends_at, before


def after_all(values, others):
    if not others:
        return list(values)
    return list(lax.optimization_barrier(tuple(values) + tuple(others))[: len(values)])


def unwritten(like, shape):
    return pl.pallas_call(
        lambda like_ref, out_ref: None,
        in_specs=[pl.BlockSpec(memory_space=pl.ANY)],
        out_specs=pl.BlockSpec(memory_space=pl.ANY),
        out_shape=jax.ShapeDtypeStruct(shape, like.dtype),
        name="buffer",
    )(like)


class Ring:
    def __init__(self):
        self.count = lax.axis_size("zy")
        count = self.count
        place = [2 * i if i < count // 2 else 2 * (count - 1 - i) + 1 for i in range(count)]
        self.right = [(place[i], place[(i + 1) % count]) for i in range(count)]
        self.left = [(b, a) for a, b in self.right]
        me = lax.axis_index("zy")
        self.spot = jnp.where(me % 2 == 0, me // 2, count - 1 - me // 2)

    def chip(self, offset):
        spot = lax.rem(self.spot + offset + self.count, self.count)
        return jnp.where(spot < self.count // 2, 2 * spot, 2 * (self.count - 1 - spot) + 1)

    def go_right(self, value):
        return lax.ppermute(value, "zy", self.right)

    def go_left(self, value):
        return lax.ppermute(value, "zy", self.left)

    def put(self, whole, part, offset, row=0):
        at = (self.chip(offset), row) + (0,) * (part.ndim - 1)
        return lax.dynamic_update_slice(whole, part[None], at)


class Gather:
    def __init__(self, ring, pieces):
        self.ring, self.step = ring, 0
        self.cuts = [piece.shape[0] // 2 for piece in pieces]
        wholes = [unwritten(piece, (ring.count,) + piece.shape) for piece in pieces]
        self.wholes = [ring.put(whole, piece, 0) for whole, piece in zip(wholes, pieces)]
        self.rightward = self.leftward = list(pieces)

    def hop(self, *others):
        ring, count = self.ring, len(self.cuts)
        both = after_all(self.rightward + self.leftward, others)
        rightward, leftward = both[:count], both[count:]
        self.step += 1
        far = self.step == ring.count // 2
        if far:
            rightward = [part[:cut] for part, cut in zip(rightward, self.cuts)]
            leftward = [part[cut:] for part, cut in zip(leftward, self.cuts)]
        rightward = [ring.go_right(part) for part in rightward]
        leftward = [ring.go_left(part) for part in leftward]
        for i, cut in enumerate(self.cuts):
            whole = ring.put(self.wholes[i], rightward[i], -self.step)
            self.wholes[i] = ring.put(whole, leftward[i], self.step, cut if far else 0)
        self.rightward, self.leftward = rightward, leftward
        return tuple(rightward) + tuple(leftward)

    def finish(self, *others):
        while self.step < self.ring.count // 2:
            self.hop(*others)
        return self.wholes


class Reduce:
    def __init__(self, ring, terms):
        self.ring, self.terms, self.left = ring, list(terms), ring.count // 2
        self.cuts = [term.shape[1] // 2 for term in terms]
        self.rightward = self.leftward = None

    def each(self, offset):
        chip = self.ring.chip(offset)
        return [lax.dynamic_index_in_dim(term, chip, 0, keepdims=False) for term in self.terms]

    def hop(self, *others):
        ring, step, count = self.ring, self.left, len(self.cuts)
        if self.rightward is None:
            far = after_all(self.each(step), others)
            rightward = [part[:cut] for part, cut in zip(far, self.cuts)]
            leftward = [part[cut:] for part, cut in zip(far, self.cuts)]
        else:
            both = after_all(self.rightward + self.leftward, others)
            rightward, leftward = both[:count], both[count:]
            mine, other = self.each(step), self.each(-step)
            if step == ring.count // 2 - 1:
                for i, cut in enumerate(self.cuts):
                    parts = [add_low(mine[i][:cut], rightward[i]), mine[i][cut:]]
                    rightward[i] = jnp.concatenate(parts, axis=0)
                    parts = [other[i][:cut], add_low(other[i][cut:], leftward[i])]
                    leftward[i] = jnp.concatenate(parts, axis=0)
            else:
                rightward = [add_low(one, part) for one, part in zip(mine, rightward)]
                leftward = [add_low(one, part) for one, part in zip(other, leftward)]
        self.rightward = [ring.go_right(part) for part in rightward]
        self.leftward = [ring.go_left(part) for part in leftward]
        self.left -= 1
        return tuple(self.rightward) + tuple(self.leftward)

    def finish(self, *others):
        while self.left > 0:
            self.hop(*others)
        return [
            mine.astype(F32) + one.astype(F32) + two.astype(F32)
            for mine, one, two in zip(self.each(0), self.rightward, self.leftward)
        ]


def add_low(left, right):
    return (left.astype(F32) + right.astype(F32)).astype(BF16)


def other_core(value):
    return lax.ppermute(value, "core", SWAP)


def other_half(value):
    return lax.ppermute(value, "tp", SWAP)


def by_core(own, other, axis):
    first = lax.axis_index("core") == 0
    return jnp.concatenate(
        [jnp.where(first, own, other), jnp.where(first, other, own)], axis=axis
    )


def split_by_core(value, axis):
    core = lax.axis_index("core")
    size = value.shape[axis] // 2
    return (
        lax.dynamic_slice_in_dim(value, core * size, size, axis),
        lax.dynamic_slice_in_dim(value, (1 - core) * size, size, axis),
    )


def split3(value):
    high = value.astype(BF16)
    rest = value - high.astype(F32)
    middle = rest.astype(BF16)
    low = (rest - middle.astype(F32)).astype(BF16)
    return high, middle, low


def causal(scores, block):
    key_at = lax.broadcasted_iota(jnp.int32, scores.shape, 0)
    query_at = lax.rem(lax.broadcasted_iota(jnp.int32, scores.shape, 1), block)
    return jnp.where(key_at <= query_at, scores, NEG)


def block_of(ref, index, block, per_piece):
    piece = lax.div(index, per_piece)
    start = pl.multiple_of(lax.rem(index, per_piece) * block, block)
    return ref[piece, 0, pl.ds(start, block), :]


def attend_kernel(
    block, rep, per_piece, count_ref, list_ref, diag_ref, query_ref, mask_ref, kv_ref, hot_ref,
    out_ref, lse_ref, query_aug, turned,
):
    at = pl.program_id(1)
    key_blocks = hot_ref.shape[0] // block - 1

    @pl.when(at == 0)
    def _():
        rows = per_piece * block
        for piece in range(kv_ref.shape[0]):
            turned[:, piece * rows : (piece + 1) * rows] = kv_ref[piece, 0].T

    query_aug[HEAD_SIZE:, :] = jnp.zeros_like(query_aug[HEAD_SIZE:, :])
    for r in range(rep):
        columns = slice(r * block, (r + 1) * block)
        query_aug[:HEAD_SIZE, columns] = query_ref[r * HEAD_SIZE : (r + 1) * HEAD_SIZE, :]
        query_aug[128:144, columns] = mask_ref[...]

    def scores_of(index):
        keys = block_of(kv_ref, jnp.minimum(index, key_blocks - 1), block, per_piece)
        hot = hot_ref[pl.ds(pl.multiple_of(index * block, block), block), :]
        return jnp.dot(
            jnp.concatenate([keys, hot], axis=1), query_aug[...], preferred_element_type=F32
        )

    def values_of(index):
        index = jnp.minimum(index, key_blocks - 1)
        return turned[HEAD_SIZE:, pl.ds(pl.multiple_of(index * block, block), block)]

    diagonal = diag_ref[at]
    scores = causal(scores_of(diagonal), block)
    top = jnp.max(scores, axis=0, keepdims=True)
    probs = jnp.exp2(scores - top)
    total = jnp.sum(probs, axis=0, keepdims=True)
    mixed = jnp.dot(values_of(diagonal), probs.astype(BF16), preferred_element_type=F32)

    def step(j, carry):
        top, total, mixed = carry
        one, two = list_ref[at, 2 * j], list_ref[at, 2 * j + 1]
        first, second = scores_of(one), scores_of(two)
        new = jnp.maximum(top, jnp.max(first, axis=0, keepdims=True))
        new = jnp.maximum(new, jnp.max(second, axis=0, keepdims=True))
        factor = jnp.exp2(top - new)
        first, second = jnp.exp2(first - new), jnp.exp2(second - new)
        total = (
            total * factor
            + jnp.sum(first, axis=0, keepdims=True)
            + jnp.sum(second, axis=0, keepdims=True)
        )
        values = jnp.concatenate([values_of(one), values_of(two)], axis=1)
        probs = jnp.concatenate([first.astype(BF16), second.astype(BF16)], axis=0)
        mixed = mixed * factor + jnp.dot(values, probs, preferred_element_type=F32)
        return new, total, mixed

    pairs = lax.div(count_ref[at] + 1, 2)
    top, total, mixed = lax.fori_loop(0, pairs, step, (top, total, mixed))
    mixed = mixed * (1.0 / total)
    lse = top + jnp.log2(total)
    for r in range(rep):
        columns = slice(r * block, (r + 1) * block)
        out_ref[r * HEAD_SIZE : (r + 1) * HEAD_SIZE, :] = mixed[:, columns].astype(BF16)
        lse_ref[0, r : r + 1, :] = lse[:, columns]


def attend(tree, tables, query, mask, kv, rep, block):
    counts, lists, diagonals, hot = tables
    heads = query.shape[0]
    pieces, _, rows, _ = kv.shape
    groups, query_blocks = heads // (rep * HEAD_SIZE), rows // block
    keys = pieces * rows
    grid_spec = pltpu.PrefetchScalarGridSpec(
        num_scalar_prefetch=3,
        grid=(groups, query_blocks),
        in_specs=[
            pl.BlockSpec(
                (rep * HEAD_SIZE, block), lambda g, q, *_: (g, tree * query_blocks + q)
            ),
            pl.BlockSpec((16, block), lambda g, q, *_: (0, q)),
            pl.BlockSpec((pieces, 1, rows, 128), lambda g, q, *_: (0, tree, 0, g)),
            pl.BlockSpec((keys + block, 128), lambda g, q, *_: (0, 0)),
        ],
        out_specs=[
            pl.BlockSpec((rep * HEAD_SIZE, block), lambda g, q, *_: (g, q)),
            pl.BlockSpec((1, rep, block), lambda g, q, *_: (g, 0, q)),
        ],
        scratch_shapes=[
            pltpu.VMEM((256, rep * block), BF16),
            pltpu.VMEM((128, keys), BF16),
        ],
    )
    return pl.pallas_call(
        functools.partial(attend_kernel, block, rep, rows // block),
        grid_spec=grid_spec,
        out_shape=[
            jax.ShapeDtypeStruct((heads, rows), BF16),
            jax.ShapeDtypeStruct((groups, rep, rows), F32),
        ],
        compiler_params=pltpu.CompilerParams(vmem_limit_bytes=48 * 2**20),
        cost_estimate=SMALL,
        name="tree_attention",
    )(counts, lists, diagonals, query, mask, kv, hot)


def attend_back_kernel(
    block, rep, per_piece, seen_ref, query_ref, mask_ref, mixed_ref, grad_ref, lse_ref, kv_ref,
    hot_ref, cosine_ref, sine_ref, before_ref, grad_query_ref, grad_kv_ref, augs, turned_rows,
    key_turned, grad_query, grad_kv,
):
    rows = per_piece * block
    query_blocks = rows // block
    key_blocks = kv_ref.shape[0] * per_piece
    width = rep * block

    for piece in range(kv_ref.shape[0]):
        key_turned[:, piece * rows : (piece + 1) * rows] = kv_ref[piece, 0].T
    grad_kv[...] = jnp.zeros_like(grad_kv)
    grad_query[...] = jnp.zeros_like(grad_query)
    augs[...] = jnp.zeros_like(augs)
    none = jnp.zeros((HEAD_SIZE, block), BF16)
    for at in range(query_blocks):
        columns = slice(at * block, (at + 1) * block)
        for r in range(rep):
            here = slice(2 * at * width + r * block, 2 * at * width + (r + 1) * block)
            there = slice((2 * at + 1) * width + r * block, (2 * at + 1) * width + (r + 1) * block)
            head = slice(r * HEAD_SIZE, (r + 1) * HEAD_SIZE)
            query, grad = query_ref[head, columns], grad_ref[head, columns]
            augs[:HEAD_SIZE, here] = query
            augs[HEAD_SIZE : 2 * HEAD_SIZE, there] = grad
            delta = jnp.sum(
                grad.astype(F32) * mixed_ref[head, columns].astype(F32), axis=0, keepdims=True
            )
            empty = jnp.zeros((13, block), BF16)
            augs[128:160, here] = jnp.concatenate(
                [mask_ref[:, columns], *split3(-lse_ref[0, r : r + 1, columns]), empty], axis=0
            )
            augs[128:160, there] = jnp.concatenate(
                [jnp.zeros((16, block), BF16), *split3(-delta), empty], axis=0
            )
            turned_rows[here, :] = jnp.concatenate([none, grad], axis=0).T
            turned_rows[there, :] = jnp.concatenate([query, none], axis=0).T

    def over_keys(index, _):
        rows_at = pl.ds(pl.multiple_of(index * block, block), block)
        for at in range(query_blocks):
            columns = slice(2 * at * width, (2 * at + 2) * width)

            def work(on_diagonal):
                both = jnp.dot(
                    jnp.concatenate(
                        [block_of(kv_ref, index, block, per_piece), hot_ref[rows_at, :]], axis=1
                    ),
                    augs[:, columns],
                    preferred_element_type=F32,
                )
                scores, grad_probs = both[:, :width], both[:, width:]
                if on_diagonal:
                    scores = causal(scores, block)
                probs = jnp.exp2(scores)
                grad_scores = (probs * grad_probs).astype(BF16)
                grad_kv[rows_at, :] += jnp.dot(
                    jnp.concatenate([probs.astype(BF16), grad_scores], axis=1),
                    turned_rows[columns, :],
                    preferred_element_type=F32,
                )
                grad_query[:, at * width : (at + 1) * width] += jnp.dot(
                    key_turned[:HEAD_SIZE, rows_at], grad_scores, preferred_element_type=F32
                )

            seen = seen_ref[at, index]
            pl.when(seen == 1)(functools.partial(work, False))
            pl.when(seen == 2)(functools.partial(work, True))
        return 0

    lax.fori_loop(0, key_blocks, over_keys, 0)
    for at in range(query_blocks):
        columns = slice(at * block, (at + 1) * block)
        cosine = cosine_ref[:, columns] * HEAD_SIZE**-0.5
        sine = -sine_ref[:, columns] * HEAD_SIZE**-0.5
        for r in range(0, rep, 2):
            parts = []
            for head in (r, r + 1):
                here = slice(at * width + head * block, at * width + (head + 1) * block)
                grad = grad_query[:, here]
                half = HEAD_SIZE // 2
                parts += turn(grad[:half], grad[half:], cosine, sine)
            grad_query_ref[columns, r * HEAD_SIZE : (r + 2) * HEAD_SIZE] = (
                jnp.concatenate(parts, axis=0).T.astype(BF16)
            )
    for piece in range(kv_ref.shape[0]):
        grads = grad_kv[piece * rows : (piece + 1) * rows, :]
        lanes = lax.broadcasted_iota(jnp.int32, grads.shape, 1)
        grad_kv_ref[piece] = jnp.where(lanes < HEAD_SIZE, grads * LN2, grads).astype(BF16)


def attend_back(
    tree, group, seen, hot, query, mask, mixed, grad, lse, kv, cosine, sine, rep, block, before
):
    pieces, _, rows, _ = kv.shape
    keys = pieces * rows
    heads = rep * HEAD_SIZE
    head = pl.BlockSpec((heads, rows), lambda i, *_: (group, 0))
    table = pl.BlockSpec((HEAD_SIZE // 2, rows), lambda i, *_: (0, tree))
    grid_spec = pltpu.PrefetchScalarGridSpec(
        num_scalar_prefetch=1,
        grid=(1,),
        in_specs=[
            pl.BlockSpec((heads, rows), lambda i, *_: (group, tree)),
            pl.BlockSpec((16, rows), lambda i, *_: (0, 0)),
            head,
            head,
            pl.BlockSpec((1, rep, rows), lambda i, *_: (group, 0, 0)),
            pl.BlockSpec((pieces, 1, rows, 128), lambda i, *_: (0, tree, 0, group)),
            pl.BlockSpec((keys + block, 128), lambda i, *_: (0, 0)),
            table,
            table,
            pl.BlockSpec(memory_space=pl.ANY),
        ],
        out_specs=[
            pl.BlockSpec((rows, heads), lambda i, *_: (0, 0)),
            pl.BlockSpec((pieces, rows, 128), lambda i, *_: (0, 0, group)),
        ],
        scratch_shapes=[
            pltpu.VMEM((256, 2 * rep * rows), BF16),
            pltpu.VMEM((2 * rep * rows, 128), BF16),
            pltpu.VMEM((128, keys), BF16),
            pltpu.VMEM((HEAD_SIZE, rep * rows), F32),
            pltpu.VMEM((keys, 128), F32),
        ],
    )
    return pl.pallas_call(
        functools.partial(attend_back_kernel, block, rep, rows // block),
        grid_spec=grid_spec,
        out_shape=[
            jax.ShapeDtypeStruct((rows, heads), BF16),
            jax.ShapeDtypeStruct((pieces, rows, kv.shape[3]), BF16),
        ],
        input_output_aliases={10: 1} if group else {},
        compiler_params=pltpu.CompilerParams(vmem_limit_bytes=56 * 2**20),
        cost_estimate=SMALL,
        name="tree_attention_back",
    )(seen, query, mask, mixed, grad, lse, kv, hot, cosine, sine, cosine if before is None else before)


def project_kernel(
    heads, columns, own_ref, other_ref, gain_ref, weight_ref, cosine_ref, sine_ref, inner_ref, query_ref,
    kv_ref, rows,
):
    mine = lax.rem(pl.program_id(0), 2) == 0

    @pl.when(mine)
    def _():
        rows[...] = own_ref[0].astype(F32)

    @pl.when(jnp.logical_not(mine))
    def _():
        rows[...] = other_ref[0].astype(F32)

    x = rows[...]
    inner = (x * row_scale_of(x) * gain_ref[...]).astype(BF16)
    inner_ref[...] = inner
    made = jnp.dot(inner, weight_ref[:, :columns], preferred_element_type=F32)
    cosine, sine = cosine_ref[...], sine_ref[...]
    half = HEAD_SIZE // 2

    def turned(values):
        parts = []
        for start in range(0, values.shape[0], HEAD_SIZE):
            parts += turn(
                values[start : start + half], values[start + half : start + HEAD_SIZE], cosine, sine
            )
        return jnp.concatenate(parts, axis=0)

    query_ref[...] = (turned(made[:, :heads].T) * (HEAD_SIZE**-0.5 / LN2)).astype(BF16)
    kv = made[:, heads:].T
    parts = []
    for start in range(0, kv.shape[0], 128):
        parts += [turned(kv[start : start + HEAD_SIZE]), kv[start + HEAD_SIZE : start + 128]]
    kv_ref[...] = jnp.concatenate(parts, axis=0).T.astype(BF16)


def project(own, other, gain, weight, cosine, sine, heads, kv_columns, tile):
    trees, rows, width = own.shape
    tiles = rows // tile
    last = trees * tiles - 1

    def place(half):
        def index(t, j):
            tree, at = t // 2, t % 2
            same = at == half
            if half == 0:
                return (jnp.where(same, tree, tree), jnp.where(same, j, tiles - 1), 0)
            return (tree, jnp.where(same, j, 0), 0)

        return index

    flat = lambda t, j: (t * tiles + j, 0)
    lanes = lambda t, j: (0, t * tiles + j)
    tokens = 2 * trees * rows
    columns = heads + kv_columns
    return pl.pallas_call(
        functools.partial(project_kernel, heads, columns),
        grid=(2 * trees, tiles),
        in_specs=[
            pl.BlockSpec((1, tile, width), place(0)),
            pl.BlockSpec((1, tile, width), place(1)),
            pl.BlockSpec((1, width), lambda t, j: (0, 0)),
            pl.BlockSpec((width, columns), lambda t, j: (0, 0)),
            pl.BlockSpec((HEAD_SIZE // 2, tile), lanes),
            pl.BlockSpec((HEAD_SIZE // 2, tile), lanes),
        ],
        out_specs=[
            pl.BlockSpec((tile, width), flat),
            pl.BlockSpec((heads, tile), lanes),
            pl.BlockSpec((tile, columns - heads), flat),
        ],
        out_shape=[
            jax.ShapeDtypeStruct((tokens, width), BF16),
            jax.ShapeDtypeStruct((heads, tokens), BF16),
            jax.ShapeDtypeStruct((tokens, columns - heads), BF16),
        ],
        scratch_shapes=[pltpu.VMEM((tile, width), F32)],
        compiler_params=pltpu.CompilerParams(vmem_limit_bytes=48 * 2**20),
        cost_estimate=SMALL,
        name="project",
    )(own, other, gain, weight, cosine, sine)


def units_kernel(
    inner_ref, grad_ref, gate_ref, up_ref, down_ref, hidden_ref, grad_gate_ref, grad_up_ref
):
    inner = inner_ref[...]
    gate = jnp.dot(inner, gate_ref[...], preferred_element_type=F32)
    up = jnp.dot(inner, up_ref[...], preferred_element_type=F32)
    grad_hidden = jnp.dot(grad_ref[...], down_ref[...], preferred_element_type=F32)
    sigmoid = jax.nn.sigmoid(gate)
    activated = gate * sigmoid
    hidden_ref[...] = (activated * up).astype(BF16)
    grad_gate_ref[...] = (grad_hidden * up * sigmoid * (1.0 + gate * (1.0 - sigmoid))).astype(BF16)
    grad_up_ref[...] = (grad_hidden * activated).astype(BF16)


def hidden_units(inner, grad, gate_up, down):
    tokens, width = inner.shape
    units = down.shape[1]
    rows, columns = math.gcd(tokens, 512), math.gcd(units, 512)
    tiles = units // columns
    tall = pl.BlockSpec((rows, width), lambda j, i: (i, 0))
    wide = pl.BlockSpec((width, columns), lambda j, i: (0, j))
    second = pl.BlockSpec((width, columns), lambda j, i: (0, tiles + j))
    tile = pl.BlockSpec((rows, columns), lambda j, i: (i, j))
    made = jax.ShapeDtypeStruct((tokens, units), BF16)
    return pl.pallas_call(
        units_kernel,
        grid=(tiles, tokens // rows),
        in_specs=[tall, tall, wide, second, wide],
        out_specs=[tile, tile, tile],
        out_shape=[made, made, made],
        compiler_params=pltpu.CompilerParams(vmem_limit_bytes=56 * 2**20),
        cost_estimate=SMALL,
        name="hidden_units",
    )(inner, grad, gate_up, gate_up, down)


def back_units_kernel(grad_gate_ref, grad_up_ref, gate_ref, up_ref, out_ref):
    contract = (((1,), (1,)), ((), ()))
    out_ref[...] = (
        lax.dot_general(grad_gate_ref[...], gate_ref[...], contract, preferred_element_type=F32)
        + lax.dot_general(grad_up_ref[...], up_ref[...], contract, preferred_element_type=F32)
    ).astype(BF16)


def back_units(tree, tokens, grad_gate, grad_up, gate_up):
    width, units = gate_up.shape[0], grad_up.shape[1]
    rows, columns = math.gcd(tokens, 1024), math.gcd(width, 512)
    first = tree * (tokens // rows)
    tall = pl.BlockSpec((rows, units), lambda j, i: (first + i, 0))
    return pl.pallas_call(
        back_units_kernel,
        grid=(width // columns, tokens // rows),
        in_specs=[
            tall,
            tall,
            pl.BlockSpec((columns, units), lambda j, i: (j, 0)),
            pl.BlockSpec((columns, units), lambda j, i: (j, 1)),
        ],
        out_specs=pl.BlockSpec((rows, columns), lambda j, i: (i, j)),
        out_shape=jax.ShapeDtypeStruct((tokens, width), BF16),
        compiler_params=pltpu.CompilerParams(vmem_limit_bytes=56 * 2**20),
        cost_estimate=SMALL,
        name="back_units",
    )(grad_gate, grad_up, gate_up, gate_up)


def unit_grads_kernel(rows_ref, grad_ref, out_ref, turned):
    @pl.when(pl.program_id(1) == 0)
    def _():
        turned[...] = rows_ref[...].T

    out_ref[...] = jnp.dot(turned[...], grad_ref[...], preferred_element_type=F32).astype(BF16)


def unit_grads(rows_in, grad):
    tokens, width = rows_in.shape
    units = grad.shape[1]
    rows, columns = math.gcd(width, 1024), math.gcd(units, 1024)
    return pl.pallas_call(
        unit_grads_kernel,
        grid=(width // rows, units // columns),
        in_specs=[
            pl.BlockSpec((tokens, rows), lambda i, j: (0, i)),
            pl.BlockSpec((tokens, columns), lambda i, j: (0, j)),
        ],
        out_specs=pl.BlockSpec((rows, columns), lambda i, j: (i, j)),
        out_shape=jax.ShapeDtypeStruct((width, units), BF16),
        scratch_shapes=[pltpu.VMEM((rows, tokens), BF16)],
        compiler_params=pltpu.CompilerParams(vmem_limit_bytes=56 * 2**20),
        cost_estimate=SMALL,
        name="unit_grads",
    )(rows_in, grad)


def shards(
    layer_in,
    out_grad,
    parents,
    seg_len,
    attn_gain,
    w_query,
    key_weight,
    value_weight,
    w_out,
    ffn_gain,
    w_gate,
    w_up,
    w_down,
):
    trees, rows, width = layer_in.shape
    ring = Ring()
    chips = ring.count
    here, core = lax.axis_index("zy"), lax.axis_index("core")
    chip_rows = 2 * rows
    keys = chips * chip_rows
    groups = KEY_VALUE_HEADS // (2 * lax.axis_size("tp"))
    rep = QUERY_HEADS // KEY_VALUE_HEADS
    heads = groups * rep
    head_cols, kv_cols = heads * HEAD_SIZE, groups * HEAD_SIZE
    block = math.gcd(rows, 256)
    per_half = rows // block
    query_blocks, key_blocks = chip_rows // block, keys // block

    def column_piece(weight):
        keep, give = split_by_core(weight, 1)
        return by_core(keep, other_core(give), 0)

    def row_piece(weight):
        keep, give = split_by_core(weight, 0)
        return by_core(keep.T, other_core(give).T, 0)

    def column_grad(total):
        keep, give = split_by_core(total, 0)
        return by_core(keep, other_core(give), 1)

    def row_grad(total):
        keep, give = split_by_core(total, 0)
        return by_core(keep, other_core(give), 1).T

    def interleave(keys, values):
        parts = []
        for group in range(groups):
            at = slice(group * HEAD_SIZE, (group + 1) * HEAD_SIZE)
            parts += [keys[:, at], values[:, at]]
        return parts

    kv_pieces = interleave(column_piece(key_weight), column_piece(value_weight))
    gains = jnp.pad(jnp.stack([attn_gain, ffn_gain], axis=1), ((0, 0), (0, 126)))
    gain_piece = by_core(gains, other_core(gains), 0)
    qkv_piece = jnp.concatenate(
        [column_piece(w_query)] + kv_pieces + [gain_piece, row_piece(w_out)], axis=1
    )
    qkv_ring = Gather(ring, [qkv_piece])
    (first_in,) = after_all((layer_in,), (qkv_piece,))
    other_in = other_core(first_in)
    hops = [qkv_ring.hop() for _ in range(chips // 2)]
    (w_attn,) = qkv_ring.finish()
    w_attn = w_attn.reshape(width, -1)
    w_qkv, gain_all, w_o = jnp.split(
        w_attn, [head_cols + 2 * kv_cols, head_cols + 2 * kv_cols + 128], axis=1
    )
    gain_all = gain_all.T[:2].astype(F32)
    gain_a, gain_f = gain_all[0], gain_all[1]

    def token_order(chip):
        first = (chip * 2 + core) * rows
        second = (chip * 2 + 1 - core) * rows
        steps = jnp.arange(rows, dtype=jnp.int32)
        return jnp.concatenate(
            [first[..., None] + steps, second[..., None] + steps], axis=-1
        ).reshape(-1)

    own_tokens = token_order(here)
    key_tokens = token_order(jnp.arange(chips, dtype=jnp.int32))
    own_block = own_tokens[::block] // block
    key_block = key_tokens[::block] // block
    diagonals = here * query_blocks + jnp.arange(query_blocks, dtype=jnp.int32)
    labels = jnp.arange(16, dtype=jnp.int32)
    tables, positions, masks, seens = [], [], [], []
    for tree in range(trees):
        row = after_all((parents[tree], seg_len[tree]), hops[min(tree, len(hops) - 1)])
        reaches, starts_at, ends_at, before = tree_tables(*row)
        seg_count = ends_at.shape[0]
        extra = 16 - seg_count
        reach16 = jnp.pad(reaches, ((0, extra), (0, extra)))
        starts16 = jnp.pad(starts_at, (0, extra))
        before16 = jnp.pad(before, (0, extra))
        ends16 = jnp.pad(ends_at, (0, extra), constant_values=2**30)
        own_seg = jnp.sum((own_tokens[:, None] >= ends_at[None, :]).astype(jnp.int32), axis=1)
        key_seg = jnp.sum((key_tokens[:, None] >= ends_at[None, :]).astype(jnp.int32), axis=1)
        member = own_seg[None, :] == labels[:, None]
        positions.append(
            own_tokens + jnp.sum(jnp.where(member, (before16 - starts16)[:, None], 0), axis=0)
        )
        seen_by = jnp.sum(
            jnp.where(member[:, None, :], reach16.astype(jnp.int32)[:, :, None], 0), axis=0
        )
        masks.append(jnp.where(seen_by > 0, 0.0, NEG).astype(BF16))
        lanes = jnp.arange(128, dtype=jnp.int32)
        key_seg_all = jnp.concatenate([key_seg, jnp.full((block,), seg_count, jnp.int32)])
        hot = (lanes[None, :] == key_seg_all[:, None]) | ((lanes >= 16) & (lanes < 19))[None, :]
        hot = hot.astype(BF16)

        def holds(blocks):
            low = blocks[:, None] * block
            return ((starts_at[None, :] < low + block) & (ends_at[None, :] > low)).astype(F32)

        linked = dot(dot(holds(own_block), reaches.astype(F32)), holds(key_block), 1, 1) > 0.5
        seen = linked & (key_block[None, :] < own_block[:, None])
        rank = jnp.cumsum(seen.astype(jnp.int32), axis=1) - 1
        slots = jnp.arange(key_blocks + 2, dtype=jnp.int32)
        index = jnp.arange(key_blocks, dtype=jnp.int32)
        chosen = seen[:, :, None] & (rank[:, :, None] == slots[None, None, :])
        lists = key_blocks + jnp.sum(
            jnp.where(chosen, index[None, :, None] - key_blocks, 0), axis=1
        )
        counts = jnp.sum(seen.astype(jnp.int32), axis=1)
        tables.append((counts, lists, diagonals, hot))
        on_diagonal = index[None, :] == diagonals[:, None]
        seens.append(jnp.where(on_diagonal, 2, seen.astype(jnp.int32)))
    position = jnp.concatenate(positions)
    angles = rope_angles(position, HEAD_SIZE)
    cosine, sine = jnp.cos(angles), jnp.sin(angles)

    inner_a, query, key_value = project(
        first_in, other_in, gain_a[None], w_attn, cosine, sine, head_cols, 2 * kv_cols,
        math.gcd(rows, 256),
    )
    cosine_rows, sine_rows = cosine.T[:, None, :], sine.T[:, None, :]
    kv_ring = Gather(ring, [key_value.reshape(trees, chip_rows, 2 * kv_cols)])
    kv_hops = [kv_ring.hop()]
    w_gate, w_up, w_down, out_grad = after_all((w_gate, w_up, w_down, out_grad), (key_value,))
    other_grad = other_core(out_grad)
    units_piece = jnp.concatenate([column_piece(w_gate), column_piece(w_up)], axis=1)
    down_piece = row_piece(w_down)
    while kv_ring.step < chips // 2 - 1:
        kv_hops.append(kv_ring.hop())
    (layer_in,) = after_all((layer_in,), kv_hops[0])
    scale_a = row_scale_of(layer_in.astype(F32))
    (out_grad,) = after_all((out_grad,), kv_hops[1])
    grad_low = jnp.concatenate([out_grad, other_grad], axis=1).reshape(trees * chip_rows, width)
    kv_hops.append(kv_ring.hop(grad_low, scale_a, units_piece, down_piece))
    units_ring = Gather(ring, [units_piece])
    units_hop = units_ring.hop(*kv_hops[-2])
    (kvs,) = kv_ring.finish()

    def core_sum(part):
        if part.ndim == 2:
            part = part.reshape(2, rows, width)
        return part[0].astype(F32) + other_core(part[1].astype(BF16)).astype(F32)

    def laid(buffer, value, tree):
        return lax.dynamic_update_slice(buffer, value[None], (tree, 0, 0))

    mixes, lses, middles, inners, normeds_f, scales_f, lows = [], [], [], [], [], [], []
    for tree in range(trees):
        mixed, lse = attend(tree, tables[tree], query, masks[tree], kvs, rep, block)
        if tree:
            units_hop += (arrived,)
        (mixed,) = after_all((mixed,), units_hop)
        units_hop = units_ring.hop(mixed)
        mixes.append(mixed)
        lses.append(lse)
        lows.append(core_sum(dot(mixed, w_o, 0, 1)).astype(BF16))
        if tree == 0:
            arrived = other_half(lows[0])
            (query,) = after_all((query,), lows)
    arrived = [after_all((arrived,), lows[1:])[0]] + [other_half(low) for low in lows[1:]]
    (layer_in,) = after_all((layer_in,), lows)
    for tree in range(trees):
        rows_in = layer_in[tree].astype(F32)
        middle = rows_in + (lows[tree].astype(F32) + arrived[tree].astype(F32))
        scale_f = row_scale_of(middle)
        normed_f = middle * scale_f
        inner = (normed_f * gain_f).astype(BF16)
        inners += [inner, other_core(inner)]
        middles.append(middle)
        scales_f.append(scale_f)
        normeds_f.append(normed_f)
    inner_f = jnp.concatenate(inners, axis=0)

    while units_ring.step < chips // 2 - 1:
        units_hop = units_ring.hop()
    down_ring = Gather(ring, [down_piece])
    down_ring.hop(*units_hop)
    down_ring.hop(arrived[-1])
    (w_units,) = units_ring.finish()
    (w_d,) = down_ring.finish()
    w_units, w_d = w_units.reshape(width, -1), w_d.reshape(width, -1)
    hidden, grad_gate, grad_up = hidden_units(inner_f, grad_low, w_units, w_d)

    def pieces(term):
        return term.astype(BF16).reshape(chips, width // chips, -1)

    spans = [slice(tree * chip_rows, (tree + 1) * chip_rows) for tree in range(trees)]
    down_ring = Reduce(ring, [pieces(unit_grads(grad_low, hidden))])
    down_hop = down_ring.hop()
    core_sums = []
    (grad_gate,) = after_all((grad_gate,), (down_ring.terms[0],))
    for tree in range(trees):
        part = back_units(tree, chip_rows, grad_gate, grad_up, w_units)
        (part,) = after_all((part,), down_hop)
        down_hop = down_ring.hop(part)
        (grad_gate,) = after_all((grad_gate,), (part,))
        core_sums.append(core_sum(part))
    lows = [own.astype(BF16) for own in core_sums]
    arrived = [other_half(lows[0])]
    inner_f, hidden = after_all((inner_f, hidden), lows)
    gate_terms = unit_grads(inner_f, grad_gate)
    (grad_up,) = after_all((grad_up,), (gate_terms, *down_hop))
    up_terms = unit_grads(inner_f, grad_up)
    up_terms, arrived[0] = after_all((up_terms, arrived[0]), (gate_terms,))
    arrived.append(other_half(after_all(lows[1:], arrived)[0]))
    gate_sum, up_sum = (
        lax.psum_scatter(terms, "zy", scatter_dimension=0, tiled=True)
        for terms in (gate_terms, up_terms)
    )
    units_hop = down_ring.hop(up_terms)
    arrived[0] = after_all(arrived[:1], (up_terms,))[0]

    grads_middle, grads_low = [], []

    def backward_norm(tree):
        grad_inner = lows[tree].astype(F32) + arrived[tree].astype(F32)
        grad_middle = out_grad[tree].astype(F32) + norm_back(
            grad_inner * gain_f, normeds_f[tree], scales_f[tree]
        )
        low = grad_middle.astype(BF16)
        grads_middle.append(grad_middle)
        grads_low.append(low)
        return jnp.concatenate([low, other_core(low)], axis=0)

    mid_lows, out_lows, out_arrived = [backward_norm(0)], [], []
    kv_rings, grad_queries, grad_kvs = [], [], []
    for tree in range(trees):
        grad_mixed = dot(w_o, mid_lows[tree], 0, 1).astype(BF16)
        for group in range(groups):
            if len(out_lows) > len(out_arrived):
                beside = other_half(out_lows[len(out_arrived)])
                out_arrived.append(beside)
                units_hop += (beside,)
            grad_query, grad_kv = attend_back(
                tree,
                group,
                seens[tree],
                tables[tree][3],
                query,
                masks[tree],
                mixes[tree],
                grad_mixed,
                lses[tree],
                kvs,
                cosine,
                sine,
                rep,
                block,
                grad_kvs[-1] if group else None,
            )
            grad_query, grad_kv = after_all((grad_query, grad_kv), units_hop)
            grad_queries.append(grad_query)
            grad_kvs.append(grad_kv)
            units_hop = ()
            for each in [down_ring] + kv_rings:
                if each.left > 0:
                    units_hop += each.hop(grad_query)
            (grad_mixed,) = after_all((grad_mixed,), (grad_query,))
            if tree == 0 and group == 0:
                (hidden,) = after_all((hidden,), (grad_query,))
                out_parts = [dot(hidden[span], w_d, 1, 1) for span in spans]
                out_parts = after_all(out_parts, arrived[1:])
                out_lows = [core_sum(part).astype(BF16) for part in out_parts]
                (grad_mixed,) = after_all((grad_mixed,), out_lows)
        kv_rings.append(Reduce(ring, grad_kvs[-1:]))
        if tree == 0:
            arrived[-1] = after_all(arrived[-1:], (grad_query,))[0]
            mid_lows.append(backward_norm(1))
            out_terms = pieces(
                dot(jnp.concatenate(mid_lows, axis=0), jnp.concatenate(mixes, axis=1), 0, 1)
            )
            kv_rings[0].hop()
            mid_lows[1] = after_all(mid_lows[1:], (out_terms,))[0]
            units_hop += kv_rings[0].hop(mid_lows[1])
            out_ring = Reduce(ring, [out_terms])
            units_hop += out_ring.hop()
            kv_rings.append(out_ring)
    out_ring = kv_rings.pop(1)
    kv_rings[1].hop()
    (down_sum,) = down_ring.finish()
    gate_sum, up_sum = gate_sum.astype(F32), up_sum.astype(F32)
    outputs = unwritten(out_terms, (trees, rows, width))
    out_arrived = after_all(out_arrived, (grad_queries[-1],))
    for tree in range(trees):
        summed = out_lows[tree].astype(F32) + out_arrived[tree].astype(F32)
        outputs = laid(outputs, (middles[tree] + summed).astype(BF16), tree)

    grads_qkv, gain_a_terms, lows = [], [], []
    (layer_in,) = after_all((layer_in,), (grad_queries[-1],))
    normed_a = layer_in.astype(F32) * scale_a
    down_grad = row_grad(down_sum)
    for tree in range(trees):
        if tree:
            while kv_rings[tree].left > 1:
                kv_rings[tree].hop(*lows)
            arrived = [other_half(lows[0])]
            kv_rings[tree].hop(*arrived)
        (kv_sums,) = kv_rings[tree].finish()
        rows_of = (cosine_rows[spans[tree]], -sine_rows[spans[tree]])
        parts = grad_queries[groups * tree : groups * (tree + 1)]
        for group in range(groups):
            kv_sum = kv_sums[:, 128 * group : 128 * (group + 1)]
            grad_k = kv_sum[:, None, :HEAD_SIZE]
            half = HEAD_SIZE // 2
            first, second = turn(grad_k[..., :half], grad_k[..., half:], *rows_of)
            kv_parts = [first[:, 0], second[:, 0], kv_sum[:, HEAD_SIZE:]]
            parts.append(jnp.concatenate(kv_parts, axis=1).astype(BF16))
        grad_qkv = jnp.concatenate(parts, axis=1)
        grads_qkv.append(grad_qkv)
        own = core_sum(dot(grad_qkv, w_qkv, 1, 1))
        gain_a_terms.append(own)
        lows.append(own.astype(BF16))
    arrived += [other_half(low) for low in lows[1:]]
    (inner_a,) = after_all((inner_a,), lows)
    (out_sum,) = out_ring.finish()
    out_proj_grad = row_grad(out_sum)
    term_qkv = unit_grads(inner_a, jnp.concatenate(grads_qkv, axis=0))
    qkv_ring = Reduce(ring, [pieces(term_qkv)])
    qkv_hop = qkv_ring.hop()
    gate_grad, up_grad = column_grad(gate_sum), column_grad(up_sum)
    core_sums = after_all(core_sums + gain_a_terms, qkv_hop)
    gain_terms = jnp.stack(
        [
            sum(jnp.sum(core_sums[trees + i] * normed_a[i], axis=0) for i in range(trees)),
            sum(jnp.sum(core_sums[i] * normeds_f[i], axis=0) for i in range(trees)),
        ]
    )
    qkv_ring.hop(gain_terms, gate_grad, up_grad, out_proj_grad, down_grad)
    qkv_ring.hop(*arrived)
    (qkv_sum,) = qkv_ring.finish()
    kv_parts = qkv_sum[:, head_cols:].reshape(-1, groups, 2, HEAD_SIZE)
    key_sum, value_sum = (kv_parts[:, :, i].reshape(-1, kv_cols) for i in range(2))

    keep, give = split_by_core(gain_terms.reshape(2, chips, 2, -1), 2)
    gain_sums = gain_sum(ring, jnp.moveaxis(keep + other_core(give), 1, 0))
    gain_sums = (gain_sums + other_half(gain_sums)).reshape(2, -1)
    gain_a_grad, gain_f_grad = gain_sums[0], gain_sums[1]
    input_grad = unwritten(scale_a, (trees, rows, width))
    for tree in range(trees):
        (theirs,) = after_all((arrived[tree],), (gain_terms,) * tree)
        grad_inner = lows[tree].astype(F32) + theirs.astype(F32)
        input_grad = laid(
            input_grad,
            grads_middle[tree] + norm_back(grad_inner * gain_a, normed_a[tree], scale_a[tree]),
            tree,
        )

    return (
        outputs,
        input_grad,
        gain_a_grad,
        column_grad(qkv_sum[:, :head_cols]),
        column_grad(key_sum),
        column_grad(value_sum),
        out_proj_grad,
        gain_f_grad,
        gate_grad,
        up_grad,
        down_grad,
    )


def gain_sum(ring, terms):
    half = ring.count // 2

    def term(offset):
        return lax.dynamic_index_in_dim(terms, ring.chip(offset), 0, keepdims=False)

    rightward, leftward = ring.go_right(term(half)), None
    for step in range(half - 1, 0, -1):
        rightward = ring.go_right(rightward + term(step))
        leftward = ring.go_left(term(-step) if leftward is None else leftward + term(-step))
    total = term(0) + rightward
    return total if leftward is None else total + leftward


def solution(mesh):
    devices = mesh.devices
    mesh = Mesh(devices.reshape(-1, 2, devices.shape[1]), ("zy", "core", "tp"))
    fsdp = ("zy", "core")
    specs = (
        P(fsdp),
        P(fsdp, "tp"),
        P(fsdp, "tp"),
        P(fsdp, "tp"),
        P("tp", fsdp),
        P(fsdp),
        P(fsdp, "tp"),
        P(fsdp, "tp"),
        P("tp", fsdp),
    )
    tokens = P(None, fsdp, None)
    return jax.shard_map(
        shards,
        mesh=mesh,
        in_specs=(tokens, tokens, P(), P()) + specs,
        out_specs=(tokens, tokens) + specs,
        check_vma=False,
    )
```

```python
import functools
import math

import jax
import jax.numpy as jnp
from jax import lax
from jax.experimental import pallas as pl
from jax.experimental.pallas import tpu as pltpu
from jax.sharding import Mesh
from jax.sharding import PartitionSpec as P

QUERY_HEADS = 32
KEY_VALUE_HEADS = 8
HEAD_SIZE = 64
LEVELS = 3

EPS = 1e-05
THETA = 500000.0
NEG = -1e30
LN2 = math.log(2.0)
SWAP = [(0, 1), (1, 0)]
F32 = jnp.float32
BF16 = jnp.bfloat16
SMALL = pl.CostEstimate(flops=2**20, bytes_accessed=2**10, transcendentals=0)


def dot(left, right, left_dim=1, right_dim=0):
    return lax.dot_general(
        left, right, (((left_dim,), (right_dim,)), ((), ())), preferred_element_type=F32
    )


def row_scale_of(rows_in):
    return lax.rsqrt(jnp.mean(rows_in * rows_in, axis=-1, keepdims=True) + EPS)


def norm_back(grad_normed, normed, row_scale):
    return row_scale * (
        grad_normed - normed * jnp.mean(grad_normed * normed, axis=-1, keepdims=True)
    )


def rope_angles(position, head_dim):
    half_dim = head_dim // 2
    index_row = jnp.arange(half_dim, dtype=F32)
    inverse = THETA ** (-2.0 * index_row / head_dim)
    wavelen = 2.0 * math.pi / inverse
    smooth = jnp.clip((8192.0 / wavelen - 1.0) / 3.0, 0.0, 1.0)
    inverse = (1.0 - smooth) * inverse / 32.0 + smooth * inverse
    return inverse[:, None] * position.astype(F32)[None, :]


def turn(first_half, second_half, cosine, sine):
    return first_half * cosine - second_half * sine, second_half * cosine + first_half * sine


def tree_tables(parents_row, lengths):
    seg_count = parents_row.shape[0]
    labels = jnp.arange(seg_count, dtype=jnp.int32)
    ends_at = jnp.cumsum(lengths)
    starts_at = ends_at - lengths
    reaches = labels[:, None] == labels[None, :]
    climber = labels
    for _ in range(LEVELS - 1):
        climber = jnp.sum(
            jnp.where(climber[:, None] == labels[None, :], parents_row[None, :], 0), axis=1
        )
        reaches = reaches | (climber[:, None] == labels[None, :])
    before = jnp.sum(
        jnp.where(reaches & (labels[:, None] != labels[None, :]), lengths[None, :], 0), axis=1
    )
    return reaches, starts_at, ends_at, before


def after_all(values, others):
    if not others:
        return list(values)
    return list(lax.optimization_barrier(tuple(values) + tuple(others))[: len(values)])


def unwritten(like, shape):
    return pl.pallas_call(
        lambda like_ref, out_ref: None,
        in_specs=[pl.BlockSpec(memory_space=pl.ANY)],
        out_specs=pl.BlockSpec(memory_space=pl.ANY),
        out_shape=jax.ShapeDtypeStruct(shape, like.dtype),
        name="buffer",
    )(like)


class Ring:
    def __init__(self):
        self.count = lax.axis_size("zy")
        count = self.count
        place = [2 * i if i < count // 2 else 2 * (count - 1 - i) + 1 for i in range(count)]
        self.right = [(place[i], place[(i + 1) % count]) for i in range(count)]
        self.left = [(b, a) for a, b in self.right]
        me = lax.axis_index("zy")
        self.spot = jnp.where(me % 2 == 0, me // 2, count - 1 - me // 2)

    def chip(self, offset):
        spot = lax.rem(self.spot + offset + self.count, self.count)
        return jnp.where(spot < self.count // 2, 2 * spot, 2 * (self.count - 1 - spot) + 1)

    def go_right(self, value):
        return lax.ppermute(value, "zy", self.right)

    def go_left(self, value):
        return lax.ppermute(value, "zy", self.left)

    def put(self, whole, part, offset, row=0):
        at = (self.chip(offset), row) + (0,) * (part.ndim - 1)
        return lax.dynamic_update_slice(whole, part[None], at)


class Gather:
    def __init__(self, ring, pieces, tidy=False):
        self.ring, self.step, self.tidy, self.laid = ring, 0, tidy, ()
        self.cuts = [piece.shape[0] // 2 for piece in pieces]
        wholes = [unwritten(piece, (ring.count,) + piece.shape) for piece in pieces]
        self.wholes = [ring.put(whole, piece, 0) for whole, piece in zip(wholes, pieces)]
        self.rightward = self.leftward = list(pieces)

    def hop(self, *others):
        ring, count = self.ring, len(self.cuts)
        both = after_all(self.rightward + self.leftward, others + self.laid)
        rightward, leftward = both[:count], both[count:]
        self.step += 1
        self.laid = tuple(self.wholes) if self.tidy else ()
        far = self.step == ring.count // 2
        if far:
            rightward = [part[:cut] for part, cut in zip(rightward, self.cuts)]
            leftward = [part[cut:] for part, cut in zip(leftward, self.cuts)]
        rightward = [ring.go_right(part) for part in rightward]
        leftward = [ring.go_left(part) for part in leftward]
        for i, cut in enumerate(self.cuts):
            whole = ring.put(self.wholes[i], rightward[i], -self.step)
            self.wholes[i] = ring.put(whole, leftward[i], self.step, cut if far else 0)
        self.rightward, self.leftward = rightward, leftward
        return tuple(rightward) + tuple(leftward)

    def finish(self, *others):
        while self.step < self.ring.count // 2:
            self.hop(*others)
        return self.wholes


class Reduce:
    def __init__(self, ring, terms):
        self.ring, self.terms, self.left = ring, list(terms), ring.count // 2
        self.cuts = [term.shape[1] // 2 for term in terms]
        self.rightward = self.leftward = None

    def each(self, offset):
        chip = self.ring.chip(offset)
        return [lax.dynamic_index_in_dim(term, chip, 0, keepdims=False) for term in self.terms]

    def hop(self, *others):
        ring, step, count = self.ring, self.left, len(self.cuts)
        if self.rightward is None:
            far = after_all(self.each(step), others)
            rightward = [part[:cut] for part, cut in zip(far, self.cuts)]
            leftward = [part[cut:] for part, cut in zip(far, self.cuts)]
        else:
            both = after_all(self.rightward + self.leftward, others)
            rightward, leftward = both[:count], both[count:]
            mine, other = self.each(step), self.each(-step)
            if step == ring.count // 2 - 1:
                for i, cut in enumerate(self.cuts):
                    parts = [add_low(mine[i][:cut], rightward[i]), mine[i][cut:]]
                    rightward[i] = jnp.concatenate(parts, axis=0)
                    parts = [other[i][:cut], add_low(other[i][cut:], leftward[i])]
                    leftward[i] = jnp.concatenate(parts, axis=0)
            else:
                rightward = [add_low(one, part) for one, part in zip(mine, rightward)]
                leftward = [add_low(one, part) for one, part in zip(other, leftward)]
        self.rightward = [ring.go_right(part) for part in rightward]
        self.leftward = [ring.go_left(part) for part in leftward]
        self.left -= 1
        return tuple(self.rightward) + tuple(self.leftward)

    def finish(self, *others):
        while self.left > 0:
            self.hop(*others)
        return [
            mine.astype(F32) + one.astype(F32) + two.astype(F32)
            for mine, one, two in zip(self.each(0), self.rightward, self.leftward)
        ]


def add_low(left, right):
    return (left.astype(F32) + right.astype(F32)).astype(BF16)


def other_core(value):
    return lax.ppermute(value, "core", SWAP)


def other_half(value):
    return lax.ppermute(value, "tp", SWAP)


def by_core(own, other, axis):
    first = lax.axis_index("core") == 0
    return jnp.concatenate(
        [jnp.where(first, own, other), jnp.where(first, other, own)], axis=axis
    )


def split_by_core(value, axis):
    core = lax.axis_index("core")
    size = value.shape[axis] // 2
    return (
        lax.dynamic_slice_in_dim(value, core * size, size, axis),
        lax.dynamic_slice_in_dim(value, (1 - core) * size, size, axis),
    )


def split3(value):
    high = value.astype(BF16)
    rest = value - high.astype(F32)
    middle = rest.astype(BF16)
    low = (rest - middle.astype(F32)).astype(BF16)
    return high, middle, low


def causal(scores, block):
    key_at = lax.broadcasted_iota(jnp.int32, scores.shape, 0)
    query_at = lax.rem(lax.broadcasted_iota(jnp.int32, scores.shape, 1), block)
    return jnp.where(key_at <= query_at, scores, NEG)


def block_of(ref, index, block, per_piece):
    piece = lax.div(index, per_piece)
    start = pl.multiple_of(lax.rem(index, per_piece) * block, block)
    return ref[piece, 0, pl.ds(start, block), :]


def attend_kernel(
    block, rep, per_piece, count_ref, list_ref, diag_ref, query_ref, mask_ref, kv_ref, hot_ref,
    out_ref, lse_ref, query_aug, turned,
):
    at = pl.program_id(1)
    key_blocks = hot_ref.shape[0] // block - 1

    @pl.when(at == 0)
    def _():
        rows = per_piece * block
        for piece in range(kv_ref.shape[0]):
            turned[:, piece * rows : (piece + 1) * rows] = kv_ref[piece, 0].T

    query_aug[HEAD_SIZE:, :] = jnp.zeros_like(query_aug[HEAD_SIZE:, :])
    for r in range(rep):
        columns = slice(r * block, (r + 1) * block)
        query_aug[:HEAD_SIZE, columns] = query_ref[r * HEAD_SIZE : (r + 1) * HEAD_SIZE, :]
        query_aug[128:144, columns] = mask_ref[...]

    def scores_of(index):
        keys = block_of(kv_ref, jnp.minimum(index, key_blocks - 1), block, per_piece)
        hot = hot_ref[pl.ds(pl.multiple_of(index * block, block), block), :]
        return jnp.dot(
            jnp.concatenate([keys, hot], axis=1), query_aug[...], preferred_element_type=F32
        )

    def values_of(index):
        index = jnp.minimum(index, key_blocks - 1)
        return turned[HEAD_SIZE:, pl.ds(pl.multiple_of(index * block, block), block)]

    diagonal = diag_ref[at]
    scores = causal(scores_of(diagonal), block)
    top = jnp.max(scores, axis=0, keepdims=True)
    probs = jnp.exp2(scores - top)
    total = jnp.sum(probs, axis=0, keepdims=True)
    mixed = jnp.dot(values_of(diagonal), probs.astype(BF16), preferred_element_type=F32)

    def step(j, carry):
        top, total, mixed = carry
        one, two = list_ref[at, 2 * j], list_ref[at, 2 * j + 1]
        first, second = scores_of(one), scores_of(two)
        new = jnp.maximum(top, jnp.max(first, axis=0, keepdims=True))
        new = jnp.maximum(new, jnp.max(second, axis=0, keepdims=True))
        factor = jnp.exp2(top - new)
        first, second = jnp.exp2(first - new), jnp.exp2(second - new)
        total = (
            total * factor
            + jnp.sum(first, axis=0, keepdims=True)
            + jnp.sum(second, axis=0, keepdims=True)
        )
        values = jnp.concatenate([values_of(one), values_of(two)], axis=1)
        probs = jnp.concatenate([first.astype(BF16), second.astype(BF16)], axis=0)
        mixed = mixed * factor + jnp.dot(values, probs, preferred_element_type=F32)
        return new, total, mixed

    pairs = lax.div(count_ref[at] + 1, 2)
    top, total, mixed = lax.fori_loop(0, pairs, step, (top, total, mixed))
    mixed = mixed * (1.0 / total)
    lse = top + jnp.log2(total)
    for r in range(rep):
        columns = slice(r * block, (r + 1) * block)
        out_ref[r * HEAD_SIZE : (r + 1) * HEAD_SIZE, :] = mixed[:, columns].astype(BF16)
        lse_ref[0, r : r + 1, :] = lse[:, columns]


def attend(tree, tables, query, mask, kv, rep, block):
    counts, lists, diagonals, hot = tables
    heads = query.shape[0]
    pieces, _, rows, _ = kv.shape
    groups, query_blocks = heads // (rep * HEAD_SIZE), rows // block
    keys = pieces * rows
    grid_spec = pltpu.PrefetchScalarGridSpec(
        num_scalar_prefetch=3,
        grid=(groups, query_blocks),
        in_specs=[
            pl.BlockSpec(
                (rep * HEAD_SIZE, block), lambda g, q, *_: (g, tree * query_blocks + q)
            ),
            pl.BlockSpec((16, block), lambda g, q, *_: (0, q)),
            pl.BlockSpec((pieces, 1, rows, 128), lambda g, q, *_: (0, tree, 0, g)),
            pl.BlockSpec((keys + block, 128), lambda g, q, *_: (0, 0)),
        ],
        out_specs=[
            pl.BlockSpec((rep * HEAD_SIZE, block), lambda g, q, *_: (g, q)),
            pl.BlockSpec((1, rep, block), lambda g, q, *_: (g, 0, q)),
        ],
        scratch_shapes=[
            pltpu.VMEM((256, rep * block), BF16),
            pltpu.VMEM((128, keys), BF16),
        ],
    )
    return pl.pallas_call(
        functools.partial(attend_kernel, block, rep, rows // block),
        grid_spec=grid_spec,
        out_shape=[
            jax.ShapeDtypeStruct((heads, rows), BF16),
            jax.ShapeDtypeStruct((groups, rep, rows), F32),
        ],
        compiler_params=pltpu.CompilerParams(vmem_limit_bytes=48 * 2**20),
        cost_estimate=SMALL,
        name="tree_attention",
    )(counts, lists, diagonals, query, mask, kv, hot)


def attend_back_kernel(
    block, rep, per_piece, seen_ref, query_ref, mask_ref, mixed_ref, grad_ref, lse_ref, kv_ref,
    hot_ref, cosine_ref, sine_ref, before_ref, grad_query_ref, grad_kv_ref, augs, turned_rows,
    key_turned, grad_query, grad_kv,
):
    rows = per_piece * block
    query_blocks = rows // block
    key_blocks = kv_ref.shape[0] * per_piece
    width = rep * block

    for piece in range(kv_ref.shape[0]):
        key_turned[:, piece * rows : (piece + 1) * rows] = kv_ref[piece, 0].T
    grad_kv[...] = jnp.zeros_like(grad_kv)
    grad_query[...] = jnp.zeros_like(grad_query)
    augs[...] = jnp.zeros_like(augs)
    none = jnp.zeros((HEAD_SIZE, block), BF16)
    for at in range(query_blocks):
        columns = slice(at * block, (at + 1) * block)
        for r in range(rep):
            here = slice(2 * at * width + r * block, 2 * at * width + (r + 1) * block)
            there = slice((2 * at + 1) * width + r * block, (2 * at + 1) * width + (r + 1) * block)
            head = slice(r * HEAD_SIZE, (r + 1) * HEAD_SIZE)
            query, grad = query_ref[head, columns], grad_ref[head, columns]
            augs[:HEAD_SIZE, here] = query
            augs[HEAD_SIZE : 2 * HEAD_SIZE, there] = grad
            delta = jnp.sum(
                grad.astype(F32) * mixed_ref[head, columns].astype(F32), axis=0, keepdims=True
            )
            empty = jnp.zeros((13, block), BF16)
            augs[128:160, here] = jnp.concatenate(
                [mask_ref[:, columns], *split3(-lse_ref[0, r : r + 1, columns]), empty], axis=0
            )
            augs[128:160, there] = jnp.concatenate(
                [jnp.zeros((16, block), BF16), *split3(-delta), empty], axis=0
            )
            turned_rows[here, :] = jnp.concatenate([none, grad], axis=0).T
            turned_rows[there, :] = jnp.concatenate([query, none], axis=0).T

    def over_keys(index, _):
        rows_at = pl.ds(pl.multiple_of(index * block, block), block)
        for at in range(query_blocks):
            columns = slice(2 * at * width, (2 * at + 2) * width)

            def work(on_diagonal):
                both = jnp.dot(
                    jnp.concatenate(
                        [block_of(kv_ref, index, block, per_piece), hot_ref[rows_at, :]], axis=1
                    ),
                    augs[:, columns],
                    preferred_element_type=F32,
                )
                scores, grad_probs = both[:, :width], both[:, width:]
                if on_diagonal:
                    scores = causal(scores, block)
                probs = jnp.exp2(scores)
                grad_scores = (probs * grad_probs).astype(BF16)
                grad_kv[rows_at, :] += jnp.dot(
                    jnp.concatenate([probs.astype(BF16), grad_scores], axis=1),
                    turned_rows[columns, :],
                    preferred_element_type=F32,
                )
                grad_query[:, at * width : (at + 1) * width] += jnp.dot(
                    key_turned[:HEAD_SIZE, rows_at], grad_scores, preferred_element_type=F32
                )

            seen = seen_ref[at, index]
            pl.when(seen == 1)(functools.partial(work, False))
            pl.when(seen == 2)(functools.partial(work, True))
        return 0

    lax.fori_loop(0, key_blocks, over_keys, 0)
    for at in range(query_blocks):
        columns = slice(at * block, (at + 1) * block)
        cosine = cosine_ref[:, columns] * HEAD_SIZE**-0.5
        sine = -sine_ref[:, columns] * HEAD_SIZE**-0.5
        for r in range(0, rep, 2):
            parts = []
            for head in (r, r + 1):
                here = slice(at * width + head * block, at * width + (head + 1) * block)
                grad = grad_query[:, here]
                half = HEAD_SIZE // 2
                parts += turn(grad[:half], grad[half:], cosine, sine)
            grad_query_ref[columns, r * HEAD_SIZE : (r + 2) * HEAD_SIZE] = (
                jnp.concatenate(parts, axis=0).T.astype(BF16)
            )
    for piece in range(kv_ref.shape[0]):
        grads = grad_kv[piece * rows : (piece + 1) * rows, :]
        lanes = lax.broadcasted_iota(jnp.int32, grads.shape, 1)
        grad_kv_ref[piece] = jnp.where(lanes < HEAD_SIZE, grads * LN2, grads).astype(BF16)


def attend_back(
    tree, group, seen, hot, query, mask, mixed, grad, lse, kv, cosine, sine, rep, block, before
):
    pieces, _, rows, _ = kv.shape
    keys = pieces * rows
    heads = rep * HEAD_SIZE
    head = pl.BlockSpec((heads, rows), lambda i, *_: (group, 0))
    table = pl.BlockSpec((HEAD_SIZE // 2, rows), lambda i, *_: (0, tree))
    grid_spec = pltpu.PrefetchScalarGridSpec(
        num_scalar_prefetch=1,
        grid=(1,),
        in_specs=[
            pl.BlockSpec((heads, rows), lambda i, *_: (group, tree)),
            pl.BlockSpec((16, rows), lambda i, *_: (0, 0)),
            head,
            head,
            pl.BlockSpec((1, rep, rows), lambda i, *_: (group, 0, 0)),
            pl.BlockSpec((pieces, 1, rows, 128), lambda i, *_: (0, tree, 0, group)),
            pl.BlockSpec((keys + block, 128), lambda i, *_: (0, 0)),
            table,
            table,
            pl.BlockSpec(memory_space=pl.ANY),
        ],
        out_specs=[
            pl.BlockSpec((rows, heads), lambda i, *_: (0, 0)),
            pl.BlockSpec((pieces, rows, 128), lambda i, *_: (0, 0, group)),
        ],
        scratch_shapes=[
            pltpu.VMEM((256, 2 * rep * rows), BF16),
            pltpu.VMEM((2 * rep * rows, 128), BF16),
            pltpu.VMEM((128, keys), BF16),
            pltpu.VMEM((HEAD_SIZE, rep * rows), F32),
            pltpu.VMEM((keys, 128), F32),
        ],
    )
    return pl.pallas_call(
        functools.partial(attend_back_kernel, block, rep, rows // block),
        grid_spec=grid_spec,
        out_shape=[
            jax.ShapeDtypeStruct((rows, heads), BF16),
            jax.ShapeDtypeStruct((pieces, rows, kv.shape[3]), BF16),
        ],
        input_output_aliases={10: 1} if group else {},
        compiler_params=pltpu.CompilerParams(vmem_limit_bytes=56 * 2**20),
        cost_estimate=SMALL,
        name="tree_attention_back",
    )(seen, query, mask, mixed, grad, lse, kv, hot, cosine, sine, cosine if before is None else before)


def project_kernel(
    heads, columns, own_ref, other_ref, gain_ref, weight_ref, cosine_ref, sine_ref, inner_ref, query_ref,
    kv_ref, rows,
):
    mine = lax.rem(pl.program_id(0), 2) == 0

    @pl.when(mine)
    def _():
        rows[...] = own_ref[0].astype(F32)

    @pl.when(jnp.logical_not(mine))
    def _():
        rows[...] = other_ref[0].astype(F32)

    x = rows[...]
    inner = (x * row_scale_of(x) * gain_ref[...]).astype(BF16)
    inner_ref[...] = inner
    made = jnp.dot(inner, weight_ref[:, :columns], preferred_element_type=F32)
    cosine, sine = cosine_ref[...], sine_ref[...]
    half = HEAD_SIZE // 2

    def turned(values):
        parts = []
        for start in range(0, values.shape[0], HEAD_SIZE):
            parts += turn(
                values[start : start + half], values[start + half : start + HEAD_SIZE], cosine, sine
            )
        return jnp.concatenate(parts, axis=0)

    query_ref[...] = (turned(made[:, :heads].T) * (HEAD_SIZE**-0.5 / LN2)).astype(BF16)
    kv = made[:, heads:].T
    parts = []
    for start in range(0, kv.shape[0], 128):
        parts += [turned(kv[start : start + HEAD_SIZE]), kv[start + HEAD_SIZE : start + 128]]
    kv_ref[...] = jnp.concatenate(parts, axis=0).T.astype(BF16)


def project(own, other, gain, weight, cosine, sine, heads, kv_columns, tile):
    trees, rows, width = own.shape
    tiles = rows // tile
    last = trees * tiles - 1

    def place(half):
        def index(t, j):
            tree, at = t // 2, t % 2
            same = at == half
            if half == 0:
                return (jnp.where(same, tree, tree), jnp.where(same, j, tiles - 1), 0)
            return (tree, jnp.where(same, j, 0), 0)

        return index

    flat = lambda t, j: (t * tiles + j, 0)
    lanes = lambda t, j: (0, t * tiles + j)
    tokens = 2 * trees * rows
    columns = heads + kv_columns
    return pl.pallas_call(
        functools.partial(project_kernel, heads, columns),
        grid=(2 * trees, tiles),
        in_specs=[
            pl.BlockSpec((1, tile, width), place(0)),
            pl.BlockSpec((1, tile, width), place(1)),
            pl.BlockSpec((1, width), lambda t, j: (0, 0)),
            pl.BlockSpec((width, columns), lambda t, j: (0, 0)),
            pl.BlockSpec((HEAD_SIZE // 2, tile), lanes),
            pl.BlockSpec((HEAD_SIZE // 2, tile), lanes),
        ],
        out_specs=[
            pl.BlockSpec((tile, width), flat),
            pl.BlockSpec((heads, tile), lanes),
            pl.BlockSpec((tile, columns - heads), flat),
        ],
        out_shape=[
            jax.ShapeDtypeStruct((tokens, width), BF16),
            jax.ShapeDtypeStruct((heads, tokens), BF16),
            jax.ShapeDtypeStruct((tokens, columns - heads), BF16),
        ],
        scratch_shapes=[pltpu.VMEM((tile, width), F32)],
        compiler_params=pltpu.CompilerParams(vmem_limit_bytes=48 * 2**20),
        cost_estimate=SMALL,
        name="project",
    )(own, other, gain, weight, cosine, sine)


def units_kernel(
    inner_ref, grad_ref, gate_ref, up_ref, down_ref, hidden_ref, grad_gate_ref, grad_up_ref
):
    inner = inner_ref[...]
    gate = jnp.dot(inner, gate_ref[...], preferred_element_type=F32)
    up = jnp.dot(inner, up_ref[...], preferred_element_type=F32)
    grad_hidden = jnp.dot(grad_ref[...], down_ref[...], preferred_element_type=F32)
    sigmoid = jax.nn.sigmoid(gate)
    activated = gate * sigmoid
    hidden_ref[...] = (activated * up).astype(BF16)
    grad_gate_ref[...] = (grad_hidden * up * sigmoid * (1.0 + gate * (1.0 - sigmoid))).astype(BF16)
    grad_up_ref[...] = (grad_hidden * activated).astype(BF16)


def hidden_units(inner, grad, weights, down):
    tokens, width = inner.shape
    units = down.shape[1]
    rows, columns = math.gcd(tokens, 512), math.gcd(units, 512)
    tiles = units // columns
    tall = pl.BlockSpec((rows, width), lambda j, i: (i, 0))
    wide = [
        pl.BlockSpec((width, columns), lambda j, i, first=first: (0, first + j))
        for first in (0, tiles, 0)
    ]
    tile = pl.BlockSpec((rows, columns), lambda j, i: (i, j))
    made = jax.ShapeDtypeStruct((tokens, units), BF16)
    return pl.pallas_call(
        units_kernel,
        grid=(tiles, tokens // rows),
        in_specs=[tall, tall, *wide],
        out_specs=[tile, tile, tile],
        out_shape=[made, made, made],
        compiler_params=pltpu.CompilerParams(vmem_limit_bytes=56 * 2**20),
        cost_estimate=SMALL,
        name="hidden_units",
    )(inner, grad, weights, weights, down)


def back_units_kernel(count, *refs):
    *refs, out_ref = refs
    contract = (((1,), (1,)), ((), ()))
    total = None
    for units_ref, weight_ref in zip(refs[:count], refs[count:]):
        term = lax.dot_general(
            units_ref[...], weight_ref[...], contract, preferred_element_type=F32
        )
        total = term if total is None else total + term
    out_ref[...] = total.astype(BF16)


def back_units(tree, tokens, units, weights, places):
    width, size = weights.shape[0], units[0].shape[1]
    rows, columns = math.gcd(tokens, 1024), math.gcd(width, 512)
    first = tree * (tokens // rows)
    tall = pl.BlockSpec((rows, size), lambda j, i: (first + i, 0))
    return pl.pallas_call(
        functools.partial(back_units_kernel, len(units)),
        grid=(width // columns, tokens // rows),
        in_specs=[tall] * len(units)
        + [pl.BlockSpec((columns, size), lambda j, i, at=at: (j, at)) for at in places],
        out_specs=pl.BlockSpec((rows, columns), lambda j, i: (i, j)),
        out_shape=jax.ShapeDtypeStruct((tokens, width), BF16),
        compiler_params=pltpu.CompilerParams(vmem_limit_bytes=56 * 2**20),
        cost_estimate=SMALL,
        name="back_units",
    )(*units, *([weights] * len(units)))


def unit_grads_kernel(tiles, rows_ref, *refs):
    *grad_refs, out_ref, turned = refs
    at = pl.program_id(1)

    @pl.when(at == 0)
    def _():
        turned[...] = rows_ref[...].T

    for i, grad_ref in enumerate(grad_refs):

        @pl.when((at >= i * tiles) & (at < (i + 1) * tiles))
        def _():
            out_ref[...] = jnp.dot(
                turned[...], grad_ref[...], preferred_element_type=F32
            ).astype(BF16)


def unit_grads(rows_in, *grads):
    tokens, width = rows_in.shape
    units = grads[0].shape[1]
    rows, columns = math.gcd(width, 1024), math.gcd(units, 1024 // len(grads))
    tiles = units // columns

    def place(i):
        return lambda at, j: (0, jnp.clip(j - i * tiles, 0, tiles - 1))

    return pl.pallas_call(
        functools.partial(unit_grads_kernel, tiles),
        grid=(width // rows, tiles * len(grads)),
        in_specs=[pl.BlockSpec((tokens, rows), lambda i, j: (0, i))]
        + [pl.BlockSpec((tokens, columns), place(i)) for i in range(len(grads))],
        out_specs=pl.BlockSpec((rows, columns), lambda i, j: (i, j)),
        out_shape=jax.ShapeDtypeStruct((width, units * len(grads)), BF16),
        scratch_shapes=[pltpu.VMEM((rows, tokens), BF16)],
        compiler_params=pltpu.CompilerParams(vmem_limit_bytes=56 * 2**20),
        cost_estimate=SMALL,
        name="unit_grads",
    )(rows_in, *grads)


def ring_place(spot, count):
    spot = lax.rem(spot + count, count)
    return jnp.where(spot < count // 2, 2 * spot, 2 * (count - 1 - spot) + 1)


def ring_sum_kernel(count, arrays, swaps, *refs):
    terms_refs, refs = refs[:arrays], refs[arrays:]
    if swaps:
        swap_ref, *refs, swap_send, swap_receive = refs
    out_refs, refs = refs[:arrays], refs[arrays:]
    if swaps:
        theirs_ref, *refs = refs
    helds, from_lefts, from_rights = (refs[i * arrays : (i + 1) * arrays] for i in range(3))
    load_sems, send_sems, receive_sems = refs[3 * arrays :]
    half = count // 2
    me = lax.axis_index("zy")
    spot = jnp.where(lax.rem(me, 2) == 0, lax.div(me, 2), count - 1 - lax.div(me, 2))
    right, left = ring_place(spot + 1, count), ring_place(spot - 1, count)

    barrier = pltpu.get_barrier_semaphore()
    for neighbour in (right, left):
        pl.semaphore_signal(
            barrier, inc=1, device_id={"zy": neighbour}, device_id_type=pl.DeviceIdType.MESH
        )
    other = {"tp": 1 - lax.axis_index("tp")}
    if swaps:
        pl.semaphore_signal(
            barrier, inc=1, device_id=other, device_id_type=pl.DeviceIdType.MESH
        )
    order = [half]
    for step in range(half - 1, 0, -1):
        order += [step, count - step]
    order.append(0)
    loads = {}
    for k in order:
        for i in range(arrays):
            loads[i, k] = pltpu.make_async_copy(
                terms_refs[i].at[ring_place(spot + k, count)], helds[i].at[k], load_sems.at[i, k]
            )
            loads[i, k].start()
    pl.semaphore_wait(barrier, 3 if swaps else 2)
    if swaps:
        swap = pltpu.make_async_remote_copy(
            src_ref=swap_ref,
            dst_ref=theirs_ref,
            send_sem=swap_send,
            recv_sem=swap_receive,
            device_id=other,
            device_id_type=pl.DeviceIdType.MESH,
        )
        swap.start()

    copies = {}

    def send(i, hop, way, source, target):
        copies[i, hop, way] = pltpu.make_async_remote_copy(
            src_ref=source,
            dst_ref=target,
            send_sem=send_sems.at[i, way, hop],
            recv_sem=receive_sems.at[i, way, hop],
            device_id={"zy": (right, left)[way]},
            device_id_type=pl.DeviceIdType.MESH,
        )
        copies[i, hop, way].start()

    def halves(i):
        cut = helds[i].shape[1] // 2
        return pl.ds(0, cut), pl.ds(cut, cut)

    for i in range(arrays):
        loads[i, half].wait()
        for way, arrived in enumerate((from_lefts[i], from_rights[i])):
            at = halves(i)[way]
            send(i, 0, way, helds[i].at[half, at], arrived.at[0, at])
    for hop in range(1, half):
        step = half - hop
        for i in range(arrays):
            for way, k in enumerate((step, count - step)):
                held, arrived = helds[i], (from_lefts[i], from_rights[i])[way]
                loads[i, k].wait()
                copies[i, hop - 1, way].wait_recv()
                at = halves(i)[way] if hop == 1 else slice(None)
                held[k, at, :] = (
                    held[k, at, :].astype(F32) + arrived[hop - 1, at, :].astype(F32)
                ).astype(BF16)
                send(i, hop, way, held.at[k], arrived.at[hop])
    for i in range(arrays):
        loads[i, 0].wait()
        for way in range(2):
            copies[i, half - 1, way].wait_recv()
        out_refs[i][...] = (
            helds[i][0].astype(F32)
            + from_lefts[i][half - 1].astype(F32)
            + from_rights[i][half - 1].astype(F32)
        )
    for copy in copies.values():
        copy.wait_send()
    if swaps:
        swap.wait()


def ring_sum(terms, collective_id, swap=None):
    arrays, count = len(terms), terms[0].shape[0]
    half = count // 2
    swaps = swap is not None
    anywhere = pl.BlockSpec(memory_space=pl.ANY)
    shapes = [term.shape[1:] for term in terms]
    return pl.pallas_call(
        functools.partial(ring_sum_kernel, count, arrays, swaps),
        in_specs=[anywhere] * (arrays + swaps),
        out_specs=[pl.BlockSpec(memory_space=pltpu.VMEM)] * arrays + [anywhere] * swaps,
        out_shape=[jax.ShapeDtypeStruct(shape, F32) for shape in shapes]
        + ([jax.ShapeDtypeStruct(swap.shape, swap.dtype)] if swaps else []),
        scratch_shapes=[pltpu.VMEM((count, *shape), BF16) for shape in shapes]
        + [pltpu.VMEM((half, *shape), BF16) for shape in shapes + shapes]
        + [
            pltpu.SemaphoreType.DMA((arrays, count)),
            pltpu.SemaphoreType.DMA((arrays, 2, half)),
            pltpu.SemaphoreType.DMA((arrays, 2, half)),
        ]
        + [pltpu.SemaphoreType.DMA] * (2 * swaps),
        compiler_params=pltpu.CompilerParams(
            collective_id=collective_id, has_side_effects=True, vmem_limit_bytes=48 * 2**20
        ),
        cost_estimate=SMALL,
        name="ring_sum",
    )(*terms, *([swap] if swaps else []))


def shards(
    layer_in,
    out_grad,
    parents,
    seg_len,
    attn_gain,
    w_query,
    key_weight,
    value_weight,
    w_out,
    ffn_gain,
    w_gate,
    w_up,
    w_down,
):
    trees, rows, width = layer_in.shape
    ring = Ring()
    chips = ring.count
    here, core = lax.axis_index("zy"), lax.axis_index("core")
    chip_rows = 2 * rows
    keys = chips * chip_rows
    groups = KEY_VALUE_HEADS // (2 * lax.axis_size("tp"))
    rep = QUERY_HEADS // KEY_VALUE_HEADS
    heads = groups * rep
    head_cols, kv_cols = heads * HEAD_SIZE, groups * HEAD_SIZE
    block = math.gcd(rows, 256)
    per_half = rows // block
    query_blocks, key_blocks = chip_rows // block, keys // block

    def column_piece(weight):
        keep, give = split_by_core(weight, 1)
        return by_core(keep, other_core(give), 0)

    def row_piece(weight):
        keep, give = split_by_core(weight, 0)
        return by_core(keep.T, other_core(give).T, 0)

    def column_grad(total):
        keep, give = split_by_core(total, 0)
        return by_core(keep, other_core(give), 1)

    def row_grad(total):
        keep, give = split_by_core(total, 0)
        return by_core(keep, other_core(give), 1).T

    def interleave(keys, values):
        parts = []
        for group in range(groups):
            at = slice(group * HEAD_SIZE, (group + 1) * HEAD_SIZE)
            parts += [keys[:, at], values[:, at]]
        return parts

    kv_pieces = interleave(column_piece(key_weight), column_piece(value_weight))
    gains = jnp.pad(jnp.stack([attn_gain, ffn_gain], axis=1), ((0, 0), (0, 126)))
    gain_piece = by_core(gains, other_core(gains), 0)
    qkv_piece = jnp.concatenate(
        [column_piece(w_query)] + kv_pieces + [gain_piece, row_piece(w_out)], axis=1
    )
    qkv_ring = Gather(ring, [qkv_piece], True)
    (first_in,) = after_all((layer_in,), (qkv_piece,))
    other_in = other_core(first_in)
    hops = [qkv_ring.hop()]
    w_gate, w_up, w_down = after_all((w_gate, w_up, w_down), hops[0])
    down_piece = row_piece(w_down)
    units_piece = unwritten(w_gate, (width // chips, w_gate.shape[1]))
    for at, piece in enumerate((column_piece(w_gate), column_piece(w_up))):
        units_piece = lax.dynamic_update_slice(units_piece, piece, (0, at * piece.shape[1]))
    while qkv_ring.step < chips // 2 - 1:
        hops.append(qkv_ring.hop())
    down_ring = Gather(ring, [down_piece])
    hops.append(qkv_ring.hop(down_piece))
    down_hop = down_ring.hop(*hops[-1])
    (w_attn,) = qkv_ring.finish()
    w_attn = w_attn.reshape(width, -1)
    w_qkv, gain_all, w_o = jnp.split(
        w_attn, [head_cols + 2 * kv_cols, head_cols + 2 * kv_cols + 128], axis=1
    )
    gain_all = gain_all.T[:2].astype(F32)
    gain_a, gain_f = gain_all[0], gain_all[1]

    def token_order(chip):
        first = (chip * 2 + core) * rows
        second = (chip * 2 + 1 - core) * rows
        steps = jnp.arange(rows, dtype=jnp.int32)
        return jnp.concatenate(
            [first[..., None] + steps, second[..., None] + steps], axis=-1
        ).reshape(-1)

    own_tokens = token_order(here)
    key_tokens = token_order(jnp.arange(chips, dtype=jnp.int32))
    own_block = own_tokens[::block] // block
    key_block = key_tokens[::block] // block
    diagonals = here * query_blocks + jnp.arange(query_blocks, dtype=jnp.int32)
    labels = jnp.arange(16, dtype=jnp.int32)
    tables, positions, masks, seens = [], [], [], []
    for tree in range(trees):
        row = after_all((parents[tree], seg_len[tree]), hops[min(tree, len(hops) - 1)])
        reaches, starts_at, ends_at, before = tree_tables(*row)
        seg_count = ends_at.shape[0]
        extra = 16 - seg_count
        reach16 = jnp.pad(reaches, ((0, extra), (0, extra)))
        starts16 = jnp.pad(starts_at, (0, extra))
        before16 = jnp.pad(before, (0, extra))
        ends16 = jnp.pad(ends_at, (0, extra), constant_values=2**30)
        own_seg = jnp.sum((own_tokens[:, None] >= ends_at[None, :]).astype(jnp.int32), axis=1)
        key_seg = jnp.sum((key_tokens[:, None] >= ends_at[None, :]).astype(jnp.int32), axis=1)
        member = own_seg[None, :] == labels[:, None]
        positions.append(
            own_tokens + jnp.sum(jnp.where(member, (before16 - starts16)[:, None], 0), axis=0)
        )
        seen_by = jnp.sum(
            jnp.where(member[:, None, :], reach16.astype(jnp.int32)[:, :, None], 0), axis=0
        )
        masks.append(jnp.where(seen_by > 0, 0.0, NEG).astype(BF16))
        lanes = jnp.arange(128, dtype=jnp.int32)
        key_seg_all = jnp.concatenate([key_seg, jnp.full((block,), seg_count, jnp.int32)])
        hot = (lanes[None, :] == key_seg_all[:, None]) | ((lanes >= 16) & (lanes < 19))[None, :]
        hot = hot.astype(BF16)

        def holds(blocks):
            low = blocks[:, None] * block
            return ((starts_at[None, :] < low + block) & (ends_at[None, :] > low)).astype(F32)

        linked = dot(dot(holds(own_block), reaches.astype(F32)), holds(key_block), 1, 1) > 0.5
        seen = linked & (key_block[None, :] < own_block[:, None])
        rank = jnp.cumsum(seen.astype(jnp.int32), axis=1) - 1
        slots = jnp.arange(key_blocks + 2, dtype=jnp.int32)
        index = jnp.arange(key_blocks, dtype=jnp.int32)
        chosen = seen[:, :, None] & (rank[:, :, None] == slots[None, None, :])
        lists = key_blocks + jnp.sum(
            jnp.where(chosen, index[None, :, None] - key_blocks, 0), axis=1
        )
        counts = jnp.sum(seen.astype(jnp.int32), axis=1)
        tables.append((counts, lists, diagonals, hot))
        on_diagonal = index[None, :] == diagonals[:, None]
        seens.append(jnp.where(on_diagonal, 2, seen.astype(jnp.int32)))
    position = jnp.concatenate(positions)
    (position,) = after_all((position,), hops[-2])
    angles = rope_angles(position, HEAD_SIZE)
    cosine, sine = jnp.cos(angles), jnp.sin(angles)

    inner_a, query, key_value = project(
        first_in, other_in, gain_a[None], w_attn, cosine, sine, head_cols, 2 * kv_cols,
        math.gcd(rows, 256),
    )
    query, key_value = after_all((query, key_value), down_hop)
    cosine_rows, sine_rows = cosine.T[:, None, :], sine.T[:, None, :]
    kv_ring = Gather(ring, [key_value.reshape(trees, chip_rows, 2 * kv_cols)], True)
    kv_hops = [kv_ring.hop()]
    kv_hops.append(kv_ring.hop())
    (out_grad,) = after_all((out_grad,), (key_value,))
    other_grad = other_core(out_grad)
    while kv_ring.step < chips // 2 - 1:
        kv_hops.append(kv_ring.hop())
    (layer_in,) = after_all((layer_in,), (key_value,))
    scale_a = row_scale_of(layer_in.astype(F32))
    (out_grad,) = after_all((out_grad,), kv_hops[0])
    grad_low = jnp.concatenate([out_grad, other_grad], axis=1).reshape(trees * chip_rows, width)
    kv_hops.append(kv_ring.hop(grad_low, scale_a))
    units_ring = Gather(ring, [units_piece])
    units_hop = units_ring.hop(*kv_hops[-1])
    units_hop += down_ring.hop(*kv_hops[-1])
    (kvs,) = kv_ring.finish()

    def core_sum(part):
        if part.ndim == 2:
            part = part.reshape(2, rows, width)
        return part[0].astype(F32) + other_core(part[1].astype(BF16)).astype(F32)

    def laid(buffer, value, tree):
        return lax.dynamic_update_slice(buffer, value[None], (tree, 0, 0))

    mixes, lses, middles, inners, normeds_f, scales_f, lows = [], [], [], [], [], [], []
    for tree in range(trees):
        mixed, lse = attend(tree, tables[tree], query, masks[tree], kvs, rep, block)
        (mixed,) = after_all((mixed,), units_hop + ((arrived,) if tree else ()))
        units_hop = units_ring.hop(mixed)
        if down_ring.step < chips // 2:
            units_hop += down_ring.hop(mixed)
        mixes.append(mixed)
        lses.append(lse)
        lows.append(core_sum(dot(mixed, w_o, 0, 1)).astype(BF16))
        if tree == 0:
            arrived = other_half(lows[0])
            (query,) = after_all((query,), lows)
    arrived = [after_all((arrived,), lows[1:])[0]] + [other_half(low) for low in lows[1:]]
    (layer_in,) = after_all((layer_in,), lows)
    for tree in range(trees):
        rows_in = layer_in[tree].astype(F32)
        middle = rows_in + (lows[tree].astype(F32) + arrived[tree].astype(F32))
        scale_f = row_scale_of(middle)
        normed_f = middle * scale_f
        inner = (normed_f * gain_f).astype(BF16)
        inners += [inner, other_core(inner)]
        middles.append(middle)
        scales_f.append(scale_f)
        normeds_f.append(normed_f)
    inner_f = jnp.concatenate(inners, axis=0)

    (w_units,) = units_ring.finish()
    (w_d,) = down_ring.finish()
    w_units, w_d = w_units.reshape(width, -1), w_d.reshape(width, -1)
    hidden, grad_gate, grad_up = hidden_units(inner_f, grad_low, w_units, w_d)

    def pieces(term):
        return term.astype(BF16).reshape(chips, width // chips, -1)

    spans = [slice(tree * chip_rows, (tree + 1) * chip_rows) for tree in range(trees)]
    down_ring = Reduce(ring, [pieces(unit_grads(grad_low, hidden))])
    down_hop = down_ring.hop()
    core_sums = []
    (grad_gate,) = after_all((grad_gate,), (down_ring.terms[0],))
    for tree in range(trees):
        part = back_units(tree, chip_rows, [grad_gate, grad_up], w_units, [0, 1])
        (part,) = after_all((part,), down_hop)
        down_hop = down_ring.hop(part)
        (grad_gate,) = after_all((grad_gate,), (part,))
        core_sums.append(core_sum(part))
    lows = [own.astype(BF16) for own in core_sums]
    arrived = [other_half(lows[0])]
    inner_f, hidden = after_all((inner_f, hidden), lows)
    units_terms = unit_grads(inner_f, grad_gate, grad_up)
    units_terms, arrived[0] = after_all((units_terms, arrived[0]), down_hop)
    arrived.append(other_half(after_all(lows[1:], arrived)[0]))
    units_ring = Reduce(ring, [pieces(units_terms)])
    units_hop = units_ring.hop() + down_ring.hop(units_terms)
    arrived[0] = after_all(arrived[:1], (units_terms,))[0]

    grads_middle, grads_low = [], []

    def backward_norm(tree):
        grad_inner = lows[tree].astype(F32) + arrived[tree].astype(F32)
        grad_middle = out_grad[tree].astype(F32) + norm_back(
            grad_inner * gain_f, normeds_f[tree], scales_f[tree]
        )
        low = grad_middle.astype(BF16)
        grads_middle.append(grad_middle)
        grads_low.append(low)
        return jnp.concatenate([low, other_core(low)], axis=0)

    mid_lows, out_lows, out_arrived = [backward_norm(0)], [], []
    grads_qkv, gain_a_terms = [], []

    def back_part(tree, kv_sums):
        rows_of = (cosine_rows[spans[tree]], -sine_rows[spans[tree]])
        parts = grad_queries[groups * tree : groups * (tree + 1)]
        for group in range(groups):
            kv_sum = kv_sums[:, 128 * group : 128 * (group + 1)]
            grad_k = kv_sum[:, None, :HEAD_SIZE]
            half = HEAD_SIZE // 2
            first, second = turn(grad_k[..., :half], grad_k[..., half:], *rows_of)
            kv_parts = [first[:, 0], second[:, 0], kv_sum[:, HEAD_SIZE:]]
            parts.append(jnp.concatenate(kv_parts, axis=1).astype(BF16))
        grad_qkv = jnp.concatenate(parts, axis=1)
        grads_qkv.append(grad_qkv)
        gain_a_terms.append(core_sum(dot(grad_qkv, w_qkv, 1, 1)))
        return gain_a_terms[-1].astype(BF16)

    grad_queries, grad_kvs = [], []
    for tree in range(trees):
        grad_mixed = dot(w_o, mid_lows[tree], 0, 1).astype(BF16)
        for group in range(groups):
            grad_query, grad_kv = attend_back(
                tree,
                group,
                seens[tree],
                tables[tree][3],
                query,
                masks[tree],
                mixes[tree],
                grad_mixed,
                lses[tree],
                kvs,
                cosine,
                sine,
                rep,
                block,
                grad_kvs[-1] if group else None,
            )
            grad_query, grad_kv = after_all((grad_query, grad_kv), units_hop)
            grad_queries.append(grad_query)
            grad_kvs.append(grad_kv)
            units_hop = ()
            if units_ring.left > 0 and group < groups - 1:
                units_hop = units_ring.hop(grad_query)
            (grad_mixed,) = after_all((grad_mixed,), (grad_query,))
            if tree == 0 and group == 0:
                (hidden,) = after_all((hidden,), (grad_query,))
                out_parts = [
                    back_units(tree, chip_rows, [hidden], w_d, [0]) for tree in range(trees)
                ]
                out_parts = after_all(out_parts, arrived[1:])
                out_lows = [core_sum(part).astype(BF16) for part in out_parts]
                (grad_mixed,) = after_all((grad_mixed,), out_lows)
                out_arrived.append(other_half(out_lows[0]))
                units_hop += tuple(out_arrived)
            elif tree and group < groups - 1:
                while kv_ring.left > 0:
                    units_hop += kv_ring.hop(grad_query)
        if tree == 0:
            kv_ring = Reduce(ring, grad_kvs[-1:])
            kv_ring.hop()
            arrived[-1] = after_all(arrived[-1:], (grad_query,))[0]
            mid_lows.append(backward_norm(1))
            kv_hop = kv_ring.hop()
            out_terms = pieces(
                dot(jnp.concatenate(mid_lows, axis=0), jnp.concatenate(mixes, axis=1), 0, 1)
            )
            mid_lows[1] = after_all(mid_lows[1:], (out_terms, *kv_hop))[0]
            out_arrived.append(other_half(after_all(out_lows[1:], (grad_query,))[0]))
            units_hop += units_ring.hop(*kv_hop) + kv_ring.hop(out_terms)
            units_hop += tuple(out_arrived[1:])
    out_arrived = after_all(out_arrived, (grad_queries[-1],))
    (down_sum,), (units_sum,) = down_ring.finish(), units_ring.finish()
    outputs = unwritten(out_terms, (trees, rows, width))
    out_arrived = after_all(out_arrived, (grad_queries[-1],))
    for tree in range(trees):
        summed = out_lows[tree].astype(F32) + out_arrived[tree].astype(F32)
        outputs = laid(outputs, (middles[tree] + summed).astype(BF16), tree)

    (layer_in,) = after_all((layer_in,), (grad_queries[-1],))
    normed_a = layer_in.astype(F32) * scale_a
    down_grad = row_grad(down_sum)
    lows = [back_part(0, kv_ring.finish()[0])]
    arrived = [other_half(lows[0])]
    (kv_terms,) = after_all(grad_kvs[-1:], lows)
    (kv_sums,) = after_all(ring_sum([kv_terms], 1), arrived)
    lows.append(back_part(1, kv_sums))
    (inner_a,) = after_all((inner_a,), (grads_qkv[-1],))
    gate_grad, up_grad = (
        column_grad(part) for part in jnp.split(units_sum, 2, axis=1)
    )
    core_sums = after_all(core_sums + gain_a_terms, lows)
    gain_terms = jnp.stack(
        [
            sum(jnp.sum(core_sums[trees + i] * normed_a[i], axis=0) for i in range(trees)),
            sum(jnp.sum(core_sums[i] * normeds_f[i], axis=0) for i in range(trees)),
        ],
        axis=1,
    )
    gain_terms = jnp.pad(gain_terms, ((0, 0), (0, 126))).astype(BF16)
    term_qkv = unit_grads(inner_a, jnp.concatenate(grads_qkv, axis=0))
    term_qkv = jnp.concatenate([term_qkv, gain_terms], axis=1)
    qkv_sum, out_sum, theirs = ring_sum([pieces(term_qkv), out_terms], 2, lows[1])
    arrived.append(theirs)
    out_proj_grad = row_grad(out_sum)
    qkv_sum, gain_sums = qkv_sum[:, : head_cols + 2 * kv_cols], qkv_sum[:, -128:]
    kv_parts = qkv_sum[:, head_cols:].reshape(-1, groups, 2, HEAD_SIZE)
    key_sum, value_sum = (kv_parts[:, :, i].reshape(-1, kv_cols) for i in range(2))

    keep, give = split_by_core(gain_sums, 0)
    gain_sums = (keep + other_core(give)).T[:8]
    gain_sums = gain_sums + other_half(gain_sums)
    gain_a_grad, gain_f_grad = gain_sums[0], gain_sums[1]
    input_grad = unwritten(scale_a, (trees, rows, width))
    for tree in range(trees):
        grad_inner = lows[tree].astype(F32) + arrived[tree].astype(F32)
        input_grad = laid(
            input_grad,
            grads_middle[tree] + norm_back(grad_inner * gain_a, normed_a[tree], scale_a[tree]),
            tree,
        )

    return (
        outputs,
        input_grad,
        gain_a_grad,
        column_grad(qkv_sum[:, :head_cols]),
        column_grad(key_sum),
        column_grad(value_sum),
        out_proj_grad,
        gain_f_grad,
        gate_grad,
        up_grad,
        down_grad,
    )


def solution(mesh):
    devices = mesh.devices
    mesh = Mesh(devices.reshape(-1, 2, devices.shape[1]), ("zy", "core", "tp"))
    fsdp = ("zy", "core")
    specs = (
        P(fsdp),
        P(fsdp, "tp"),
        P(fsdp, "tp"),
        P(fsdp, "tp"),
        P("tp", fsdp),
        P(fsdp),
        P(fsdp, "tp"),
        P(fsdp, "tp"),
        P("tp", fsdp),
    )
    tokens = P(None, fsdp, None)
    return jax.shard_map(
        shards,
        mesh=mesh,
        in_specs=(tokens, tokens, P(), P()) + specs,
        out_specs=(tokens, tokens) + specs,
        check_vma=False,
    )
```

```python
import functools
import math

import jax
import jax.numpy as jnp
from jax import lax
from jax.experimental import pallas as pl
from jax.experimental.pallas import tpu as pltpu
from jax.sharding import Mesh
from jax.sharding import PartitionSpec as P

QUERY_HEADS = 32
KEY_VALUE_HEADS = 8
HEAD_SIZE = 64
LEVELS = 3

EPS = 1e-05
THETA = 500000.0
NEG = -1e30
LN2 = math.log(2.0)
SWAP = [(0, 1), (1, 0)]
F32 = jnp.float32
BF16 = jnp.bfloat16
SMALL = pl.CostEstimate(flops=2**20, bytes_accessed=2**10, transcendentals=0)


def dot(left, right, left_dim=1, right_dim=0):
    return lax.dot_general(
        left, right, (((left_dim,), (right_dim,)), ((), ())), preferred_element_type=F32
    )


def row_scale_of(rows_in):
    return lax.rsqrt(jnp.mean(rows_in * rows_in, axis=-1, keepdims=True) + EPS)


def norm_back(grad_normed, normed, row_scale):
    return row_scale * (
        grad_normed - normed * jnp.mean(grad_normed * normed, axis=-1, keepdims=True)
    )


def rope_angles(position, head_dim):
    half_dim = head_dim // 2
    index_row = jnp.arange(half_dim, dtype=F32)
    inverse = THETA ** (-2.0 * index_row / head_dim)
    wavelen = 2.0 * math.pi / inverse
    smooth = jnp.clip((8192.0 / wavelen - 1.0) / 3.0, 0.0, 1.0)
    inverse = (1.0 - smooth) * inverse / 32.0 + smooth * inverse
    return inverse[:, None] * position.astype(F32)[None, :]


def turn(first_half, second_half, cosine, sine):
    return first_half * cosine - second_half * sine, second_half * cosine + first_half * sine


def tree_tables(parents_row, lengths):
    seg_count = parents_row.shape[0]
    labels = jnp.arange(seg_count, dtype=jnp.int32)
    ends_at = jnp.cumsum(lengths)
    starts_at = ends_at - lengths
    reaches = labels[:, None] == labels[None, :]
    climber = labels
    for _ in range(LEVELS - 1):
        climber = jnp.sum(
            jnp.where(climber[:, None] == labels[None, :], parents_row[None, :], 0), axis=1
        )
        reaches = reaches | (climber[:, None] == labels[None, :])
    before = jnp.sum(
        jnp.where(reaches & (labels[:, None] != labels[None, :]), lengths[None, :], 0), axis=1
    )
    return reaches, starts_at, ends_at, before


def after_all(values, others):
    if not others:
        return list(values)
    return list(lax.optimization_barrier(tuple(values) + tuple(others))[: len(values)])


def unwritten(like, shape):
    return pl.pallas_call(
        lambda like_ref, out_ref: None,
        in_specs=[pl.BlockSpec(memory_space=pl.ANY)],
        out_specs=pl.BlockSpec(memory_space=pl.ANY),
        out_shape=jax.ShapeDtypeStruct(shape, like.dtype),
        name="buffer",
    )(like)


class Ring:
    def __init__(self):
        self.count = lax.axis_size("zy")
        count = self.count
        place = [2 * i if i < count // 2 else 2 * (count - 1 - i) + 1 for i in range(count)]
        self.right = [(place[i], place[(i + 1) % count]) for i in range(count)]
        self.left = [(b, a) for a, b in self.right]
        me = lax.axis_index("zy")
        self.spot = jnp.where(me % 2 == 0, me // 2, count - 1 - me // 2)

    def chip(self, offset):
        spot = lax.rem(self.spot + offset + self.count, self.count)
        return jnp.where(spot < self.count // 2, 2 * spot, 2 * (self.count - 1 - spot) + 1)

    def go_right(self, value):
        return lax.ppermute(value, "zy", self.right)

    def go_left(self, value):
        return lax.ppermute(value, "zy", self.left)

    def put(self, whole, part, offset, row=0):
        at = (self.chip(offset), row) + (0,) * (part.ndim - 1)
        return lax.dynamic_update_slice(whole, part[None], at)


class Gather:
    def __init__(self, ring, pieces, tidy=False):
        self.ring, self.step, self.tidy, self.laid = ring, 0, tidy, ()
        self.cuts = [piece.shape[0] // 2 for piece in pieces]
        wholes = [unwritten(piece, (ring.count,) + piece.shape) for piece in pieces]
        self.wholes = [ring.put(whole, piece, 0) for whole, piece in zip(wholes, pieces)]
        self.rightward = self.leftward = list(pieces)

    def hop(self, *others):
        ring, count = self.ring, len(self.cuts)
        both = after_all(self.rightward + self.leftward, others + self.laid)
        rightward, leftward = both[:count], both[count:]
        self.step += 1
        self.laid = tuple(self.wholes) if self.tidy else ()
        far = self.step == ring.count // 2
        if far:
            rightward = [part[:cut] for part, cut in zip(rightward, self.cuts)]
            leftward = [part[cut:] for part, cut in zip(leftward, self.cuts)]
        rightward = [ring.go_right(part) for part in rightward]
        leftward = [ring.go_left(part) for part in leftward]
        for i, cut in enumerate(self.cuts):
            whole = ring.put(self.wholes[i], rightward[i], -self.step)
            self.wholes[i] = ring.put(whole, leftward[i], self.step, cut if far else 0)
        self.rightward, self.leftward = rightward, leftward
        return tuple(rightward) + tuple(leftward)

    def finish(self, *others):
        while self.step < self.ring.count // 2:
            self.hop(*others)
        return self.wholes


class Reduce:
    def __init__(self, ring, terms):
        self.ring, self.terms, self.left = ring, list(terms), ring.count // 2
        self.cuts = [term.shape[1] // 2 for term in terms]
        self.rightward = self.leftward = None

    def each(self, offset):
        chip = self.ring.chip(offset)
        return [lax.dynamic_index_in_dim(term, chip, 0, keepdims=False) for term in self.terms]

    def hop(self, *others):
        ring, step, count = self.ring, self.left, len(self.cuts)
        if self.rightward is None:
            far = after_all(self.each(step), others)
            rightward = [part[:cut] for part, cut in zip(far, self.cuts)]
            leftward = [part[cut:] for part, cut in zip(far, self.cuts)]
        else:
            both = after_all(self.rightward + self.leftward, others)
            rightward, leftward = both[:count], both[count:]
            mine, other = self.each(step), self.each(-step)
            if step == ring.count // 2 - 1:
                for i, cut in enumerate(self.cuts):
                    parts = [add_low(mine[i][:cut], rightward[i]), mine[i][cut:]]
                    rightward[i] = jnp.concatenate(parts, axis=0)
                    parts = [other[i][:cut], add_low(other[i][cut:], leftward[i])]
                    leftward[i] = jnp.concatenate(parts, axis=0)
            else:
                rightward = [add_low(one, part) for one, part in zip(mine, rightward)]
                leftward = [add_low(one, part) for one, part in zip(other, leftward)]
        self.rightward = [ring.go_right(part) for part in rightward]
        self.leftward = [ring.go_left(part) for part in leftward]
        self.left -= 1
        return tuple(self.rightward) + tuple(self.leftward)

    def finish(self, *others):
        while self.left > 0:
            self.hop(*others)
        return [
            mine.astype(F32) + one.astype(F32) + two.astype(F32)
            for mine, one, two in zip(self.each(0), self.rightward, self.leftward)
        ]


def add_low(left, right):
    return (left.astype(F32) + right.astype(F32)).astype(BF16)


def other_core(value):
    return lax.ppermute(value, "core", SWAP)


def other_half(value):
    return lax.ppermute(value, "tp", SWAP)


def by_core(own, other, axis):
    first = lax.axis_index("core") == 0
    return jnp.concatenate(
        [jnp.where(first, own, other), jnp.where(first, other, own)], axis=axis
    )


def split_by_core(value, axis):
    core = lax.axis_index("core")
    size = value.shape[axis] // 2
    return (
        lax.dynamic_slice_in_dim(value, core * size, size, axis),
        lax.dynamic_slice_in_dim(value, (1 - core) * size, size, axis),
    )


def split3(value):
    high = value.astype(BF16)
    rest = value - high.astype(F32)
    middle = rest.astype(BF16)
    low = (rest - middle.astype(F32)).astype(BF16)
    return high, middle, low


def causal(scores, block):
    key_at = lax.broadcasted_iota(jnp.int32, scores.shape, 0)
    query_at = lax.rem(lax.broadcasted_iota(jnp.int32, scores.shape, 1), block)
    return jnp.where(key_at <= query_at, scores, NEG)


def block_of(ref, index, block, per_piece):
    piece = lax.div(index, per_piece)
    start = pl.multiple_of(lax.rem(index, per_piece) * block, block)
    return ref[piece, 0, pl.ds(start, block), :]


def attend_kernel(
    block, rep, per_piece, count_ref, list_ref, diag_ref, query_ref, mask_ref, kv_ref, hot_ref,
    out_ref, lse_ref, query_aug, turned,
):
    at = pl.program_id(1)
    key_blocks = hot_ref.shape[0] // block - 1

    @pl.when(at == 0)
    def _():
        rows = per_piece * block
        for piece in range(kv_ref.shape[0]):
            turned[:, piece * rows : (piece + 1) * rows] = kv_ref[piece, 0].T

    query_aug[HEAD_SIZE:, :] = jnp.zeros_like(query_aug[HEAD_SIZE:, :])
    for r in range(rep):
        columns = slice(r * block, (r + 1) * block)
        query_aug[:HEAD_SIZE, columns] = query_ref[r * HEAD_SIZE : (r + 1) * HEAD_SIZE, :]
        query_aug[128:144, columns] = mask_ref[...]

    def scores_of(index):
        keys = block_of(kv_ref, jnp.minimum(index, key_blocks - 1), block, per_piece)
        hot = hot_ref[pl.ds(pl.multiple_of(index * block, block), block), :]
        return jnp.dot(
            jnp.concatenate([keys, hot], axis=1), query_aug[...], preferred_element_type=F32
        )

    def values_of(index):
        index = jnp.minimum(index, key_blocks - 1)
        return turned[HEAD_SIZE:, pl.ds(pl.multiple_of(index * block, block), block)]

    diagonal = diag_ref[at]
    scores = causal(scores_of(diagonal), block)
    top = jnp.max(scores, axis=0, keepdims=True)
    probs = jnp.exp2(scores - top)
    total = jnp.sum(probs, axis=0, keepdims=True)
    mixed = jnp.dot(values_of(diagonal), probs.astype(BF16), preferred_element_type=F32)

    def step(j, carry):
        top, total, mixed = carry
        one, two = list_ref[at, 2 * j], list_ref[at, 2 * j + 1]
        first, second = scores_of(one), scores_of(two)
        new = jnp.maximum(top, jnp.max(first, axis=0, keepdims=True))
        new = jnp.maximum(new, jnp.max(second, axis=0, keepdims=True))
        factor = jnp.exp2(top - new)
        first, second = jnp.exp2(first - new), jnp.exp2(second - new)
        total = (
            total * factor
            + jnp.sum(first, axis=0, keepdims=True)
            + jnp.sum(second, axis=0, keepdims=True)
        )
        values = jnp.concatenate([values_of(one), values_of(two)], axis=1)
        probs = jnp.concatenate([first.astype(BF16), second.astype(BF16)], axis=0)
        mixed = mixed * factor + jnp.dot(values, probs, preferred_element_type=F32)
        return new, total, mixed

    pairs = lax.div(count_ref[at] + 1, 2)
    top, total, mixed = lax.fori_loop(0, pairs, step, (top, total, mixed))
    mixed = mixed * (1.0 / total)
    lse = top + jnp.log2(total)
    for r in range(rep):
        columns = slice(r * block, (r + 1) * block)
        out_ref[r * HEAD_SIZE : (r + 1) * HEAD_SIZE, :] = mixed[:, columns].astype(BF16)
        lse_ref[0, r : r + 1, :] = lse[:, columns]


def attend(tree, tables, query, mask, kv, rep, block):
    counts, lists, diagonals, hot = tables
    heads = query.shape[0]
    pieces, _, rows, _ = kv.shape
    groups, query_blocks = heads // (rep * HEAD_SIZE), rows // block
    keys = pieces * rows
    grid_spec = pltpu.PrefetchScalarGridSpec(
        num_scalar_prefetch=3,
        grid=(groups, query_blocks),
        in_specs=[
            pl.BlockSpec(
                (rep * HEAD_SIZE, block), lambda g, q, *_: (g, tree * query_blocks + q)
            ),
            pl.BlockSpec((16, block), lambda g, q, *_: (0, q)),
            pl.BlockSpec((pieces, 1, rows, 128), lambda g, q, *_: (0, 0, 0, g)),
            pl.BlockSpec((keys + block, 128), lambda g, q, *_: (0, 0)),
        ],
        out_specs=[
            pl.BlockSpec((rep * HEAD_SIZE, block), lambda g, q, *_: (g, q)),
            pl.BlockSpec((1, rep, block), lambda g, q, *_: (g, 0, q)),
        ],
        scratch_shapes=[
            pltpu.VMEM((256, rep * block), BF16),
            pltpu.VMEM((128, keys), BF16),
        ],
    )
    return pl.pallas_call(
        functools.partial(attend_kernel, block, rep, rows // block),
        grid_spec=grid_spec,
        out_shape=[
            jax.ShapeDtypeStruct((heads, rows), BF16),
            jax.ShapeDtypeStruct((groups, rep, rows), F32),
        ],
        compiler_params=pltpu.CompilerParams(vmem_limit_bytes=48 * 2**20),
        cost_estimate=SMALL,
        name="tree_attention",
    )(counts, lists, diagonals, query, mask, kv, hot)


def attend_back_kernel(
    block, rep, per_piece, seen_ref, query_ref, mask_ref, mixed_ref, grad_ref, lse_ref, kv_ref,
    hot_ref, cosine_ref, sine_ref, before_ref, grad_query_ref, grad_kv_ref, augs, turned_rows,
    key_turned, grad_query, grad_kv,
):
    rows = per_piece * block
    query_blocks = rows // block
    key_blocks = kv_ref.shape[0] * per_piece
    width = rep * block

    for piece in range(kv_ref.shape[0]):
        key_turned[:, piece * rows : (piece + 1) * rows] = kv_ref[piece, 0].T
    grad_kv[...] = jnp.zeros_like(grad_kv)
    grad_query[...] = jnp.zeros_like(grad_query)
    augs[...] = jnp.zeros_like(augs)
    none = jnp.zeros((HEAD_SIZE, block), BF16)
    for at in range(query_blocks):
        columns = slice(at * block, (at + 1) * block)
        for r in range(rep):
            here = slice(2 * at * width + r * block, 2 * at * width + (r + 1) * block)
            there = slice((2 * at + 1) * width + r * block, (2 * at + 1) * width + (r + 1) * block)
            head = slice(r * HEAD_SIZE, (r + 1) * HEAD_SIZE)
            query, grad = query_ref[head, columns], grad_ref[head, columns]
            augs[:HEAD_SIZE, here] = query
            augs[HEAD_SIZE : 2 * HEAD_SIZE, there] = grad
            delta = jnp.sum(
                grad.astype(F32) * mixed_ref[head, columns].astype(F32), axis=0, keepdims=True
            )
            empty = jnp.zeros((13, block), BF16)
            augs[128:160, here] = jnp.concatenate(
                [mask_ref[:, columns], *split3(-lse_ref[0, r : r + 1, columns]), empty], axis=0
            )
            augs[128:160, there] = jnp.concatenate(
                [jnp.zeros((16, block), BF16), *split3(-delta), empty], axis=0
            )
            turned_rows[here, :] = jnp.concatenate([none, grad], axis=0).T
            turned_rows[there, :] = jnp.concatenate([query, none], axis=0).T

    def over_keys(index, _):
        rows_at = pl.ds(pl.multiple_of(index * block, block), block)
        for at in range(query_blocks):
            columns = slice(2 * at * width, (2 * at + 2) * width)

            def work(on_diagonal):
                both = jnp.dot(
                    jnp.concatenate(
                        [block_of(kv_ref, index, block, per_piece), hot_ref[rows_at, :]], axis=1
                    ),
                    augs[:, columns],
                    preferred_element_type=F32,
                )
                scores, grad_probs = both[:, :width], both[:, width:]
                if on_diagonal:
                    scores = causal(scores, block)
                probs = jnp.exp2(scores)
                grad_scores = (probs * grad_probs).astype(BF16)
                grad_kv[rows_at, :] += jnp.dot(
                    jnp.concatenate([probs.astype(BF16), grad_scores], axis=1),
                    turned_rows[columns, :],
                    preferred_element_type=F32,
                )
                grad_query[:, at * width : (at + 1) * width] += jnp.dot(
                    key_turned[:HEAD_SIZE, rows_at], grad_scores, preferred_element_type=F32
                )

            seen = seen_ref[at, index]
            pl.when(seen == 1)(functools.partial(work, False))
            pl.when(seen == 2)(functools.partial(work, True))
        return 0

    lax.fori_loop(0, key_blocks, over_keys, 0)
    for at in range(query_blocks):
        columns = slice(at * block, (at + 1) * block)
        cosine = cosine_ref[:, columns] * HEAD_SIZE**-0.5
        sine = -sine_ref[:, columns] * HEAD_SIZE**-0.5
        for r in range(0, rep, 2):
            parts = []
            for head in (r, r + 1):
                here = slice(at * width + head * block, at * width + (head + 1) * block)
                grad = grad_query[:, here]
                half = HEAD_SIZE // 2
                parts += turn(grad[:half], grad[half:], cosine, sine)
            grad_query_ref[columns, r * HEAD_SIZE : (r + 2) * HEAD_SIZE] = (
                jnp.concatenate(parts, axis=0).T.astype(BF16)
            )
    for piece in range(kv_ref.shape[0]):
        grads = grad_kv[piece * rows : (piece + 1) * rows, :]
        lanes = lax.broadcasted_iota(jnp.int32, grads.shape, 1)
        grad_kv_ref[piece] = jnp.where(lanes < HEAD_SIZE, grads * LN2, grads).astype(BF16)


def attend_back(
    tree, group, seen, hot, query, mask, mixed, grad, lse, kv, cosine, sine, rep, block, before
):
    pieces, _, rows, _ = kv.shape
    keys = pieces * rows
    heads = rep * HEAD_SIZE
    head = pl.BlockSpec((heads, rows), lambda i, *_: (group, 0))
    table = pl.BlockSpec((HEAD_SIZE // 2, rows), lambda i, *_: (0, tree))
    grid_spec = pltpu.PrefetchScalarGridSpec(
        num_scalar_prefetch=1,
        grid=(1,),
        in_specs=[
            pl.BlockSpec((heads, rows), lambda i, *_: (group, tree)),
            pl.BlockSpec((16, rows), lambda i, *_: (0, 0)),
            head,
            head,
            pl.BlockSpec((1, rep, rows), lambda i, *_: (group, 0, 0)),
            pl.BlockSpec((pieces, 1, rows, 128), lambda i, *_: (0, 0, 0, group)),
            pl.BlockSpec((keys + block, 128), lambda i, *_: (0, 0)),
            table,
            table,
            pl.BlockSpec(memory_space=pl.ANY),
        ],
        out_specs=[
            pl.BlockSpec((rows, heads), lambda i, *_: (0, 0)),
            pl.BlockSpec((pieces, rows, 128), lambda i, *_: (0, 0, group)),
        ],
        scratch_shapes=[
            pltpu.VMEM((256, 2 * rep * rows), BF16),
            pltpu.VMEM((2 * rep * rows, 128), BF16),
            pltpu.VMEM((128, keys), BF16),
            pltpu.VMEM((HEAD_SIZE, rep * rows), F32),
            pltpu.VMEM((keys, 128), F32),
        ],
    )
    return pl.pallas_call(
        functools.partial(attend_back_kernel, block, rep, rows // block),
        grid_spec=grid_spec,
        out_shape=[
            jax.ShapeDtypeStruct((rows, heads), BF16),
            jax.ShapeDtypeStruct((pieces, rows, kv.shape[3]), BF16),
        ],
        input_output_aliases={10: 1} if group else {},
        compiler_params=pltpu.CompilerParams(vmem_limit_bytes=56 * 2**20),
        cost_estimate=SMALL,
        name="tree_attention_back",
    )(seen, query, mask, mixed, grad, lse, kv, hot, cosine, sine, cosine if before is None else before)


def project_kernel(
    heads, columns, own_ref, other_ref, gain_ref, weight_ref, cosine_ref, sine_ref, inner_ref, query_ref,
    kv_ref, rows,
):
    mine = lax.rem(pl.program_id(0), 2) == 0

    @pl.when(mine)
    def _():
        rows[...] = own_ref[0].astype(F32)

    @pl.when(jnp.logical_not(mine))
    def _():
        rows[...] = other_ref[0].astype(F32)

    x = rows[...]
    inner = (x * row_scale_of(x) * gain_ref[...]).astype(BF16)
    inner_ref[...] = inner
    made = jnp.dot(inner, weight_ref[:, :columns], preferred_element_type=F32)
    cosine, sine = cosine_ref[...], sine_ref[...]
    half = HEAD_SIZE // 2

    def turned(values):
        parts = []
        for start in range(0, values.shape[0], HEAD_SIZE):
            parts += turn(
                values[start : start + half], values[start + half : start + HEAD_SIZE], cosine, sine
            )
        return jnp.concatenate(parts, axis=0)

    query_ref[...] = (turned(made[:, :heads].T) * (HEAD_SIZE**-0.5 / LN2)).astype(BF16)
    kv = made[:, heads:].T
    parts = []
    for start in range(0, kv.shape[0], 128):
        parts += [turned(kv[start : start + HEAD_SIZE]), kv[start + HEAD_SIZE : start + 128]]
    kv_ref[...] = jnp.concatenate(parts, axis=0).T.astype(BF16)


def project(own, other, gain, weight, cosine, sine, heads, kv_columns, tile):
    trees, rows, width = own.shape
    tiles = rows // tile
    last = trees * tiles - 1

    def place(half):
        def index(t, j):
            tree, at = t // 2, t % 2
            same = at == half
            if half == 0:
                return (jnp.where(same, tree, tree), jnp.where(same, j, tiles - 1), 0)
            return (tree, jnp.where(same, j, 0), 0)

        return index

    flat = lambda t, j: (t * tiles + j, 0)
    lanes = lambda t, j: (0, t * tiles + j)
    tokens = 2 * trees * rows
    columns = heads + kv_columns
    return pl.pallas_call(
        functools.partial(project_kernel, heads, columns),
        grid=(2 * trees, tiles),
        in_specs=[
            pl.BlockSpec((1, tile, width), place(0)),
            pl.BlockSpec((1, tile, width), place(1)),
            pl.BlockSpec((1, width), lambda t, j: (0, 0)),
            pl.BlockSpec((width, columns), lambda t, j: (0, 0)),
            pl.BlockSpec((HEAD_SIZE // 2, tile), lanes),
            pl.BlockSpec((HEAD_SIZE // 2, tile), lanes),
        ],
        out_specs=[
            pl.BlockSpec((tile, width), flat),
            pl.BlockSpec((heads, tile), lanes),
            pl.BlockSpec((tile, columns - heads), flat),
        ],
        out_shape=[
            jax.ShapeDtypeStruct((tokens, width), BF16),
            jax.ShapeDtypeStruct((heads, tokens), BF16),
            jax.ShapeDtypeStruct((tokens, columns - heads), BF16),
        ],
        scratch_shapes=[pltpu.VMEM((tile, width), F32)],
        compiler_params=pltpu.CompilerParams(vmem_limit_bytes=48 * 2**20),
        cost_estimate=SMALL,
        name="project",
    )(own, other, gain, weight, cosine, sine)


def units_kernel(inner_ref, gate_ref, up_ref, hidden_ref, slope_ref, activated_ref):
    inner = inner_ref[...]
    gate = jnp.dot(inner, gate_ref[...], preferred_element_type=F32)
    up = jnp.dot(inner, up_ref[...], preferred_element_type=F32)
    sigmoid = jax.nn.sigmoid(gate)
    activated = gate * sigmoid
    hidden_ref[...] = (activated * up).astype(BF16)
    slope_ref[...] = (up * sigmoid * (1.0 + gate * (1.0 - sigmoid))).astype(BF16)
    activated_ref[...] = activated.astype(BF16)


def back_hidden_kernel(grad_ref, down_ref, slope_ref, activated_ref, grad_gate_ref, grad_up_ref):
    grad_hidden = jnp.dot(grad_ref[...], down_ref[...], preferred_element_type=F32)
    grad_gate_ref[...] = (grad_hidden * slope_ref[...].astype(F32)).astype(BF16)
    grad_up_ref[...] = (grad_hidden * activated_ref[...].astype(F32)).astype(BF16)


def over_units(kernel, rows_in, weights, firsts, units, tiles_in, made, name):
    tokens, width = rows_in.shape
    rows, columns = math.gcd(tokens, 2048 // len(firsts)), math.gcd(units, 512)
    tiles = units // columns
    tile = pl.BlockSpec((rows, columns), lambda j, i: (i, j))
    wide = [
        pl.BlockSpec((width, columns), lambda j, i, first=first: (0, first * tiles + j))
        for first in firsts
    ]
    return pl.pallas_call(
        kernel,
        grid=(tiles, tokens // rows),
        in_specs=[pl.BlockSpec((rows, width), lambda j, i: (i, 0)), *wide]
        + [tile] * len(tiles_in),
        out_specs=[tile] * made,
        out_shape=[jax.ShapeDtypeStruct((tokens, units), BF16)] * made,
        compiler_params=pltpu.CompilerParams(vmem_limit_bytes=56 * 2**20),
        cost_estimate=SMALL,
        name=name,
    )(rows_in, *([weights] * len(firsts)), *tiles_in)


def hidden_units(inner, weights):
    units = weights.shape[1] // 2
    return over_units(units_kernel, inner, weights, (0, 1), units, (), 3, "hidden_units")


def back_hidden(grad, down, slope, activated):
    units = down.shape[1]
    return over_units(
        back_hidden_kernel, grad, down, (0,), units, (slope, activated), 2, "back_hidden"
    )


def back_units_kernel(count, *refs):
    *refs, own_ref, other_ref = refs
    contract = (((1,), (1,)), ((), ()))
    total = None
    for units_ref, weight_ref in zip(refs[:count], refs[count:]):
        term = lax.dot_general(
            units_ref[...], weight_ref[...], contract, preferred_element_type=F32
        )
        total = term if total is None else total + term
    half = own_ref.shape[0]
    own_ref[...] = total[:half].astype(BF16)
    other_ref[...] = total[half:].astype(BF16)


def back_units(tree, tokens, units, weights, places):
    width, size = weights.shape[0], units[0].shape[1]
    columns = math.gcd(width, 512)
    tall = pl.BlockSpec((tokens, size), lambda j: (tree, 0))
    made = jax.ShapeDtypeStruct((tokens // 2, width), BF16)
    return pl.pallas_call(
        functools.partial(back_units_kernel, len(units)),
        grid=(width // columns,),
        in_specs=[tall] * len(units)
        + [pl.BlockSpec((columns, size), lambda j, at=at: (j, at)) for at in places],
        out_specs=[pl.BlockSpec((tokens // 2, columns), lambda j: (0, j))] * 2,
        out_shape=[made, made],
        compiler_params=pltpu.CompilerParams(vmem_limit_bytes=56 * 2**20),
        cost_estimate=SMALL,
        name="back_units",
    )(*units, *([weights] * len(units)))


def unit_grads_kernel(tiles, rows_ref, *refs):
    *grad_refs, out_ref, turned = refs
    at = pl.program_id(1)

    @pl.when(at == 0)
    def _():
        turned[...] = rows_ref[...].T

    for i, grad_ref in enumerate(grad_refs):

        @pl.when((at >= i * tiles) & (at < (i + 1) * tiles))
        def _():
            out_ref[...] = jnp.dot(
                turned[...], grad_ref[...], preferred_element_type=F32
            ).astype(BF16)


def unit_grads(rows_in, *grads):
    tokens, width = rows_in.shape
    units = grads[0].shape[1]
    rows, columns = math.gcd(width, 1024), math.gcd(units, 1024 // len(grads))
    tiles = units // columns

    def place(i):
        return lambda at, j: (0, jnp.clip(j - i * tiles, 0, tiles - 1))

    return pl.pallas_call(
        functools.partial(unit_grads_kernel, tiles),
        grid=(width // rows, tiles * len(grads)),
        in_specs=[pl.BlockSpec((tokens, rows), lambda i, j: (0, i))]
        + [pl.BlockSpec((tokens, columns), place(i)) for i in range(len(grads))],
        out_specs=pl.BlockSpec((rows, columns), lambda i, j: (i, j)),
        out_shape=jax.ShapeDtypeStruct((width, units * len(grads)), BF16),
        scratch_shapes=[pltpu.VMEM((rows, tokens), BF16)],
        compiler_params=pltpu.CompilerParams(vmem_limit_bytes=56 * 2**20),
        cost_estimate=SMALL,
        name="unit_grads",
    )(rows_in, *grads)


def ring_place(spot, count):
    spot = lax.rem(spot + count, count)
    return jnp.where(spot < count // 2, 2 * spot, 2 * (count - 1 - spot) + 1)


def ring_sum_kernel(count, arrays, swaps, *refs):
    terms_refs, refs = refs[:arrays], refs[arrays:]
    if swaps:
        swap_ref, *refs, swap_send, swap_receive = refs
    out_refs, refs = refs[:arrays], refs[arrays:]
    if swaps:
        theirs_ref, *refs = refs
    helds, from_lefts, from_rights = (refs[i * arrays : (i + 1) * arrays] for i in range(3))
    load_sems, send_sems, receive_sems = refs[3 * arrays :]
    half = count // 2
    me = lax.axis_index("zy")
    spot = jnp.where(lax.rem(me, 2) == 0, lax.div(me, 2), count - 1 - lax.div(me, 2))
    right, left = ring_place(spot + 1, count), ring_place(spot - 1, count)

    barrier = pltpu.get_barrier_semaphore()
    for neighbour in (right, left):
        pl.semaphore_signal(
            barrier, inc=1, device_id={"zy": neighbour}, device_id_type=pl.DeviceIdType.MESH
        )
    other = {"tp": 1 - lax.axis_index("tp")}
    if swaps:
        pl.semaphore_signal(
            barrier, inc=1, device_id=other, device_id_type=pl.DeviceIdType.MESH
        )
    order = [half]
    for step in range(half - 1, 0, -1):
        order += [step, count - step]
    order.append(0)
    loads = {}
    for k in order:
        for i in range(arrays):
            loads[i, k] = pltpu.make_async_copy(
                terms_refs[i].at[ring_place(spot + k, count)], helds[i].at[k], load_sems.at[i, k]
            )
            loads[i, k].start()
    pl.semaphore_wait(barrier, 3 if swaps else 2)
    if swaps:
        swap = pltpu.make_async_remote_copy(
            src_ref=swap_ref,
            dst_ref=theirs_ref,
            send_sem=swap_send,
            recv_sem=swap_receive,
            device_id=other,
            device_id_type=pl.DeviceIdType.MESH,
        )
        swap.start()

    copies = {}

    def send(i, hop, way, source, target):
        copies[i, hop, way] = pltpu.make_async_remote_copy(
            src_ref=source,
            dst_ref=target,
            send_sem=send_sems.at[i, way, hop],
            recv_sem=receive_sems.at[i, way, hop],
            device_id={"zy": (right, left)[way]},
            device_id_type=pl.DeviceIdType.MESH,
        )
        copies[i, hop, way].start()

    def halves(i):
        cut = helds[i].shape[1] // 2
        return pl.ds(0, cut), pl.ds(cut, cut)

    for i in range(arrays):
        loads[i, half].wait()
        for way, arrived in enumerate((from_lefts[i], from_rights[i])):
            at = halves(i)[way]
            send(i, 0, way, helds[i].at[half, at], arrived.at[0, at])
    for hop in range(1, half):
        step = half - hop
        for i in range(arrays):
            for way, k in enumerate((step, count - step)):
                held, arrived = helds[i], (from_lefts[i], from_rights[i])[way]
                loads[i, k].wait()
                copies[i, hop - 1, way].wait_recv()
                at = halves(i)[way] if hop == 1 else slice(None)
                held[k, at, :] = (
                    held[k, at, :].astype(F32) + arrived[hop - 1, at, :].astype(F32)
                ).astype(BF16)
                send(i, hop, way, held.at[k], arrived.at[hop])
    for i in range(arrays):
        loads[i, 0].wait()
        for way in range(2):
            copies[i, half - 1, way].wait_recv()
        out_refs[i][...] = (
            helds[i][0].astype(F32)
            + from_lefts[i][half - 1].astype(F32)
            + from_rights[i][half - 1].astype(F32)
        )
    for copy in copies.values():
        copy.wait_send()
    if swaps:
        swap.wait()


def ring_sum(terms, collective_id, swap=None):
    arrays, count = len(terms), terms[0].shape[0]
    half = count // 2
    swaps = swap is not None
    anywhere = pl.BlockSpec(memory_space=pl.ANY)
    shapes = [term.shape[1:] for term in terms]
    return pl.pallas_call(
        functools.partial(ring_sum_kernel, count, arrays, swaps),
        in_specs=[anywhere] * (arrays + swaps),
        out_specs=[pl.BlockSpec(memory_space=pltpu.VMEM)] * arrays + [anywhere] * swaps,
        out_shape=[jax.ShapeDtypeStruct(shape, F32) for shape in shapes]
        + ([jax.ShapeDtypeStruct(swap.shape, swap.dtype)] if swaps else []),
        scratch_shapes=[pltpu.VMEM((count, *shape), BF16) for shape in shapes]
        + [pltpu.VMEM((half, *shape), BF16) for shape in shapes + shapes]
        + [
            pltpu.SemaphoreType.DMA((arrays, count)),
            pltpu.SemaphoreType.DMA((arrays, 2, half)),
            pltpu.SemaphoreType.DMA((arrays, 2, half)),
        ]
        + [pltpu.SemaphoreType.DMA] * (2 * swaps),
        compiler_params=pltpu.CompilerParams(
            collective_id=collective_id, has_side_effects=True, vmem_limit_bytes=48 * 2**20
        ),
        cost_estimate=SMALL,
        name="ring_sum",
    )(*terms, *([swap] if swaps else []))


def shards(
    layer_in,
    out_grad,
    parents,
    seg_len,
    attn_gain,
    w_query,
    key_weight,
    value_weight,
    w_out,
    ffn_gain,
    w_gate,
    w_up,
    w_down,
):
    trees, rows, width = layer_in.shape
    ring = Ring()
    chips = ring.count
    here, core = lax.axis_index("zy"), lax.axis_index("core")
    chip_rows = 2 * rows
    keys = chips * chip_rows
    groups = KEY_VALUE_HEADS // (2 * lax.axis_size("tp"))
    rep = QUERY_HEADS // KEY_VALUE_HEADS
    heads = groups * rep
    head_cols, kv_cols = heads * HEAD_SIZE, groups * HEAD_SIZE
    block = math.gcd(rows, 256)
    per_half = rows // block
    query_blocks, key_blocks = chip_rows // block, keys // block

    def column_piece(weight):
        keep, give = split_by_core(weight, 1)
        return by_core(keep, other_core(give), 0)

    def row_piece(weight):
        keep, give = split_by_core(weight, 0)
        return by_core(keep.T, other_core(give).T, 0)

    def column_grad(total):
        keep, give = split_by_core(total, 0)
        return by_core(keep, other_core(give), 1)

    def row_grad(total):
        keep, give = split_by_core(total, 0)
        return by_core(keep, other_core(give), 1).T

    def interleave(keys, values):
        parts = []
        for group in range(groups):
            at = slice(group * HEAD_SIZE, (group + 1) * HEAD_SIZE)
            parts += [keys[:, at], values[:, at]]
        return parts

    kv_pieces = interleave(column_piece(key_weight), column_piece(value_weight))
    gains = jnp.pad(jnp.stack([attn_gain, ffn_gain], axis=1), ((0, 0), (0, 126)))
    gain_piece = by_core(gains, other_core(gains), 0)
    qkv_piece = jnp.concatenate(
        [column_piece(w_query)] + kv_pieces + [gain_piece, row_piece(w_out)], axis=1
    )
    qkv_ring = Gather(ring, [qkv_piece], True)
    (first_in,) = after_all((layer_in,), (qkv_piece,))
    other_in = other_core(first_in)
    hops = [qkv_ring.hop()]
    w_gate, w_up, w_down = after_all((w_gate, w_up, w_down), hops[0])
    down_piece = row_piece(w_down)
    units_piece = unwritten(w_gate, (width // chips, w_gate.shape[1]))
    for at, piece in enumerate((column_piece(w_gate), column_piece(w_up))):
        units_piece = lax.dynamic_update_slice(units_piece, piece, (0, at * piece.shape[1]))
    while qkv_ring.step < chips // 2 - 1:
        hops.append(qkv_ring.hop())
    down_ring = Gather(ring, [down_piece])
    hops.append(qkv_ring.hop(down_piece))
    down_hop = down_ring.hop(*hops[-1])
    (w_attn,) = qkv_ring.finish()
    w_attn = w_attn.reshape(width, -1)
    w_qkv, gain_all, w_o = jnp.split(
        w_attn, [head_cols + 2 * kv_cols, head_cols + 2 * kv_cols + 128], axis=1
    )
    gain_all = gain_all.T[:2].astype(F32)
    gain_a, gain_f = gain_all[0], gain_all[1]

    def token_order(chip):
        first = (chip * 2 + core) * rows
        second = (chip * 2 + 1 - core) * rows
        steps = jnp.arange(rows, dtype=jnp.int32)
        return jnp.concatenate(
            [first[..., None] + steps, second[..., None] + steps], axis=-1
        ).reshape(-1)

    own_tokens = token_order(here)
    key_tokens = token_order(jnp.arange(chips, dtype=jnp.int32))
    own_block = own_tokens[::block] // block
    key_block = key_tokens[::block] // block
    diagonals = here * query_blocks + jnp.arange(query_blocks, dtype=jnp.int32)
    labels = jnp.arange(16, dtype=jnp.int32)
    tables, positions, masks, seens = [], [], [], []
    for tree in range(trees):
        row = after_all((parents[tree], seg_len[tree]), hops[min(tree, len(hops) - 1)])
        reaches, starts_at, ends_at, before = tree_tables(*row)
        seg_count = ends_at.shape[0]
        extra = 16 - seg_count
        reach16 = jnp.pad(reaches, ((0, extra), (0, extra)))
        starts16 = jnp.pad(starts_at, (0, extra))
        before16 = jnp.pad(before, (0, extra))
        ends16 = jnp.pad(ends_at, (0, extra), constant_values=2**30)
        own_seg = jnp.sum((own_tokens[:, None] >= ends_at[None, :]).astype(jnp.int32), axis=1)
        key_seg = jnp.sum((key_tokens[:, None] >= ends_at[None, :]).astype(jnp.int32), axis=1)
        member = own_seg[None, :] == labels[:, None]
        positions.append(
            own_tokens + jnp.sum(jnp.where(member, (before16 - starts16)[:, None], 0), axis=0)
        )
        seen_by = jnp.sum(
            jnp.where(member[:, None, :], reach16.astype(jnp.int32)[:, :, None], 0), axis=0
        )
        masks.append(jnp.where(seen_by > 0, 0.0, NEG).astype(BF16))
        lanes = jnp.arange(128, dtype=jnp.int32)
        key_seg_all = jnp.concatenate([key_seg, jnp.full((block,), seg_count, jnp.int32)])
        hot = (lanes[None, :] == key_seg_all[:, None]) | ((lanes >= 16) & (lanes < 19))[None, :]
        hot = hot.astype(BF16)

        def holds(blocks):
            low = blocks[:, None] * block
            return ((starts_at[None, :] < low + block) & (ends_at[None, :] > low)).astype(F32)

        linked = dot(dot(holds(own_block), reaches.astype(F32)), holds(key_block), 1, 1) > 0.5
        seen = linked & (key_block[None, :] < own_block[:, None])
        rank = jnp.cumsum(seen.astype(jnp.int32), axis=1) - 1
        slots = jnp.arange(key_blocks + 2, dtype=jnp.int32)
        index = jnp.arange(key_blocks, dtype=jnp.int32)
        chosen = seen[:, :, None] & (rank[:, :, None] == slots[None, None, :])
        lists = key_blocks + jnp.sum(
            jnp.where(chosen, index[None, :, None] - key_blocks, 0), axis=1
        )
        counts = jnp.sum(seen.astype(jnp.int32), axis=1)
        tables.append((counts, lists, diagonals, hot))
        on_diagonal = index[None, :] == diagonals[:, None]
        seens.append(jnp.where(on_diagonal, 2, seen.astype(jnp.int32)))
    position = jnp.concatenate(positions)
    (position,) = after_all((position,), hops[-2])
    angles = rope_angles(position, HEAD_SIZE)
    cosine, sine = jnp.cos(angles), jnp.sin(angles)

    inner_a, query, key_value = project(
        first_in, other_in, gain_a[None], w_attn, cosine, sine, head_cols, 2 * kv_cols,
        math.gcd(rows, 256),
    )
    query, key_value = after_all((query, key_value), down_hop)
    kv_rings = [
        Gather(ring, [key_value[tree * chip_rows : (tree + 1) * chip_rows]], True)
        for tree in range(trees)
    ]
    (out_grad,) = after_all((out_grad,), (key_value,))
    other_grad = other_core(out_grad)
    while kv_rings[0].step < chips // 2:
        mark, kv_hop = kv_hop if kv_rings[0].step else None, kv_rings[0].hop()
    kv_hop = kv_rings[1].hop(*mark)
    units_ring = Gather(ring, [units_piece])
    units_hop = units_ring.hop(*kv_rings[0].rightward, *kv_rings[0].leftward) + kv_hop
    kvs = [kv_rings[0].finish()[0].reshape(chips, 1, chip_rows, 2 * kv_cols)]

    def core_sum(own, other):
        return own.astype(F32) + other_core(other.astype(BF16)).astype(F32)

    def laid(buffer, value, tree):
        return lax.dynamic_update_slice(buffer, value[None], (tree, 0, 0))

    mixes, lses, middles, inners, normeds_f, scales_f, lows = [], [], [], [], [], [], []
    for tree in range(trees):
        mixed, lse = attend(tree, tables[tree], query, masks[tree], kvs[tree], rep, block)
        (mixed,) = after_all((mixed,), units_hop)
        part_hop = ()
        if tree == 0:
            while kv_rings[1].step < chips // 2 - 1:
                kv_hop = kv_rings[1].hop(mixed)
            last_hop = kv_rings[1].hop()
            down_hop = down_ring.hop(*kv_hop)
            units_hop = units_ring.hop(*last_hop)
        else:
            units_ring.hop(mixed)
            part_hop = down_hop
        mixes.append(mixed)
        lses.append(lse)
        (part,) = after_all((dot(mixed, w_o, 0, 1),), part_hop)
        lows.append(core_sum(part[:rows], part[rows:]).astype(BF16))
        if tree == 0:
            arrived = other_half(lows[0])
            units_hop += (arrived,)
            (query,) = after_all((query,), lows)
            kvs.append(kv_rings[1].finish()[0].reshape(chips, 1, chip_rows, 2 * kv_cols))
    arrived = [after_all((arrived,), lows[1:])[0]] + [other_half(low) for low in lows[1:]]
    layer_in, out_grad, position = after_all((layer_in, out_grad, position), lows)
    scale_a = row_scale_of(layer_in.astype(F32))
    grad_low = jnp.concatenate([out_grad, other_grad], axis=1).reshape(trees * chip_rows, width)
    cosine_rows, sine_rows = (
        table(rope_angles(position, HEAD_SIZE)).T[:, None, :] for table in (jnp.cos, jnp.sin)
    )
    for tree in range(trees):
        rows_in = layer_in[tree].astype(F32)
        middle = rows_in + (lows[tree].astype(F32) + arrived[tree].astype(F32))
        scale_f = row_scale_of(middle)
        normed_f = middle * scale_f
        inner = (normed_f * gain_f).astype(BF16)
        inners += [inner, other_core(inner)]
        middles.append(middle)
        scales_f.append(scale_f)
        normeds_f.append(normed_f)
    inner_f = jnp.concatenate(inners, axis=0)

    (w_units,) = units_ring.finish(*arrived[1:], grad_low, cosine_rows, sine_rows, scale_a)
    w_units = w_units.reshape(width, -1)
    down_hop = ()
    while down_ring.step < chips // 2 - 1:
        down_hop += down_ring.hop(*arrived[1:])
    hidden, gate_slope, activated = after_all(hidden_units(inner_f, w_units), down_hop)
    down_hop = down_ring.hop(hidden)
    down_terms, grad_low = after_all((unit_grads(grad_low, hidden), grad_low), down_hop)
    (w_d,) = down_ring.finish()
    w_d = w_d.reshape(width, -1)
    (grad_low,) = after_all((grad_low,), (down_terms,))
    grad_gate, grad_up = back_hidden(grad_low, w_d, gate_slope, activated)

    def pieces(term):
        return term.astype(BF16).reshape(chips, width // chips, -1)

    spans = [slice(tree * chip_rows, (tree + 1) * chip_rows) for tree in range(trees)]
    down_ring = Reduce(ring, [pieces(down_terms)])
    down_hop = down_ring.hop()
    core_sums = []
    (grad_gate,) = after_all((grad_gate,), (down_ring.terms[0],))
    for tree in range(trees):
        part = back_units(tree, chip_rows, [grad_gate, grad_up], w_units, [0, 1])
        part = after_all(part, down_hop)
        down_hop = down_ring.hop(part[0])
        (grad_gate,) = after_all((grad_gate,), part)
        core_sums.append(core_sum(*part))
    lows = [own.astype(BF16) for own in core_sums]
    arrived = [other_half(lows[0])]
    inner_f, hidden = after_all((inner_f, hidden), lows)
    units_terms = unit_grads(inner_f, grad_gate, grad_up)
    units_terms, arrived[0] = after_all((units_terms, arrived[0]), down_hop)
    arrived.append(other_half(after_all(lows[1:], arrived)[0]))
    units_ring = Reduce(ring, [pieces(units_terms)])
    units_hop = units_ring.hop() + down_ring.hop(units_terms)
    arrived[0] = after_all(arrived[:1], (units_terms,))[0]

    grads_middle, grads_low = [], []

    def backward_norm(tree):
        grad_inner = lows[tree].astype(F32) + arrived[tree].astype(F32)
        grad_middle = out_grad[tree].astype(F32) + norm_back(
            grad_inner * gain_f, normeds_f[tree], scales_f[tree]
        )
        low = grad_middle.astype(BF16)
        grads_middle.append(grad_middle)
        grads_low.append(low)
        return jnp.concatenate([low, other_core(low)], axis=0)

    mid_lows, out_lows, out_arrived = [backward_norm(0)], [], []
    grads_qkv, gain_a_terms = [], []

    def back_part(tree, kv_sums):
        rows_of = (cosine_rows[spans[tree]], -sine_rows[spans[tree]])
        parts = grad_queries[groups * tree : groups * (tree + 1)]
        for group in range(groups):
            kv_sum = kv_sums[:, 128 * group : 128 * (group + 1)]
            grad_k = kv_sum[:, None, :HEAD_SIZE]
            half = HEAD_SIZE // 2
            first, second = turn(grad_k[..., :half], grad_k[..., half:], *rows_of)
            kv_parts = [first[:, 0], second[:, 0], kv_sum[:, HEAD_SIZE:]]
            parts.append(jnp.concatenate(kv_parts, axis=1).astype(BF16))
        grad_qkv = jnp.concatenate(parts, axis=1)
        grads_qkv.append(grad_qkv)
        part = dot(grad_qkv, w_qkv, 1, 1)
        gain_a_terms.append(core_sum(part[:rows], part[rows:]))
        return gain_a_terms[-1].astype(BF16)

    grad_queries, grad_kvs = [], []
    for tree in range(trees):
        grad_mixed = dot(w_o, mid_lows[tree], 0, 1).astype(BF16)
        for group in range(groups):
            grad_query, grad_kv = attend_back(
                tree,
                group,
                seens[tree],
                tables[tree][3],
                query,
                masks[tree],
                mixes[tree],
                grad_mixed,
                lses[tree],
                kvs[tree],
                cosine,
                sine,
                rep,
                block,
                grad_kvs[-1] if group else None,
            )
            grad_query, grad_kv = after_all((grad_query, grad_kv), units_hop)
            grad_queries.append(grad_query)
            grad_kvs.append(grad_kv)
            units_hop = ()
            if units_ring.left > 0 and group < groups - 1:
                units_hop = units_ring.hop(grad_query)
            (grad_mixed,) = after_all((grad_mixed,), (grad_query,))
            if tree == 0 and group == 0:
                (hidden,) = after_all((hidden,), (grad_query,))
                out_parts = [
                    back_units(tree, chip_rows, [hidden], w_d, [0]) for tree in range(trees)
                ]
                out_parts[0] = after_all(out_parts[0], arrived[1:])
                out_lows = [core_sum(*part).astype(BF16) for part in out_parts]
                (grad_mixed,) = after_all((grad_mixed,), out_lows)
                out_arrived.append(other_half(out_lows[0]))
                units_hop += tuple(out_arrived)
            elif tree and group < groups - 1:
                while kv_ring.left > 0:
                    units_hop += kv_ring.hop(grad_query)
        if tree == 0:
            kv_ring = Reduce(ring, grad_kvs[-1:])
            kv_ring.hop()
            arrived[-1] = after_all(arrived[-1:], (grad_query,))[0]
            mid_lows.append(backward_norm(1))
            kv_hop = kv_ring.hop()
            out_terms = pieces(
                dot(jnp.concatenate(mid_lows, axis=0), jnp.concatenate(mixes, axis=1), 0, 1)
            )
            mid_lows[1] = after_all(mid_lows[1:], (out_terms, *kv_hop))[0]
            out_arrived.append(other_half(after_all(out_lows[1:], (grad_query,))[0]))
            units_hop += units_ring.hop(*kv_hop) + kv_ring.hop(out_terms)
            units_hop += tuple(out_arrived[1:])
    out_arrived = after_all(out_arrived, (grad_queries[-1],))
    (down_sum,), (units_sum,) = down_ring.finish(), units_ring.finish()
    outputs = unwritten(out_terms, (trees, rows, width))
    out_arrived = after_all(out_arrived, (grad_queries[-1],))
    for tree in range(trees):
        summed = out_lows[tree].astype(F32) + out_arrived[tree].astype(F32)
        outputs = laid(outputs, (middles[tree] + summed).astype(BF16), tree)

    (layer_in,) = after_all((layer_in,), (grad_queries[-1],))
    normed_a = layer_in.astype(F32) * scale_a
    down_grad = row_grad(down_sum)
    lows = [back_part(0, kv_ring.finish()[0])]
    arrived = [other_half(lows[0])]
    (kv_terms,) = after_all(grad_kvs[-1:], lows)
    (kv_sums,) = after_all(ring_sum([kv_terms], 1), arrived)
    lows.append(back_part(1, kv_sums))
    (inner_a,) = after_all((inner_a,), (grads_qkv[-1],))
    gate_grad, up_grad = (
        column_grad(part) for part in jnp.split(units_sum, 2, axis=1)
    )
    core_sums = after_all(core_sums + gain_a_terms, lows)
    gain_terms = jnp.stack(
        [
            sum(jnp.sum(core_sums[trees + i] * normed_a[i], axis=0) for i in range(trees)),
            sum(jnp.sum(core_sums[i] * normeds_f[i], axis=0) for i in range(trees)),
        ]
    )
    gain_terms = jnp.moveaxis(gain_terms.astype(BF16).reshape(2, chips, width // chips), 1, 0)
    gain_terms = jnp.pad(gain_terms, ((0, 0), (0, 30), (0, 0)))
    term_qkv = unit_grads(inner_a, jnp.concatenate(grads_qkv, axis=0))
    qkv_sum, out_sum, gain_sums, theirs = ring_sum(
        [pieces(term_qkv), out_terms, gain_terms], 2, lows[1]
    )
    arrived.append(theirs)
    out_proj_grad = row_grad(out_sum)
    kv_parts = qkv_sum[:, head_cols:].reshape(-1, groups, 2, HEAD_SIZE)
    key_sum, value_sum = (kv_parts[:, :, i].reshape(-1, kv_cols) for i in range(2))

    keep, give = split_by_core(gain_sums[:8], 1)
    gain_sums = keep + other_core(give)
    gain_sums = gain_sums + other_half(gain_sums)
    gain_a_grad, gain_f_grad = gain_sums[0], gain_sums[1]
    input_grad = unwritten(scale_a, (trees, rows, width))
    for tree in range(trees):
        grad_inner = lows[tree].astype(F32) + arrived[tree].astype(F32)
        input_grad = laid(
            input_grad,
            grads_middle[tree] + norm_back(grad_inner * gain_a, normed_a[tree], scale_a[tree]),
            tree,
        )

    return (
        outputs,
        input_grad,
        gain_a_grad,
        column_grad(qkv_sum[:, :head_cols]),
        column_grad(key_sum),
        column_grad(value_sum),
        out_proj_grad,
        gain_f_grad,
        gate_grad,
        up_grad,
        down_grad,
    )


def solution(mesh):
    devices = mesh.devices
    mesh = Mesh(devices.reshape(-1, 2, devices.shape[1]), ("zy", "core", "tp"))
    fsdp = ("zy", "core")
    specs = (
        P(fsdp),
        P(fsdp, "tp"),
        P(fsdp, "tp"),
        P(fsdp, "tp"),
        P("tp", fsdp),
        P(fsdp),
        P(fsdp, "tp"),
        P(fsdp, "tp"),
        P("tp", fsdp),
    )
    tokens = P(None, fsdp, None)
    return jax.shard_map(
        shards,
        mesh=mesh,
        in_specs=(tokens, tokens, P(), P()) + specs,
        out_specs=(tokens, tokens) + specs,
        check_vma=False,
    )
```

```python
import functools
import math

import jax
import jax.numpy as jnp
from jax import lax
from jax.experimental import pallas as pl
from jax.experimental.pallas import tpu as pltpu
from jax.sharding import Mesh
from jax.sharding import PartitionSpec as P

QUERY_HEADS = 32
KEY_VALUE_HEADS = 8
HEAD_SIZE = 64
LEVELS = 3

EPS = 1e-05
THETA = 500000.0
NEG = -1e30
LN2 = math.log(2.0)
SWAP = [(0, 1), (1, 0)]
F32 = jnp.float32
BF16 = jnp.bfloat16
SMALL = pl.CostEstimate(flops=2**20, bytes_accessed=2**10, transcendentals=0)


def dot(left, right, left_dim=1, right_dim=0):
    return lax.dot_general(
        left, right, (((left_dim,), (right_dim,)), ((), ())), preferred_element_type=F32
    )


def row_scale_of(rows_in):
    return lax.rsqrt(jnp.mean(rows_in * rows_in, axis=-1, keepdims=True) + EPS)


def norm_back(grad_normed, normed, row_scale):
    return row_scale * (
        grad_normed - normed * jnp.mean(grad_normed * normed, axis=-1, keepdims=True)
    )


def rope_angles(position, head_dim):
    half_dim = head_dim // 2
    index_row = jnp.arange(half_dim, dtype=F32)
    inverse = THETA ** (-2.0 * index_row / head_dim)
    wavelen = 2.0 * math.pi / inverse
    smooth = jnp.clip((8192.0 / wavelen - 1.0) / 3.0, 0.0, 1.0)
    inverse = (1.0 - smooth) * inverse / 32.0 + smooth * inverse
    return inverse[:, None] * position.astype(F32)[None, :]


def turn(first_half, second_half, cosine, sine):
    return first_half * cosine - second_half * sine, second_half * cosine + first_half * sine


def tree_tables(parents_row, lengths):
    seg_count = parents_row.shape[0]
    labels = jnp.arange(seg_count, dtype=jnp.int32)
    ends_at = jnp.cumsum(lengths)
    starts_at = ends_at - lengths
    reaches = labels[:, None] == labels[None, :]
    climber = labels
    for _ in range(LEVELS - 1):
        climber = jnp.sum(
            jnp.where(climber[:, None] == labels[None, :], parents_row[None, :], 0), axis=1
        )
        reaches = reaches | (climber[:, None] == labels[None, :])
    before = jnp.sum(
        jnp.where(reaches & (labels[:, None] != labels[None, :]), lengths[None, :], 0), axis=1
    )
    return reaches, starts_at, ends_at, before


def after_all(values, others):
    if not others:
        return list(values)
    return list(lax.optimization_barrier(tuple(values) + tuple(others))[: len(values)])


def unwritten(like, shape):
    return pl.pallas_call(
        lambda like_ref, out_ref: None,
        in_specs=[pl.BlockSpec(memory_space=pl.ANY)],
        out_specs=pl.BlockSpec(memory_space=pl.ANY),
        out_shape=jax.ShapeDtypeStruct(shape, like.dtype),
        name="buffer",
    )(like)


class Ring:
    def __init__(self):
        self.count = lax.axis_size("zy")
        count = self.count
        place = [2 * i if i < count // 2 else 2 * (count - 1 - i) + 1 for i in range(count)]
        self.right = [(place[i], place[(i + 1) % count]) for i in range(count)]
        self.left = [(b, a) for a, b in self.right]
        me = lax.axis_index("zy")
        self.spot = jnp.where(me % 2 == 0, me // 2, count - 1 - me // 2)

    def chip(self, offset):
        spot = lax.rem(self.spot + offset + self.count, self.count)
        return jnp.where(spot < self.count // 2, 2 * spot, 2 * (self.count - 1 - spot) + 1)

    def go_right(self, value):
        return lax.ppermute(value, "zy", self.right)

    def go_left(self, value):
        return lax.ppermute(value, "zy", self.left)

    def put(self, whole, part, offset, row=0):
        at = (self.chip(offset), row) + (0,) * (part.ndim - 1)
        return lax.dynamic_update_slice(whole, part[None], at)


class Gather:
    def __init__(self, ring, pieces, tidy=False):
        self.ring, self.step, self.tidy, self.laid = ring, 0, tidy, ()
        self.cuts = [piece.shape[0] // 2 for piece in pieces]
        wholes = [unwritten(piece, (ring.count,) + piece.shape) for piece in pieces]
        self.wholes = [ring.put(whole, piece, 0) for whole, piece in zip(wholes, pieces)]
        self.rightward = self.leftward = list(pieces)

    def hop(self, *others):
        ring, count = self.ring, len(self.cuts)
        both = after_all(self.rightward + self.leftward, others + self.laid)
        rightward, leftward = both[:count], both[count:]
        self.step += 1
        self.laid = tuple(self.wholes) if self.tidy else ()
        far = self.step == ring.count // 2
        if far:
            rightward = [part[:cut] for part, cut in zip(rightward, self.cuts)]
            leftward = [part[cut:] for part, cut in zip(leftward, self.cuts)]
        rightward = [ring.go_right(part) for part in rightward]
        leftward = [ring.go_left(part) for part in leftward]
        for i, cut in enumerate(self.cuts):
            whole = ring.put(self.wholes[i], rightward[i], -self.step)
            self.wholes[i] = ring.put(whole, leftward[i], self.step, cut if far else 0)
        self.rightward, self.leftward = rightward, leftward
        return tuple(rightward) + tuple(leftward)

    def finish(self, *others):
        while self.step < self.ring.count // 2:
            self.hop(*others)
        return self.wholes


class Reduce:
    def __init__(self, ring, terms):
        self.ring, self.terms, self.left = ring, list(terms), ring.count // 2
        self.cuts = [term.shape[1] // 2 for term in terms]
        self.rightward = self.leftward = None

    def each(self, offset):
        chip = self.ring.chip(offset)
        return [lax.dynamic_index_in_dim(term, chip, 0, keepdims=False) for term in self.terms]

    def hop(self, *others):
        ring, step, count = self.ring, self.left, len(self.cuts)
        if self.rightward is None:
            far = self.each(step)
            rightward = [part[:cut] for part, cut in zip(far, self.cuts)]
            leftward = [part[cut:] for part, cut in zip(far, self.cuts)]
        else:
            rightward, leftward = list(self.rightward), list(self.leftward)
            mine, other = self.each(step), self.each(-step)
            if step == ring.count // 2 - 1:
                for i, cut in enumerate(self.cuts):
                    parts = [add_low(mine[i][:cut], rightward[i]), mine[i][cut:]]
                    rightward[i] = jnp.concatenate(parts, axis=0)
                    parts = [other[i][:cut], add_low(other[i][cut:], leftward[i])]
                    leftward[i] = jnp.concatenate(parts, axis=0)
            else:
                rightward = [add_low(one, part) for one, part in zip(mine, rightward)]
                leftward = [add_low(one, part) for one, part in zip(other, leftward)]
        both = after_all(rightward + leftward, others)
        rightward, leftward = both[:count], both[count:]
        self.rightward = [ring.go_right(part) for part in rightward]
        self.leftward = [ring.go_left(part) for part in leftward]
        self.left -= 1
        return tuple(self.rightward) + tuple(self.leftward)

    def finish(self, *others):
        while self.left > 0:
            self.hop(*others)
        return [
            mine.astype(F32) + one.astype(F32) + two.astype(F32)
            for mine, one, two in zip(self.each(0), self.rightward, self.leftward)
        ]


def add_low(left, right):
    return (left.astype(F32) + right.astype(F32)).astype(BF16)


def other_core(value):
    return lax.ppermute(value, "core", SWAP)


def other_half(value):
    return lax.ppermute(value, "tp", SWAP)


def by_core(own, other, axis):
    first = lax.axis_index("core") == 0
    return jnp.concatenate(
        [jnp.where(first, own, other), jnp.where(first, other, own)], axis=axis
    )


def split_by_core(value, axis):
    core = lax.axis_index("core")
    size = value.shape[axis] // 2
    return (
        lax.dynamic_slice_in_dim(value, core * size, size, axis),
        lax.dynamic_slice_in_dim(value, (1 - core) * size, size, axis),
    )


def split3(value):
    high = value.astype(BF16)
    rest = value - high.astype(F32)
    middle = rest.astype(BF16)
    low = (rest - middle.astype(F32)).astype(BF16)
    return high, middle, low


def causal(scores, block):
    key_at = lax.broadcasted_iota(jnp.int32, scores.shape, 0)
    query_at = lax.rem(lax.broadcasted_iota(jnp.int32, scores.shape, 1), block)
    return jnp.where(key_at <= query_at, scores, NEG)


def block_of(ref, index, block, per_piece):
    piece = lax.div(index, per_piece)
    start = pl.multiple_of(lax.rem(index, per_piece) * block, block)
    return ref[piece, 0, pl.ds(start, block), :]


def attend_kernel(
    block, rep, per_piece, count_ref, list_ref, diag_ref, query_ref, mask_ref, kv_ref, hot_ref,
    out_ref, lse_ref, query_aug, turned,
):
    at = pl.program_id(1)
    key_blocks = hot_ref.shape[0] // block - 1

    @pl.when(at == 0)
    def _():
        rows = per_piece * block
        for piece in range(kv_ref.shape[0]):
            turned[:, piece * rows : (piece + 1) * rows] = kv_ref[piece, 0].T

    query_aug[HEAD_SIZE:, :] = jnp.zeros_like(query_aug[HEAD_SIZE:, :])
    for r in range(rep):
        columns = slice(r * block, (r + 1) * block)
        query_aug[:HEAD_SIZE, columns] = query_ref[r * HEAD_SIZE : (r + 1) * HEAD_SIZE, :]
        query_aug[128:144, columns] = mask_ref[...]

    def scores_of(index):
        keys = block_of(kv_ref, jnp.minimum(index, key_blocks - 1), block, per_piece)
        hot = hot_ref[pl.ds(pl.multiple_of(index * block, block), block), :]
        return jnp.dot(
            jnp.concatenate([keys, hot], axis=1), query_aug[...], preferred_element_type=F32
        )

    def values_of(index):
        index = jnp.minimum(index, key_blocks - 1)
        return turned[HEAD_SIZE:, pl.ds(pl.multiple_of(index * block, block), block)]

    diagonal = diag_ref[at]
    scores = causal(scores_of(diagonal), block)
    top = jnp.max(scores, axis=0, keepdims=True)
    probs = jnp.exp2(scores - top)
    total = jnp.sum(probs, axis=0, keepdims=True)
    mixed = jnp.dot(values_of(diagonal), probs.astype(BF16), preferred_element_type=F32)

    def step(j, carry):
        top, total, mixed = carry
        one, two = list_ref[at, 2 * j], list_ref[at, 2 * j + 1]
        first, second = scores_of(one), scores_of(two)
        new = jnp.maximum(top, jnp.max(first, axis=0, keepdims=True))
        new = jnp.maximum(new, jnp.max(second, axis=0, keepdims=True))
        factor = jnp.exp2(top - new)
        first, second = jnp.exp2(first - new), jnp.exp2(second - new)
        total = (
            total * factor
            + jnp.sum(first, axis=0, keepdims=True)
            + jnp.sum(second, axis=0, keepdims=True)
        )
        values = jnp.concatenate([values_of(one), values_of(two)], axis=1)
        probs = jnp.concatenate([first.astype(BF16), second.astype(BF16)], axis=0)
        mixed = mixed * factor + jnp.dot(values, probs, preferred_element_type=F32)
        return new, total, mixed

    pairs = lax.div(count_ref[at] + 1, 2)
    top, total, mixed = lax.fori_loop(0, pairs, step, (top, total, mixed))
    mixed = mixed * (1.0 / total)
    lse = top + jnp.log2(total)
    for r in range(rep):
        columns = slice(r * block, (r + 1) * block)
        out_ref[r * HEAD_SIZE : (r + 1) * HEAD_SIZE, :] = mixed[:, columns].astype(BF16)
        lse_ref[0, r : r + 1, :] = lse[:, columns]


def attend(tree, tables, query, mask, kv, rep, block):
    counts, lists, diagonals, hot = tables
    heads = query.shape[0]
    pieces, _, rows, _ = kv.shape
    groups, query_blocks = heads // (rep * HEAD_SIZE), rows // block
    keys = pieces * rows
    grid_spec = pltpu.PrefetchScalarGridSpec(
        num_scalar_prefetch=3,
        grid=(groups, query_blocks),
        in_specs=[
            pl.BlockSpec(
                (rep * HEAD_SIZE, block), lambda g, q, *_: (g, tree * query_blocks + q)
            ),
            pl.BlockSpec((16, block), lambda g, q, *_: (0, q)),
            pl.BlockSpec((pieces, 1, rows, 128), lambda g, q, *_: (0, 0, 0, g)),
            pl.BlockSpec((keys + block, 128), lambda g, q, *_: (0, 0)),
        ],
        out_specs=[
            pl.BlockSpec((rep * HEAD_SIZE, block), lambda g, q, *_: (g, q)),
            pl.BlockSpec((1, rep, block), lambda g, q, *_: (g, 0, q)),
        ],
        scratch_shapes=[
            pltpu.VMEM((256, rep * block), BF16),
            pltpu.VMEM((128, keys), BF16),
        ],
    )
    return pl.pallas_call(
        functools.partial(attend_kernel, block, rep, rows // block),
        grid_spec=grid_spec,
        out_shape=[
            jax.ShapeDtypeStruct((heads, rows), BF16),
            jax.ShapeDtypeStruct((groups, rep, rows), F32),
        ],
        compiler_params=pltpu.CompilerParams(vmem_limit_bytes=48 * 2**20),
        cost_estimate=SMALL,
        name="tree_attention",
    )(counts, lists, diagonals, query, mask, kv, hot)


def attend_back_kernel(
    block, rep, per_piece, seen_ref, query_ref, mask_ref, mixed_ref, grad_ref, lse_ref, kv_ref,
    hot_ref, cosine_ref, sine_ref, before_ref, grad_query_ref, grad_kv_ref, augs, turned_rows,
    key_turned, grad_query, grad_kv,
):
    rows = per_piece * block
    query_blocks = rows // block
    key_blocks = kv_ref.shape[0] * per_piece
    width = rep * block

    for piece in range(kv_ref.shape[0]):
        key_turned[:, piece * rows : (piece + 1) * rows] = kv_ref[piece, 0].T
    grad_kv[...] = jnp.zeros_like(grad_kv)
    grad_query[...] = jnp.zeros_like(grad_query)
    augs[...] = jnp.zeros_like(augs)
    none = jnp.zeros((HEAD_SIZE, block), BF16)
    for at in range(query_blocks):
        columns = slice(at * block, (at + 1) * block)
        for r in range(rep):
            here = slice(2 * at * width + r * block, 2 * at * width + (r + 1) * block)
            there = slice((2 * at + 1) * width + r * block, (2 * at + 1) * width + (r + 1) * block)
            head = slice(r * HEAD_SIZE, (r + 1) * HEAD_SIZE)
            query, grad = query_ref[head, columns], grad_ref[head, columns]
            augs[:HEAD_SIZE, here] = query
            augs[HEAD_SIZE : 2 * HEAD_SIZE, there] = grad
            delta = jnp.sum(
                grad.astype(F32) * mixed_ref[head, columns].astype(F32), axis=0, keepdims=True
            )
            empty = jnp.zeros((13, block), BF16)
            augs[128:160, here] = jnp.concatenate(
                [mask_ref[:, columns], *split3(-lse_ref[0, r : r + 1, columns]), empty], axis=0
            )
            augs[128:160, there] = jnp.concatenate(
                [jnp.zeros((16, block), BF16), *split3(-delta), empty], axis=0
            )
            turned_rows[here, :] = jnp.concatenate([none, grad], axis=0).T
            turned_rows[there, :] = jnp.concatenate([query, none], axis=0).T

    def over_keys(index, _):
        rows_at = pl.ds(pl.multiple_of(index * block, block), block)
        for at in range(query_blocks):
            columns = slice(2 * at * width, (2 * at + 2) * width)

            def work(on_diagonal):
                both = jnp.dot(
                    jnp.concatenate(
                        [block_of(kv_ref, index, block, per_piece), hot_ref[rows_at, :]], axis=1
                    ),
                    augs[:, columns],
                    preferred_element_type=F32,
                )
                scores, grad_probs = both[:, :width], both[:, width:]
                if on_diagonal:
                    scores = causal(scores, block)
                probs = jnp.exp2(scores)
                grad_scores = (probs * grad_probs).astype(BF16)
                grad_kv[rows_at, :] += jnp.dot(
                    jnp.concatenate([probs.astype(BF16), grad_scores], axis=1),
                    turned_rows[columns, :],
                    preferred_element_type=F32,
                )
                grad_query[:, at * width : (at + 1) * width] += jnp.dot(
                    key_turned[:HEAD_SIZE, rows_at], grad_scores, preferred_element_type=F32
                )

            seen = seen_ref[at, index]
            pl.when(seen == 1)(functools.partial(work, False))
            pl.when(seen == 2)(functools.partial(work, True))
        return 0

    lax.fori_loop(0, key_blocks, over_keys, 0)
    for at in range(query_blocks):
        columns = slice(at * block, (at + 1) * block)
        cosine = cosine_ref[:, columns] * HEAD_SIZE**-0.5
        sine = -sine_ref[:, columns] * HEAD_SIZE**-0.5
        for r in range(0, rep, 2):
            parts = []
            for head in (r, r + 1):
                here = slice(at * width + head * block, at * width + (head + 1) * block)
                grad = grad_query[:, here]
                half = HEAD_SIZE // 2
                parts += turn(grad[:half], grad[half:], cosine, sine)
            grad_query_ref[columns, r * HEAD_SIZE : (r + 2) * HEAD_SIZE] = (
                jnp.concatenate(parts, axis=0).T.astype(BF16)
            )
    for piece in range(kv_ref.shape[0]):
        grads = grad_kv[piece * rows : (piece + 1) * rows, :]
        lanes = lax.broadcasted_iota(jnp.int32, grads.shape, 1)
        grad_kv_ref[piece] = jnp.where(lanes < HEAD_SIZE, grads * LN2, grads).astype(BF16)


def attend_back(
    tree, group, seen, hot, query, mask, mixed, grad, lse, kv, cosine, sine, rep, block, before
):
    pieces, _, rows, _ = kv.shape
    keys = pieces * rows
    heads = rep * HEAD_SIZE
    head = pl.BlockSpec((heads, rows), lambda i, *_: (group, 0))
    table = pl.BlockSpec((HEAD_SIZE // 2, rows), lambda i, *_: (0, tree))
    grid_spec = pltpu.PrefetchScalarGridSpec(
        num_scalar_prefetch=1,
        grid=(1,),
        in_specs=[
            pl.BlockSpec((heads, rows), lambda i, *_: (group, tree)),
            pl.BlockSpec((16, rows), lambda i, *_: (0, 0)),
            head,
            head,
            pl.BlockSpec((1, rep, rows), lambda i, *_: (group, 0, 0)),
            pl.BlockSpec((pieces, 1, rows, 128), lambda i, *_: (0, 0, 0, group)),
            pl.BlockSpec((keys + block, 128), lambda i, *_: (0, 0)),
            table,
            table,
            pl.BlockSpec(memory_space=pl.ANY),
        ],
        out_specs=[
            pl.BlockSpec((rows, heads), lambda i, *_: (0, 0)),
            pl.BlockSpec((pieces, rows, 128), lambda i, *_: (0, 0, group)),
        ],
        scratch_shapes=[
            pltpu.VMEM((256, 2 * rep * rows), BF16),
            pltpu.VMEM((2 * rep * rows, 128), BF16),
            pltpu.VMEM((128, keys), BF16),
            pltpu.VMEM((HEAD_SIZE, rep * rows), F32),
            pltpu.VMEM((keys, 128), F32),
        ],
    )
    return pl.pallas_call(
        functools.partial(attend_back_kernel, block, rep, rows // block),
        grid_spec=grid_spec,
        out_shape=[
            jax.ShapeDtypeStruct((rows, heads), BF16),
            jax.ShapeDtypeStruct((pieces, rows, kv.shape[3]), BF16),
        ],
        input_output_aliases={10: 1} if group else {},
        compiler_params=pltpu.CompilerParams(vmem_limit_bytes=56 * 2**20),
        cost_estimate=SMALL,
        name="tree_attention_back",
    )(seen, query, mask, mixed, grad, lse, kv, hot, cosine, sine, cosine if before is None else before)


def project_kernel(
    heads, columns, own_ref, other_ref, gain_ref, weight_ref, cosine_ref, sine_ref, inner_ref, query_ref,
    kv_ref, rows,
):
    mine = lax.rem(pl.program_id(0), 2) == 0

    @pl.when(mine)
    def _():
        rows[...] = own_ref[0].astype(F32)

    @pl.when(jnp.logical_not(mine))
    def _():
        rows[...] = other_ref[0].astype(F32)

    x = rows[...]
    inner = (x * row_scale_of(x) * gain_ref[...]).astype(BF16)
    inner_ref[...] = inner
    made = jnp.dot(inner, weight_ref[:, :columns], preferred_element_type=F32)
    cosine, sine = cosine_ref[...], sine_ref[...]
    half = HEAD_SIZE // 2

    def turned(values):
        parts = []
        for start in range(0, values.shape[0], HEAD_SIZE):
            parts += turn(
                values[start : start + half], values[start + half : start + HEAD_SIZE], cosine, sine
            )
        return jnp.concatenate(parts, axis=0)

    query_ref[...] = (turned(made[:, :heads].T) * (HEAD_SIZE**-0.5 / LN2)).astype(BF16)
    kv = made[:, heads:].T
    parts = []
    for start in range(0, kv.shape[0], 128):
        parts += [turned(kv[start : start + HEAD_SIZE]), kv[start + HEAD_SIZE : start + 128]]
    kv_ref[...] = jnp.concatenate(parts, axis=0).T.astype(BF16)


def project(own, other, gain, weight, cosine, sine, heads, kv_columns, tile):
    trees, rows, width = own.shape
    tiles = rows // tile
    last = trees * tiles - 1

    def place(half):
        def index(t, j):
            tree, at = t // 2, t % 2
            same = at == half
            if half == 0:
                return (jnp.where(same, tree, tree), jnp.where(same, j, tiles - 1), 0)
            return (tree, jnp.where(same, j, 0), 0)

        return index

    flat = lambda t, j: (t * tiles + j, 0)
    lanes = lambda t, j: (0, t * tiles + j)
    tokens = 2 * trees * rows
    columns = heads + kv_columns
    return pl.pallas_call(
        functools.partial(project_kernel, heads, columns),
        grid=(2 * trees, tiles),
        in_specs=[
            pl.BlockSpec((1, tile, width), place(0)),
            pl.BlockSpec((1, tile, width), place(1)),
            pl.BlockSpec((1, width), lambda t, j: (0, 0)),
            pl.BlockSpec((width, columns), lambda t, j: (0, 0)),
            pl.BlockSpec((HEAD_SIZE // 2, tile), lanes),
            pl.BlockSpec((HEAD_SIZE // 2, tile), lanes),
        ],
        out_specs=[
            pl.BlockSpec((tile, width), flat),
            pl.BlockSpec((heads, tile), lanes),
            pl.BlockSpec((tile, columns - heads), flat),
        ],
        out_shape=[
            jax.ShapeDtypeStruct((tokens, width), BF16),
            jax.ShapeDtypeStruct((heads, tokens), BF16),
            jax.ShapeDtypeStruct((tokens, columns - heads), BF16),
        ],
        scratch_shapes=[pltpu.VMEM((tile, width), F32)],
        compiler_params=pltpu.CompilerParams(vmem_limit_bytes=48 * 2**20),
        cost_estimate=SMALL,
        name="project",
    )(own, other, gain, weight, cosine, sine)


def units_kernel(inner_ref, gate_ref, up_ref, hidden_ref, slope_ref, activated_ref):
    inner = inner_ref[...]
    gate = jnp.dot(inner, gate_ref[...], preferred_element_type=F32)
    up = jnp.dot(inner, up_ref[...], preferred_element_type=F32)
    sigmoid = jax.nn.sigmoid(gate)
    activated = gate * sigmoid
    hidden_ref[...] = (activated * up).astype(BF16)
    slope_ref[...] = (up * sigmoid * (1.0 + gate * (1.0 - sigmoid))).astype(BF16)
    activated_ref[...] = activated.astype(BF16)


def back_hidden_kernel(grad_ref, down_ref, slope_ref, activated_ref, grad_gate_ref, grad_up_ref):
    grad_hidden = jnp.dot(grad_ref[...], down_ref[...], preferred_element_type=F32)
    grad_gate_ref[...] = (grad_hidden * slope_ref[...].astype(F32)).astype(BF16)
    grad_up_ref[...] = (grad_hidden * activated_ref[...].astype(F32)).astype(BF16)


def over_units(kernel, rows_in, weights, firsts, units, tiles_in, made, name):
    tokens, width = rows_in.shape
    rows, columns = math.gcd(tokens, 2048 // len(firsts)), math.gcd(units, 512)
    tiles = units // columns
    tile = pl.BlockSpec((rows, columns), lambda j, i: (i, j))
    wide = [
        pl.BlockSpec((width, columns), lambda j, i, first=first: (0, first * tiles + j))
        for first in firsts
    ]
    return pl.pallas_call(
        kernel,
        grid=(tiles, tokens // rows),
        in_specs=[pl.BlockSpec((rows, width), lambda j, i: (i, 0)), *wide]
        + [tile] * len(tiles_in),
        out_specs=[tile] * made,
        out_shape=[jax.ShapeDtypeStruct((tokens, units), BF16)] * made,
        compiler_params=pltpu.CompilerParams(vmem_limit_bytes=56 * 2**20),
        cost_estimate=SMALL,
        name=name,
    )(rows_in, *([weights] * len(firsts)), *tiles_in)


def hidden_units(inner, weights):
    units = weights.shape[1] // 2
    return over_units(units_kernel, inner, weights, (0, 1), units, (), 3, "hidden_units")


def back_hidden(grad, down, slope, activated):
    units = down.shape[1]
    return over_units(
        back_hidden_kernel, grad, down, (0,), units, (slope, activated), 2, "back_hidden"
    )


def back_units_kernel(count, *refs):
    *refs, own_ref, other_ref = refs
    contract = (((1,), (1,)), ((), ()))
    total = None
    for units_ref, weight_ref in zip(refs[:count], refs[count:]):
        term = lax.dot_general(
            units_ref[...], weight_ref[...], contract, preferred_element_type=F32
        )
        total = term if total is None else total + term
    half = own_ref.shape[0]
    own_ref[...] = total[:half].astype(BF16)
    other_ref[...] = total[half:].astype(BF16)


def back_units(tree, tokens, units, weights, places):
    width, size = weights.shape[0], units[0].shape[1]
    columns = math.gcd(width, 512)
    tall = pl.BlockSpec((tokens, size), lambda j: (tree, 0))
    made = jax.ShapeDtypeStruct((tokens // 2, width), BF16)
    return pl.pallas_call(
        functools.partial(back_units_kernel, len(units)),
        grid=(width // columns,),
        in_specs=[tall] * len(units)
        + [pl.BlockSpec((columns, size), lambda j, at=at: (j, at)) for at in places],
        out_specs=[pl.BlockSpec((tokens // 2, columns), lambda j: (0, j))] * 2,
        out_shape=[made, made],
        compiler_params=pltpu.CompilerParams(vmem_limit_bytes=56 * 2**20),
        cost_estimate=SMALL,
        name="back_units",
    )(*units, *([weights] * len(units)))


def unit_grads_kernel(tiles, rows_ref, *refs):
    *grad_refs, out_ref, turned = refs
    at = pl.program_id(1)

    @pl.when(at == 0)
    def _():
        turned[...] = rows_ref[...].T

    for i, grad_ref in enumerate(grad_refs):

        @pl.when((at >= i * tiles) & (at < (i + 1) * tiles))
        def _():
            out_ref[...] = jnp.dot(
                turned[...], grad_ref[...], preferred_element_type=F32
            ).astype(BF16)


def unit_grads(rows_in, *grads):
    tokens, width = rows_in.shape
    units = grads[0].shape[1]
    rows, columns = math.gcd(width, 1024), math.gcd(units, 1024 // len(grads))
    tiles = units // columns

    def place(i):
        return lambda at, j: (0, jnp.clip(j - i * tiles, 0, tiles - 1))

    return pl.pallas_call(
        functools.partial(unit_grads_kernel, tiles),
        grid=(width // rows, tiles * len(grads)),
        in_specs=[pl.BlockSpec((tokens, rows), lambda i, j: (0, i))]
        + [pl.BlockSpec((tokens, columns), place(i)) for i in range(len(grads))],
        out_specs=pl.BlockSpec((rows, columns), lambda i, j: (i, j)),
        out_shape=jax.ShapeDtypeStruct((width, units * len(grads)), BF16),
        scratch_shapes=[pltpu.VMEM((rows, tokens), BF16)],
        compiler_params=pltpu.CompilerParams(vmem_limit_bytes=56 * 2**20),
        cost_estimate=SMALL,
        name="unit_grads",
    )(rows_in, *grads)


def ring_place(spot, count):
    spot = lax.rem(spot + count, count)
    return jnp.where(spot < count // 2, 2 * spot, 2 * (count - 1 - spot) + 1)


def ring_sum_kernel(count, arrays, swaps, *refs):
    terms_refs, refs = refs[:arrays], refs[arrays:]
    if swaps:
        swap_ref, *refs, swap_send, swap_receive = refs
    out_refs, refs = refs[:arrays], refs[arrays:]
    if swaps:
        theirs_ref, *refs = refs
    helds, from_lefts, from_rights = (refs[i * arrays : (i + 1) * arrays] for i in range(3))
    load_sems, send_sems, receive_sems = refs[3 * arrays :]
    half = count // 2
    me = lax.axis_index("zy")
    spot = jnp.where(lax.rem(me, 2) == 0, lax.div(me, 2), count - 1 - lax.div(me, 2))
    right, left = ring_place(spot + 1, count), ring_place(spot - 1, count)

    barrier = pltpu.get_barrier_semaphore()
    for neighbour in (right, left):
        pl.semaphore_signal(
            barrier, inc=1, device_id={"zy": neighbour}, device_id_type=pl.DeviceIdType.MESH
        )
    other = {"tp": 1 - lax.axis_index("tp")}
    if swaps:
        pl.semaphore_signal(
            barrier, inc=1, device_id=other, device_id_type=pl.DeviceIdType.MESH
        )
    order = [half]
    for step in range(half - 1, 0, -1):
        order += [step, count - step]
    order.append(0)
    loads = {}
    for k in order:
        for i in range(arrays):
            loads[i, k] = pltpu.make_async_copy(
                terms_refs[i].at[ring_place(spot + k, count)], helds[i].at[k], load_sems.at[i, k]
            )
            loads[i, k].start()
    pl.semaphore_wait(barrier, 3 if swaps else 2)
    if swaps:
        swap = pltpu.make_async_remote_copy(
            src_ref=swap_ref,
            dst_ref=theirs_ref,
            send_sem=swap_send,
            recv_sem=swap_receive,
            device_id=other,
            device_id_type=pl.DeviceIdType.MESH,
        )
        swap.start()

    copies = {}

    def send(i, hop, way, source, target):
        copies[i, hop, way] = pltpu.make_async_remote_copy(
            src_ref=source,
            dst_ref=target,
            send_sem=send_sems.at[i, way, hop],
            recv_sem=receive_sems.at[i, way, hop],
            device_id={"zy": (right, left)[way]},
            device_id_type=pl.DeviceIdType.MESH,
        )
        copies[i, hop, way].start()

    def halves(i):
        cut = helds[i].shape[1] // 2
        return pl.ds(0, cut), pl.ds(cut, cut)

    for i in range(arrays):
        loads[i, half].wait()
        for way, arrived in enumerate((from_lefts[i], from_rights[i])):
            at = halves(i)[way]
            send(i, 0, way, helds[i].at[half, at], arrived.at[0, at])
    for hop in range(1, half):
        step = half - hop
        for i in range(arrays):
            for way, k in enumerate((step, count - step)):
                held, arrived = helds[i], (from_lefts[i], from_rights[i])[way]
                loads[i, k].wait()
                copies[i, hop - 1, way].wait_recv()
                at = halves(i)[way] if hop == 1 else slice(None)
                held[k, at, :] = (
                    held[k, at, :].astype(F32) + arrived[hop - 1, at, :].astype(F32)
                ).astype(BF16)
                send(i, hop, way, held.at[k], arrived.at[hop])
    for i in range(arrays):
        loads[i, 0].wait()
        for way in range(2):
            copies[i, half - 1, way].wait_recv()
        out_refs[i][...] = (
            helds[i][0].astype(F32)
            + from_lefts[i][half - 1].astype(F32)
            + from_rights[i][half - 1].astype(F32)
        )
    for copy in copies.values():
        copy.wait_send()
    if swaps:
        swap.wait()


def ring_sum(terms, collective_id, swap=None):
    arrays, count = len(terms), terms[0].shape[0]
    half = count // 2
    swaps = swap is not None
    anywhere = pl.BlockSpec(memory_space=pl.ANY)
    shapes = [term.shape[1:] for term in terms]
    return pl.pallas_call(
        functools.partial(ring_sum_kernel, count, arrays, swaps),
        in_specs=[anywhere] * (arrays + swaps),
        out_specs=[pl.BlockSpec(memory_space=pltpu.VMEM)] * arrays + [anywhere] * swaps,
        out_shape=[jax.ShapeDtypeStruct(shape, F32) for shape in shapes]
        + ([jax.ShapeDtypeStruct(swap.shape, swap.dtype)] if swaps else []),
        scratch_shapes=[pltpu.VMEM((count, *shape), BF16) for shape in shapes]
        + [pltpu.VMEM((half, *shape), BF16) for shape in shapes + shapes]
        + [
            pltpu.SemaphoreType.DMA((arrays, count)),
            pltpu.SemaphoreType.DMA((arrays, 2, half)),
            pltpu.SemaphoreType.DMA((arrays, 2, half)),
        ]
        + [pltpu.SemaphoreType.DMA] * (2 * swaps),
        compiler_params=pltpu.CompilerParams(
            collective_id=collective_id, has_side_effects=True, vmem_limit_bytes=48 * 2**20
        ),
        cost_estimate=SMALL,
        name="ring_sum",
    )(*terms, *([swap] if swaps else []))


def shards(
    layer_in,
    out_grad,
    parents,
    seg_len,
    attn_gain,
    w_query,
    key_weight,
    value_weight,
    w_out,
    ffn_gain,
    w_gate,
    w_up,
    w_down,
):
    trees, rows, width = layer_in.shape
    ring = Ring()
    chips = ring.count
    here, core = lax.axis_index("zy"), lax.axis_index("core")
    chip_rows = 2 * rows
    keys = chips * chip_rows
    groups = KEY_VALUE_HEADS // (2 * lax.axis_size("tp"))
    rep = QUERY_HEADS // KEY_VALUE_HEADS
    heads = groups * rep
    head_cols, kv_cols = heads * HEAD_SIZE, groups * HEAD_SIZE
    block = math.gcd(rows, 256)
    per_half = rows // block
    query_blocks, key_blocks = chip_rows // block, keys // block

    def column_piece(weight):
        keep, give = split_by_core(weight, 1)
        return by_core(keep, other_core(give), 0)

    def row_piece(weight):
        keep, give = split_by_core(weight, 0)
        return by_core(keep.T, other_core(give).T, 0)

    def column_grad(total):
        keep, give = split_by_core(total, 0)
        return by_core(keep, other_core(give), 1)

    def row_grad(total):
        keep, give = split_by_core(total, 0)
        return by_core(keep, other_core(give), 1).T

    def interleave(keys, values):
        parts = []
        for group in range(groups):
            at = slice(group * HEAD_SIZE, (group + 1) * HEAD_SIZE)
            parts += [keys[:, at], values[:, at]]
        return parts

    kv_pieces = interleave(column_piece(key_weight), column_piece(value_weight))
    gains = jnp.pad(jnp.stack([attn_gain, ffn_gain], axis=1), ((0, 0), (0, 126)))
    gain_piece = by_core(gains, other_core(gains), 0)
    qkv_piece = jnp.concatenate(
        [column_piece(w_query)] + kv_pieces + [gain_piece, row_piece(w_out)], axis=1
    )
    qkv_ring = Gather(ring, [qkv_piece], True)
    (first_in,) = after_all((layer_in,), (qkv_piece,))
    other_in = other_core(first_in)
    hops = [qkv_ring.hop()]
    w_gate, w_up, w_down = after_all((w_gate, w_up, w_down), hops[0])
    down_piece = row_piece(w_down)
    units_piece = unwritten(w_gate, (width // chips, w_gate.shape[1]))
    for at, piece in enumerate((column_piece(w_gate), column_piece(w_up))):
        units_piece = lax.dynamic_update_slice(units_piece, piece, (0, at * piece.shape[1]))
    while qkv_ring.step < chips // 2 - 1:
        hops.append(qkv_ring.hop())
    down_ring = Gather(ring, [down_piece])
    hops.append(qkv_ring.hop(down_piece))
    down_hop = down_ring.hop(*hops[-1])
    (w_attn,) = qkv_ring.finish()
    w_attn = w_attn.reshape(width, -1)
    w_qkv, gain_all, w_o = jnp.split(
        w_attn, [head_cols + 2 * kv_cols, head_cols + 2 * kv_cols + 128], axis=1
    )
    gain_all = gain_all.T[:2].astype(F32)
    gain_a, gain_f = gain_all[0], gain_all[1]

    def token_order(chip):
        first = (chip * 2 + core) * rows
        second = (chip * 2 + 1 - core) * rows
        steps = jnp.arange(rows, dtype=jnp.int32)
        return jnp.concatenate(
            [first[..., None] + steps, second[..., None] + steps], axis=-1
        ).reshape(-1)

    own_tokens = token_order(here)
    key_tokens = token_order(jnp.arange(chips, dtype=jnp.int32))
    own_block = own_tokens[::block] // block
    key_block = key_tokens[::block] // block
    diagonals = here * query_blocks + jnp.arange(query_blocks, dtype=jnp.int32)
    labels = jnp.arange(16, dtype=jnp.int32)
    tables, positions, masks, seens = [], [], [], []
    for tree in range(trees):
        row = after_all((parents[tree], seg_len[tree]), hops[min(tree, len(hops) - 1)])
        reaches, starts_at, ends_at, before = tree_tables(*row)
        seg_count = ends_at.shape[0]
        extra = 16 - seg_count
        reach16 = jnp.pad(reaches, ((0, extra), (0, extra)))
        starts16 = jnp.pad(starts_at, (0, extra))
        before16 = jnp.pad(before, (0, extra))
        ends16 = jnp.pad(ends_at, (0, extra), constant_values=2**30)
        own_seg = jnp.sum((own_tokens[:, None] >= ends_at[None, :]).astype(jnp.int32), axis=1)
        key_seg = jnp.sum((key_tokens[:, None] >= ends_at[None, :]).astype(jnp.int32), axis=1)
        member = own_seg[None, :] == labels[:, None]
        positions.append(
            own_tokens + jnp.sum(jnp.where(member, (before16 - starts16)[:, None], 0), axis=0)
        )
        seen_by = jnp.sum(
            jnp.where(member[:, None, :], reach16.astype(jnp.int32)[:, :, None], 0), axis=0
        )
        masks.append(jnp.where(seen_by > 0, 0.0, NEG).astype(BF16))
        lanes = jnp.arange(128, dtype=jnp.int32)
        key_seg_all = jnp.concatenate([key_seg, jnp.full((block,), seg_count, jnp.int32)])
        hot = (lanes[None, :] == key_seg_all[:, None]) | ((lanes >= 16) & (lanes < 19))[None, :]
        hot = hot.astype(BF16)

        def holds(blocks):
            low = blocks[:, None] * block
            return ((starts_at[None, :] < low + block) & (ends_at[None, :] > low)).astype(F32)

        linked = dot(dot(holds(own_block), reaches.astype(F32)), holds(key_block), 1, 1) > 0.5
        seen = linked & (key_block[None, :] < own_block[:, None])
        rank = jnp.cumsum(seen.astype(jnp.int32), axis=1) - 1
        slots = jnp.arange(key_blocks + 2, dtype=jnp.int32)
        index = jnp.arange(key_blocks, dtype=jnp.int32)
        chosen = seen[:, :, None] & (rank[:, :, None] == slots[None, None, :])
        lists = key_blocks + jnp.sum(
            jnp.where(chosen, index[None, :, None] - key_blocks, 0), axis=1
        )
        counts = jnp.sum(seen.astype(jnp.int32), axis=1)
        tables.append((counts, lists, diagonals, hot))
        on_diagonal = index[None, :] == diagonals[:, None]
        seens.append(jnp.where(on_diagonal, 2, seen.astype(jnp.int32)))
    position = jnp.concatenate(positions)
    (position,) = after_all((position,), hops[-2])
    angles = rope_angles(position, HEAD_SIZE)
    cosine, sine = jnp.cos(angles), jnp.sin(angles)

    inner_a, query, key_value = project(
        first_in, other_in, gain_a[None], w_attn, cosine, sine, head_cols, 2 * kv_cols,
        math.gcd(rows, 256),
    )
    query, key_value = after_all((query, key_value), down_hop)
    kv_rings = [
        Gather(ring, [key_value[tree * chip_rows : (tree + 1) * chip_rows]], True)
        for tree in range(trees)
    ]
    (out_grad,) = after_all((out_grad,), (key_value,))
    other_grad = other_core(out_grad)
    while kv_rings[0].step < chips // 2:
        mark, kv_hop = kv_hop if kv_rings[0].step else None, kv_rings[0].hop()
    kv_hop = kv_rings[1].hop(*mark)
    units_ring = Gather(ring, [units_piece])
    units_hop = units_ring.hop(*kv_rings[0].rightward, *kv_rings[0].leftward) + kv_hop
    kvs = [kv_rings[0].finish()[0].reshape(chips, 1, chip_rows, 2 * kv_cols)]

    def core_sum(own, other):
        return own.astype(F32) + other_core(other.astype(BF16)).astype(F32)

    def laid(buffer, value, tree):
        return lax.dynamic_update_slice(buffer, value[None], (tree, 0, 0))

    mixes, lses, middles, inners, normeds_f, scales_f, lows = [], [], [], [], [], [], []
    for tree in range(trees):
        mixed, lse = attend(tree, tables[tree], query, masks[tree], kvs[tree], rep, block)
        (mixed,) = after_all((mixed,), units_hop)
        part_hop = ()
        if tree == 0:
            while kv_rings[1].step < chips // 2 - 1:
                kv_hop = kv_rings[1].hop(mixed)
            last_hop = kv_rings[1].hop()
            down_hop = down_ring.hop(*kv_hop)
            units_hop = units_ring.hop(*last_hop)
        else:
            units_ring.hop(mixed)
            part_hop = down_hop
        mixes.append(mixed)
        lses.append(lse)
        (part,) = after_all((dot(mixed, w_o, 0, 1),), part_hop)
        lows.append(core_sum(part[:rows], part[rows:]).astype(BF16))
        if tree == 0:
            arrived = other_half(lows[0])
            units_hop += (arrived,)
            (query,) = after_all((query,), lows)
            kvs.append(kv_rings[1].finish()[0].reshape(chips, 1, chip_rows, 2 * kv_cols))
    arrived = [after_all((arrived,), lows[1:])[0]] + [other_half(low) for low in lows[1:]]
    layer_in, out_grad, position = after_all((layer_in, out_grad, position), lows)
    scale_a = row_scale_of(layer_in.astype(F32))
    grad_low = jnp.concatenate([out_grad, other_grad], axis=1).reshape(trees * chip_rows, width)
    cosine_rows, sine_rows = (
        table(rope_angles(position, HEAD_SIZE)).T[:, None, :] for table in (jnp.cos, jnp.sin)
    )
    for tree in range(trees):
        rows_in = layer_in[tree].astype(F32)
        middle = rows_in + (lows[tree].astype(F32) + arrived[tree].astype(F32))
        scale_f = row_scale_of(middle)
        normed_f = middle * scale_f
        inner = (normed_f * gain_f).astype(BF16)
        inners += [inner, other_core(inner)]
        middles.append(middle)
        scales_f.append(scale_f)
        normeds_f.append(normed_f)
    inner_f = jnp.concatenate(inners, axis=0)

    (w_units,) = units_ring.finish(*arrived[1:], grad_low, cosine_rows, sine_rows, scale_a)
    w_units = w_units.reshape(width, -1)
    down_hop = ()
    while down_ring.step < chips // 2 - 1:
        down_hop += down_ring.hop(*arrived[1:])
    hidden, gate_slope, activated = after_all(hidden_units(inner_f, w_units), down_hop)
    down_hop = down_ring.hop(hidden)
    down_terms, grad_low = after_all((unit_grads(grad_low, hidden), grad_low), down_hop)
    (w_d,) = down_ring.finish()
    w_d = w_d.reshape(width, -1)
    (grad_low,) = after_all((grad_low,), (down_terms,))
    grad_gate, grad_up = back_hidden(grad_low, w_d, gate_slope, activated)

    def pieces(term):
        return term.astype(BF16).reshape(chips, width // chips, -1)

    spans = [slice(tree * chip_rows, (tree + 1) * chip_rows) for tree in range(trees)]
    down_ring = Reduce(ring, [pieces(down_terms)])
    down_hop = down_ring.hop()
    core_sums = []
    (grad_gate,) = after_all((grad_gate,), (down_ring.terms[0],))
    for tree in range(trees):
        part = back_units(tree, chip_rows, [grad_gate, grad_up], w_units, [0, 1])
        part = after_all(part, down_hop)
        down_hop = down_ring.hop(part[0])
        (grad_gate,) = after_all((grad_gate,), part)
        core_sums.append(core_sum(*part))
    lows = unit_lows = [own.astype(BF16) for own in core_sums]
    arrived = [other_half(lows[0])]
    inner_f, hidden = after_all((inner_f, hidden), lows)
    units_terms = unit_grads(inner_f, grad_gate, grad_up)
    units_terms, arrived[0] = after_all((units_terms, arrived[0]), down_hop)
    arrived.append(other_half(after_all(lows[1:], arrived)[0]))
    units_ring = Reduce(ring, [pieces(units_terms)])
    units_hop = units_ring.hop() + down_ring.hop(units_terms)
    arrived[0] = after_all(arrived[:1], (units_terms,))[0]

    grads_middle, grads_low = [], []

    def backward_norm(tree):
        grad_inner = lows[tree].astype(F32) + arrived[tree].astype(F32)
        grad_middle = out_grad[tree].astype(F32) + norm_back(
            grad_inner * gain_f, normeds_f[tree], scales_f[tree]
        )
        low = grad_middle.astype(BF16)
        grads_middle.append(grad_middle)
        grads_low.append(low)
        return jnp.concatenate([low, other_core(low)], axis=0)

    mid_lows, out_lows, out_arrived = [backward_norm(0)], [], []
    grads_qkv = []

    def back_part(tree, kv_sums):
        rows_of = (cosine_rows[spans[tree]], -sine_rows[spans[tree]])
        parts = grad_queries[groups * tree : groups * (tree + 1)]
        for group in range(groups):
            kv_sum = kv_sums[:, 128 * group : 128 * (group + 1)]
            grad_k = kv_sum[:, None, :HEAD_SIZE]
            half = HEAD_SIZE // 2
            first, second = turn(grad_k[..., :half], grad_k[..., half:], *rows_of)
            kv_parts = [first[:, 0], second[:, 0], kv_sum[:, HEAD_SIZE:]]
            parts.append(jnp.concatenate(kv_parts, axis=1).astype(BF16))
        grad_qkv = jnp.concatenate(parts, axis=1)
        grads_qkv.append(grad_qkv)
        part = dot(grad_qkv, w_qkv, 1, 1)
        return core_sum(part[:rows], part[rows:]).astype(BF16)

    grad_queries, grad_kvs = [], []
    for tree in range(trees):
        grad_mixed = dot(w_o, mid_lows[tree], 0, 1).astype(BF16)
        for group in range(groups):
            grad_query, grad_kv = attend_back(
                tree,
                group,
                seens[tree],
                tables[tree][3],
                query,
                masks[tree],
                mixes[tree],
                grad_mixed,
                lses[tree],
                kvs[tree],
                cosine,
                sine,
                rep,
                block,
                grad_kvs[-1] if group else None,
            )
            grad_query, grad_kv = after_all((grad_query, grad_kv), units_hop)
            grad_queries.append(grad_query)
            grad_kvs.append(grad_kv)
            units_hop = ()
            if units_ring.left > 0 and group < groups - 1:
                units_hop = units_ring.hop(grad_query)
            (grad_mixed,) = after_all((grad_mixed,), (grad_query,))
            if tree == 0 and group == 0:
                (hidden,) = after_all((hidden,), (grad_query,))
                out_parts = [
                    back_units(tree, chip_rows, [hidden], w_d, [0]) for tree in range(trees)
                ]
                out_parts[0] = after_all(out_parts[0], arrived[1:])
                out_lows = [core_sum(*part).astype(BF16) for part in out_parts]
                (grad_mixed,) = after_all((grad_mixed,), out_lows)
                out_arrived.append(other_half(out_lows[0]))
                units_hop += tuple(out_arrived)
            elif tree and group < groups - 1:
                while kv_ring.left > 0:
                    units_hop += kv_ring.hop(grad_query)
        if tree == 0:
            kv_ring = Reduce(ring, grad_kvs[-1:])
            kv_ring.hop()
            arrived[-1] = after_all(arrived[-1:], (grad_query,))[0]
            mid_lows.append(backward_norm(1))
            kv_hop = kv_ring.hop()
            out_terms = pieces(
                dot(jnp.concatenate(mid_lows, axis=0), jnp.concatenate(mixes, axis=1), 0, 1)
            )
            mid_lows[1] = after_all(mid_lows[1:], (out_terms, *kv_hop))[0]
            out_arrived.append(other_half(after_all(out_lows[1:], (grad_query,))[0]))
            units_hop += units_ring.hop(*kv_hop) + kv_ring.hop(out_terms)
            units_hop += tuple(out_arrived[1:])
    out_arrived = after_all(out_arrived, (grad_queries[-1],))
    (down_sum,), (units_sum,) = down_ring.finish(), units_ring.finish()
    outputs = unwritten(out_terms, (trees, rows, width))
    out_arrived = after_all(out_arrived, (grad_queries[-1],))
    for tree in range(trees):
        summed = out_lows[tree].astype(F32) + out_arrived[tree].astype(F32)
        outputs = laid(outputs, (middles[tree] + summed).astype(BF16), tree)

    (layer_in,) = after_all((layer_in,), (grad_queries[-1],))

    def normed_rows(tree, *others):
        return after_all((layer_in,), others)[0][tree].astype(F32) * scale_a[tree]

    down_grad = row_grad(down_sum)
    lows = [back_part(0, kv_ring.finish()[0])]
    arrived = [other_half(lows[0])]
    (kv_terms,) = after_all(grad_kvs[-1:], lows)
    (kv_sums,) = after_all(ring_sum([kv_terms], 1), arrived)
    lows.append(back_part(1, kv_sums))
    (inner_a,) = after_all((inner_a,), (grads_qkv[-1],))
    gate_grad, up_grad = (
        column_grad(part) for part in jnp.split(units_sum, 2, axis=1)
    )
    gain_terms = jnp.stack(
        [
            sum(jnp.sum(low * normed_rows(i, lows[0]), axis=0) for i, low in enumerate(lows)),
            sum(jnp.sum(low * normeds_f[i], axis=0) for i, low in enumerate(unit_lows)),
        ]
    )
    gain_terms = jnp.moveaxis(gain_terms.astype(BF16).reshape(2, chips, width // chips), 1, 0)
    gain_terms = jnp.pad(gain_terms, ((0, 0), (0, 30), (0, 0)))
    term_qkv = unit_grads(inner_a, jnp.concatenate(grads_qkv, axis=0))
    qkv_sum, out_sum, gain_sums, theirs = ring_sum(
        [pieces(term_qkv), out_terms, gain_terms], 2, lows[1]
    )
    arrived.append(theirs)
    out_proj_grad = row_grad(out_sum)
    kv_parts = qkv_sum[:, head_cols:].reshape(-1, groups, 2, HEAD_SIZE)
    key_sum, value_sum = (kv_parts[:, :, i].reshape(-1, kv_cols) for i in range(2))

    keep, give = split_by_core(gain_sums[:8], 1)
    gain_sums = keep + other_core(give)
    gain_sums = gain_sums + other_half(gain_sums)
    gain_a_grad, gain_f_grad = gain_sums[0], gain_sums[1]
    input_grad = unwritten(scale_a, (trees, rows, width))
    for tree in range(trees):
        grad_inner = lows[tree].astype(F32) + arrived[tree].astype(F32)
        normed_a = normed_rows(tree, arrived[1])
        input_grad = laid(
            input_grad,
            grads_middle[tree] + norm_back(grad_inner * gain_a, normed_a, scale_a[tree]),
            tree,
        )

    return (
        outputs,
        input_grad,
        gain_a_grad,
        column_grad(qkv_sum[:, :head_cols]),
        column_grad(key_sum),
        column_grad(value_sum),
        out_proj_grad,
        gain_f_grad,
        gate_grad,
        up_grad,
        down_grad,
    )


def solution(mesh):
    devices = mesh.devices
    mesh = Mesh(devices.reshape(-1, 2, devices.shape[1]), ("zy", "core", "tp"))
    fsdp = ("zy", "core")
    specs = (
        P(fsdp),
        P(fsdp, "tp"),
        P(fsdp, "tp"),
        P(fsdp, "tp"),
        P("tp", fsdp),
        P(fsdp),
        P(fsdp, "tp"),
        P(fsdp, "tp"),
        P("tp", fsdp),
    )
    tokens = P(None, fsdp, None)
    return jax.shard_map(
        shards,
        mesh=mesh,
        in_specs=(tokens, tokens, P(), P()) + specs,
        out_specs=(tokens, tokens) + specs,
        check_vma=False,
    )
```

```python
import functools
import math

import jax
import jax.numpy as jnp
from jax import lax
from jax.experimental import pallas as pl
from jax.experimental.pallas import tpu as pltpu
from jax.sharding import Mesh
from jax.sharding import PartitionSpec as P

QUERY_HEADS = 32
KEY_VALUE_HEADS = 8
HEAD_SIZE = 64
LEVELS = 3

EPS = 1e-05
THETA = 500000.0
NEG = -1e30
LN2 = math.log(2.0)
SWAP = [(0, 1), (1, 0)]
F32 = jnp.float32
BF16 = jnp.bfloat16
SMALL = pl.CostEstimate(flops=2**20, bytes_accessed=2**10, transcendentals=0)


def dot(left, right, left_dim=1, right_dim=0):
    return lax.dot_general(
        left, right, (((left_dim,), (right_dim,)), ((), ())), preferred_element_type=F32
    )


def row_scale_of(rows_in):
    return lax.rsqrt(jnp.mean(rows_in * rows_in, axis=-1, keepdims=True) + EPS)


def norm_back(grad_normed, normed, row_scale):
    return row_scale * (
        grad_normed - normed * jnp.mean(grad_normed * normed, axis=-1, keepdims=True)
    )


def rope_angles(position, head_dim):
    half_dim = head_dim // 2
    index_row = jnp.arange(half_dim, dtype=F32)
    inverse = THETA ** (-2.0 * index_row / head_dim)
    wavelen = 2.0 * math.pi / inverse
    smooth = jnp.clip((8192.0 / wavelen - 1.0) / 3.0, 0.0, 1.0)
    inverse = (1.0 - smooth) * inverse / 32.0 + smooth * inverse
    return inverse[:, None] * position.astype(F32)[None, :]


def turn(first_half, second_half, cosine, sine):
    return first_half * cosine - second_half * sine, second_half * cosine + first_half * sine


def tree_tables(parents_row, lengths):
    seg_count = parents_row.shape[0]
    labels = jnp.arange(seg_count, dtype=jnp.int32)
    ends_at = jnp.cumsum(lengths)
    starts_at = ends_at - lengths
    reaches = labels[:, None] == labels[None, :]
    climber = labels
    for _ in range(LEVELS - 1):
        climber = jnp.sum(
            jnp.where(climber[:, None] == labels[None, :], parents_row[None, :], 0), axis=1
        )
        reaches = reaches | (climber[:, None] == labels[None, :])
    before = jnp.sum(
        jnp.where(reaches & (labels[:, None] != labels[None, :]), lengths[None, :], 0), axis=1
    )
    return reaches, starts_at, ends_at, before


def after_all(values, others):
    if not others:
        return list(values)
    return list(lax.optimization_barrier(tuple(values) + tuple(others))[: len(values)])


def unwritten(like, shape):
    return pl.pallas_call(
        lambda like_ref, out_ref: None,
        in_specs=[pl.BlockSpec(memory_space=pl.ANY)],
        out_specs=pl.BlockSpec(memory_space=pl.ANY),
        out_shape=jax.ShapeDtypeStruct(shape, like.dtype),
        name="buffer",
    )(like)


class Ring:
    def __init__(self):
        self.count = lax.axis_size("zy")
        count = self.count
        place = [2 * i if i < count // 2 else 2 * (count - 1 - i) + 1 for i in range(count)]
        self.right = [(place[i], place[(i + 1) % count]) for i in range(count)]
        self.left = [(b, a) for a, b in self.right]
        me = lax.axis_index("zy")
        self.spot = jnp.where(me % 2 == 0, me // 2, count - 1 - me // 2)

    def chip(self, offset):
        spot = lax.rem(self.spot + offset + self.count, self.count)
        return jnp.where(spot < self.count // 2, 2 * spot, 2 * (self.count - 1 - spot) + 1)

    def go_right(self, value):
        return lax.ppermute(value, "zy", self.right)

    def go_left(self, value):
        return lax.ppermute(value, "zy", self.left)

    def put(self, whole, part, offset, row=0):
        at = (self.chip(offset), row) + (0,) * (part.ndim - 1)
        return lax.dynamic_update_slice(whole, part[None], at)


class Gather:
    def __init__(self, ring, pieces, tidy=False):
        self.ring, self.step, self.tidy, self.laid = ring, 0, tidy, ()
        self.cuts = [piece.shape[0] // 2 for piece in pieces]
        wholes = [unwritten(piece, (ring.count,) + piece.shape) for piece in pieces]
        self.wholes = [ring.put(whole, piece, 0) for whole, piece in zip(wholes, pieces)]
        self.rightward = self.leftward = list(pieces)

    def hop(self, *others):
        ring, count = self.ring, len(self.cuts)
        both = after_all(self.rightward + self.leftward, others + self.laid)
        rightward, leftward = both[:count], both[count:]
        self.step += 1
        self.laid = tuple(self.wholes) if self.tidy else ()
        far = self.step == ring.count // 2
        if far:
            rightward = [part[:cut] for part, cut in zip(rightward, self.cuts)]
            leftward = [part[cut:] for part, cut in zip(leftward, self.cuts)]
        rightward = [ring.go_right(part) for part in rightward]
        leftward = [ring.go_left(part) for part in leftward]
        for i, cut in enumerate(self.cuts):
            whole = ring.put(self.wholes[i], rightward[i], -self.step)
            self.wholes[i] = ring.put(whole, leftward[i], self.step, cut if far else 0)
        self.rightward, self.leftward = rightward, leftward
        return tuple(rightward) + tuple(leftward)

    def finish(self, *others):
        while self.step < self.ring.count // 2:
            self.hop(*others)
        return self.wholes


class Reduce:
    def __init__(self, ring, terms):
        self.ring, self.terms, self.left = ring, list(terms), ring.count // 2
        self.cuts = [term.shape[1] // 2 for term in terms]
        self.rightward = self.leftward = None

    def each(self, offset):
        chip = self.ring.chip(offset)
        return [lax.dynamic_index_in_dim(term, chip, 0, keepdims=False) for term in self.terms]

    def hop(self, *others):
        ring, step, count = self.ring, self.left, len(self.cuts)
        if self.rightward is None:
            far = self.each(step)
            rightward = [part[:cut] for part, cut in zip(far, self.cuts)]
            leftward = [part[cut:] for part, cut in zip(far, self.cuts)]
        else:
            rightward, leftward = list(self.rightward), list(self.leftward)
            mine, other = self.each(step), self.each(-step)
            if step == ring.count // 2 - 1:
                for i, cut in enumerate(self.cuts):
                    parts = [add_low(mine[i][:cut], rightward[i]), mine[i][cut:]]
                    rightward[i] = jnp.concatenate(parts, axis=0)
                    parts = [other[i][:cut], add_low(other[i][cut:], leftward[i])]
                    leftward[i] = jnp.concatenate(parts, axis=0)
            else:
                rightward = [add_low(one, part) for one, part in zip(mine, rightward)]
                leftward = [add_low(one, part) for one, part in zip(other, leftward)]
        both = after_all(rightward + leftward, others)
        rightward, leftward = both[:count], both[count:]
        self.rightward = [ring.go_right(part) for part in rightward]
        self.leftward = [ring.go_left(part) for part in leftward]
        self.left -= 1
        return tuple(self.rightward) + tuple(self.leftward)

    def finish(self, *others):
        while self.left > 0:
            self.hop(*others)
        return [
            mine.astype(F32) + one.astype(F32) + two.astype(F32)
            for mine, one, two in zip(self.each(0), self.rightward, self.leftward)
        ]


def add_low(left, right):
    return (left.astype(F32) + right.astype(F32)).astype(BF16)


def other_core(value):
    return lax.ppermute(value, "core", SWAP)


def other_half(value):
    return lax.ppermute(value, "tp", SWAP)


def by_core(own, other, axis):
    first = lax.axis_index("core") == 0
    return jnp.concatenate(
        [jnp.where(first, own, other), jnp.where(first, other, own)], axis=axis
    )


def split_by_core(value, axis):
    core = lax.axis_index("core")
    size = value.shape[axis] // 2
    return (
        lax.dynamic_slice_in_dim(value, core * size, size, axis),
        lax.dynamic_slice_in_dim(value, (1 - core) * size, size, axis),
    )


def split3(value):
    high = value.astype(BF16)
    rest = value - high.astype(F32)
    middle = rest.astype(BF16)
    low = (rest - middle.astype(F32)).astype(BF16)
    return high, middle, low


def causal(scores, block):
    key_at = lax.broadcasted_iota(jnp.int32, scores.shape, 0)
    query_at = lax.rem(lax.broadcasted_iota(jnp.int32, scores.shape, 1), block)
    return jnp.where(key_at <= query_at, scores, NEG)


def block_of(ref, index, block, per_piece):
    piece = lax.div(index, per_piece)
    start = pl.multiple_of(lax.rem(index, per_piece) * block, block)
    return ref[piece, 0, pl.ds(start, block), :]


def attend_kernel(
    block, rep, per_piece, count_ref, list_ref, diag_ref, query_ref, mask_ref, kv_ref, hot_ref,
    out_ref, lse_ref, query_aug, turned,
):
    at = pl.program_id(1)
    key_blocks = hot_ref.shape[0] // block - 1

    @pl.when(at == 0)
    def _():
        rows = per_piece * block
        for piece in range(kv_ref.shape[0]):
            turned[:, piece * rows : (piece + 1) * rows] = kv_ref[piece, 0].T

    query_aug[HEAD_SIZE:, :] = jnp.zeros_like(query_aug[HEAD_SIZE:, :])
    for r in range(rep):
        columns = slice(r * block, (r + 1) * block)
        query_aug[:HEAD_SIZE, columns] = query_ref[r * HEAD_SIZE : (r + 1) * HEAD_SIZE, :]
        query_aug[128:144, columns] = mask_ref[...]

    def scores_of(index):
        keys = block_of(kv_ref, jnp.minimum(index, key_blocks - 1), block, per_piece)
        hot = hot_ref[pl.ds(pl.multiple_of(index * block, block), block), :]
        return jnp.dot(
            jnp.concatenate([keys, hot], axis=1), query_aug[...], preferred_element_type=F32
        )

    def values_of(index):
        index = jnp.minimum(index, key_blocks - 1)
        return turned[HEAD_SIZE:, pl.ds(pl.multiple_of(index * block, block), block)]

    diagonal = diag_ref[at]
    scores = causal(scores_of(diagonal), block)
    top = jnp.max(scores, axis=0, keepdims=True)
    probs = jnp.exp2(scores - top)
    total = jnp.sum(probs, axis=0, keepdims=True)
    mixed = jnp.dot(values_of(diagonal), probs.astype(BF16), preferred_element_type=F32)

    def step(j, carry):
        top, total, mixed = carry
        one, two = list_ref[at, 2 * j], list_ref[at, 2 * j + 1]
        first, second = scores_of(one), scores_of(two)
        new = jnp.maximum(top, jnp.max(first, axis=0, keepdims=True))
        new = jnp.maximum(new, jnp.max(second, axis=0, keepdims=True))
        factor = jnp.exp2(top - new)
        first, second = jnp.exp2(first - new), jnp.exp2(second - new)
        total = (
            total * factor
            + jnp.sum(first, axis=0, keepdims=True)
            + jnp.sum(second, axis=0, keepdims=True)
        )
        values = jnp.concatenate([values_of(one), values_of(two)], axis=1)
        probs = jnp.concatenate([first.astype(BF16), second.astype(BF16)], axis=0)
        mixed = mixed * factor + jnp.dot(values, probs, preferred_element_type=F32)
        return new, total, mixed

    pairs = lax.div(count_ref[at] + 1, 2)
    top, total, mixed = lax.fori_loop(0, pairs, step, (top, total, mixed))
    mixed = mixed * (1.0 / total)
    lse = top + jnp.log2(total)
    for r in range(rep):
        columns = slice(r * block, (r + 1) * block)
        out_ref[r * HEAD_SIZE : (r + 1) * HEAD_SIZE, :] = mixed[:, columns].astype(BF16)
        lse_ref[0, r : r + 1, :] = lse[:, columns]


def attend(tree, tables, query, mask, kv, rep, block):
    counts, lists, diagonals, hot = tables
    heads = query.shape[0]
    pieces, _, rows, _ = kv.shape
    groups, query_blocks = heads // (rep * HEAD_SIZE), rows // block
    keys = pieces * rows
    grid_spec = pltpu.PrefetchScalarGridSpec(
        num_scalar_prefetch=3,
        grid=(groups, query_blocks),
        in_specs=[
            pl.BlockSpec(
                (rep * HEAD_SIZE, block), lambda g, q, *_: (g, tree * query_blocks + q)
            ),
            pl.BlockSpec((16, block), lambda g, q, *_: (0, q)),
            pl.BlockSpec((pieces, 1, rows, 128), lambda g, q, *_: (0, 0, 0, g)),
            pl.BlockSpec((keys + block, 128), lambda g, q, *_: (0, 0)),
        ],
        out_specs=[
            pl.BlockSpec((rep * HEAD_SIZE, block), lambda g, q, *_: (g, q)),
            pl.BlockSpec((1, rep, block), lambda g, q, *_: (g, 0, q)),
        ],
        scratch_shapes=[
            pltpu.VMEM((256, rep * block), BF16),
            pltpu.VMEM((128, keys), BF16),
        ],
    )
    return pl.pallas_call(
        functools.partial(attend_kernel, block, rep, rows // block),
        grid_spec=grid_spec,
        out_shape=[
            jax.ShapeDtypeStruct((heads, rows), BF16),
            jax.ShapeDtypeStruct((groups, rep, rows), F32),
        ],
        compiler_params=pltpu.CompilerParams(vmem_limit_bytes=48 * 2**20),
        cost_estimate=SMALL,
        name="tree_attention",
    )(counts, lists, diagonals, query, mask, kv, hot)


def attend_back_kernel(
    block, rep, per_piece, seen_ref, query_ref, mask_ref, mixed_ref, grad_ref, lse_ref, kv_ref,
    hot_ref, cosine_ref, sine_ref, before_ref, grad_query_ref, grad_kv_ref, augs, turned_rows,
    key_turned, grad_query, grad_kv,
):
    rows = per_piece * block
    query_blocks = rows // block
    key_blocks = kv_ref.shape[0] * per_piece
    width = rep * block

    for piece in range(kv_ref.shape[0]):
        key_turned[:, piece * rows : (piece + 1) * rows] = kv_ref[piece, 0].T
    grad_kv[...] = jnp.zeros_like(grad_kv)
    grad_query[...] = jnp.zeros_like(grad_query)
    augs[...] = jnp.zeros_like(augs)
    none = jnp.zeros((HEAD_SIZE, block), BF16)
    for at in range(query_blocks):
        columns = slice(at * block, (at + 1) * block)
        for r in range(rep):
            here = slice(2 * at * width + r * block, 2 * at * width + (r + 1) * block)
            there = slice((2 * at + 1) * width + r * block, (2 * at + 1) * width + (r + 1) * block)
            head = slice(r * HEAD_SIZE, (r + 1) * HEAD_SIZE)
            query, grad = query_ref[head, columns], grad_ref[head, columns]
            augs[:HEAD_SIZE, here] = query
            augs[HEAD_SIZE : 2 * HEAD_SIZE, there] = grad
            delta = jnp.sum(
                grad.astype(F32) * mixed_ref[head, columns].astype(F32), axis=0, keepdims=True
            )
            empty = jnp.zeros((13, block), BF16)
            augs[128:160, here] = jnp.concatenate(
                [mask_ref[:, columns], *split3(-lse_ref[0, r : r + 1, columns]), empty], axis=0
            )
            augs[128:160, there] = jnp.concatenate(
                [jnp.zeros((16, block), BF16), *split3(-delta), empty], axis=0
            )
            turned_rows[here, :] = jnp.concatenate([none, grad], axis=0).T
            turned_rows[there, :] = jnp.concatenate([query, none], axis=0).T

    def over_keys(index, _):
        rows_at = pl.ds(pl.multiple_of(index * block, block), block)
        for at in range(query_blocks):
            columns = slice(2 * at * width, (2 * at + 2) * width)

            def work(on_diagonal):
                both = jnp.dot(
                    jnp.concatenate(
                        [block_of(kv_ref, index, block, per_piece), hot_ref[rows_at, :]], axis=1
                    ),
                    augs[:, columns],
                    preferred_element_type=F32,
                )
                scores, grad_probs = both[:, :width], both[:, width:]
                if on_diagonal:
                    scores = causal(scores, block)
                probs = jnp.exp2(scores)
                grad_scores = (probs * grad_probs).astype(BF16)
                grad_kv[rows_at, :] += jnp.dot(
                    jnp.concatenate([probs.astype(BF16), grad_scores], axis=1),
                    turned_rows[columns, :],
                    preferred_element_type=F32,
                )
                grad_query[:, at * width : (at + 1) * width] += jnp.dot(
                    key_turned[:HEAD_SIZE, rows_at], grad_scores, preferred_element_type=F32
                )

            seen = seen_ref[at, index]
            pl.when(seen == 1)(functools.partial(work, False))
            pl.when(seen == 2)(functools.partial(work, True))
        return 0

    lax.fori_loop(0, key_blocks, over_keys, 0)
    for at in range(query_blocks):
        columns = slice(at * block, (at + 1) * block)
        cosine = cosine_ref[:, columns] * HEAD_SIZE**-0.5
        sine = -sine_ref[:, columns] * HEAD_SIZE**-0.5
        for r in range(0, rep, 2):
            parts = []
            for head in (r, r + 1):
                here = slice(at * width + head * block, at * width + (head + 1) * block)
                grad = grad_query[:, here]
                half = HEAD_SIZE // 2
                parts += turn(grad[:half], grad[half:], cosine, sine)
            grad_query_ref[columns, r * HEAD_SIZE : (r + 2) * HEAD_SIZE] = (
                jnp.concatenate(parts, axis=0).T.astype(BF16)
            )
    for piece in range(kv_ref.shape[0]):
        grads = grad_kv[piece * rows : (piece + 1) * rows, :]
        lanes = lax.broadcasted_iota(jnp.int32, grads.shape, 1)
        grad_kv_ref[piece] = jnp.where(lanes < HEAD_SIZE, grads * LN2, grads).astype(BF16)


def attend_back(
    tree, group, seen, hot, query, mask, mixed, grad, lse, kv, cosine, sine, rep, block, before
):
    pieces, _, rows, _ = kv.shape
    keys = pieces * rows
    heads = rep * HEAD_SIZE
    head = pl.BlockSpec((heads, rows), lambda i, *_: (group, 0))
    table = pl.BlockSpec((HEAD_SIZE // 2, rows), lambda i, *_: (0, tree))
    grid_spec = pltpu.PrefetchScalarGridSpec(
        num_scalar_prefetch=1,
        grid=(1,),
        in_specs=[
            pl.BlockSpec((heads, rows), lambda i, *_: (group, tree)),
            pl.BlockSpec((16, rows), lambda i, *_: (0, 0)),
            head,
            head,
            pl.BlockSpec((1, rep, rows), lambda i, *_: (group, 0, 0)),
            pl.BlockSpec((pieces, 1, rows, 128), lambda i, *_: (0, 0, 0, group)),
            pl.BlockSpec((keys + block, 128), lambda i, *_: (0, 0)),
            table,
            table,
            pl.BlockSpec(memory_space=pl.ANY),
        ],
        out_specs=[
            pl.BlockSpec((rows, heads), lambda i, *_: (0, 0)),
            pl.BlockSpec((pieces, rows, 128), lambda i, *_: (0, 0, group)),
        ],
        scratch_shapes=[
            pltpu.VMEM((256, 2 * rep * rows), BF16),
            pltpu.VMEM((2 * rep * rows, 128), BF16),
            pltpu.VMEM((128, keys), BF16),
            pltpu.VMEM((HEAD_SIZE, rep * rows), F32),
            pltpu.VMEM((keys, 128), F32),
        ],
    )
    return pl.pallas_call(
        functools.partial(attend_back_kernel, block, rep, rows // block),
        grid_spec=grid_spec,
        out_shape=[
            jax.ShapeDtypeStruct((rows, heads), BF16),
            jax.ShapeDtypeStruct((pieces, rows, kv.shape[3]), BF16),
        ],
        input_output_aliases={10: 1} if group else {},
        compiler_params=pltpu.CompilerParams(vmem_limit_bytes=56 * 2**20),
        cost_estimate=SMALL,
        name="tree_attention_back",
    )(seen, query, mask, mixed, grad, lse, kv, hot, cosine, sine, cosine if before is None else before)


def project_kernel(
    heads, columns, own_ref, other_ref, gain_ref, weight_ref, cosine_ref, sine_ref, inner_ref, query_ref,
    kv_ref, rows,
):
    mine = lax.rem(pl.program_id(0), 2) == 0

    @pl.when(mine)
    def _():
        rows[...] = own_ref[0].astype(F32)

    @pl.when(jnp.logical_not(mine))
    def _():
        rows[...] = other_ref[0].astype(F32)

    x = rows[...]
    inner = (x * row_scale_of(x) * gain_ref[...]).astype(BF16)
    inner_ref[...] = inner
    made = jnp.dot(inner, weight_ref[:, :columns], preferred_element_type=F32)
    cosine, sine = cosine_ref[...], sine_ref[...]
    half = HEAD_SIZE // 2

    def turned(values):
        parts = []
        for start in range(0, values.shape[0], HEAD_SIZE):
            parts += turn(
                values[start : start + half], values[start + half : start + HEAD_SIZE], cosine, sine
            )
        return jnp.concatenate(parts, axis=0)

    query_ref[...] = (turned(made[:, :heads].T) * (HEAD_SIZE**-0.5 / LN2)).astype(BF16)
    kv = made[:, heads:].T
    parts = []
    for start in range(0, kv.shape[0], 128):
        parts += [turned(kv[start : start + HEAD_SIZE]), kv[start + HEAD_SIZE : start + 128]]
    kv_ref[...] = jnp.concatenate(parts, axis=0).T.astype(BF16)


def project(own, other, gain, weight, cosine, sine, heads, kv_columns, tile):
    trees, rows, width = own.shape
    tiles = rows // tile
    last = trees * tiles - 1

    def place(half):
        def index(t, j):
            tree, at = t // 2, t % 2
            same = at == half
            if half == 0:
                return (jnp.where(same, tree, tree), jnp.where(same, j, tiles - 1), 0)
            return (tree, jnp.where(same, j, 0), 0)

        return index

    flat = lambda t, j: (t * tiles + j, 0)
    lanes = lambda t, j: (0, t * tiles + j)
    tokens = 2 * trees * rows
    columns = heads + kv_columns
    return pl.pallas_call(
        functools.partial(project_kernel, heads, columns),
        grid=(2 * trees, tiles),
        in_specs=[
            pl.BlockSpec((1, tile, width), place(0)),
            pl.BlockSpec((1, tile, width), place(1)),
            pl.BlockSpec((1, width), lambda t, j: (0, 0)),
            pl.BlockSpec((width, columns), lambda t, j: (0, 0)),
            pl.BlockSpec((HEAD_SIZE // 2, tile), lanes),
            pl.BlockSpec((HEAD_SIZE // 2, tile), lanes),
        ],
        out_specs=[
            pl.BlockSpec((tile, width), flat),
            pl.BlockSpec((heads, tile), lanes),
            pl.BlockSpec((tile, columns - heads), flat),
        ],
        out_shape=[
            jax.ShapeDtypeStruct((tokens, width), BF16),
            jax.ShapeDtypeStruct((heads, tokens), BF16),
            jax.ShapeDtypeStruct((tokens, columns - heads), BF16),
        ],
        scratch_shapes=[pltpu.VMEM((tile, width), F32)],
        compiler_params=pltpu.CompilerParams(vmem_limit_bytes=48 * 2**20),
        cost_estimate=SMALL,
        name="project",
    )(own, other, gain, weight, cosine, sine)


def units_kernel(inner_ref, gate_ref, up_ref, hidden_ref, slope_ref, activated_ref):
    inner = inner_ref[...]
    gate = jnp.dot(inner, gate_ref[...], preferred_element_type=F32)
    up = jnp.dot(inner, up_ref[...], preferred_element_type=F32)
    sigmoid = jax.nn.sigmoid(gate)
    activated = gate * sigmoid
    hidden_ref[...] = (activated * up).astype(BF16)
    slope_ref[...] = (up * sigmoid * (1.0 + gate * (1.0 - sigmoid))).astype(BF16)
    activated_ref[...] = activated.astype(BF16)


def back_hidden_kernel(grad_ref, down_ref, slope_ref, activated_ref, grad_gate_ref, grad_up_ref):
    grad_hidden = jnp.dot(grad_ref[...], down_ref[...], preferred_element_type=F32)
    grad_gate_ref[...] = (grad_hidden * slope_ref[...].astype(F32)).astype(BF16)
    grad_up_ref[...] = (grad_hidden * activated_ref[...].astype(F32)).astype(BF16)


def over_units(kernel, rows_in, weights, firsts, units, tiles_in, made, name):
    tokens, width = rows_in.shape
    rows, columns = math.gcd(tokens, 2048 // len(firsts)), math.gcd(units, 512)
    tiles = units // columns
    tile = pl.BlockSpec((rows, columns), lambda j, i: (i, j))
    wide = [
        pl.BlockSpec((width, columns), lambda j, i, first=first: (0, first * tiles + j))
        for first in firsts
    ]
    return pl.pallas_call(
        kernel,
        grid=(tiles, tokens // rows),
        in_specs=[pl.BlockSpec((rows, width), lambda j, i: (i, 0)), *wide]
        + [tile] * len(tiles_in),
        out_specs=[tile] * made,
        out_shape=[jax.ShapeDtypeStruct((tokens, units), BF16)] * made,
        compiler_params=pltpu.CompilerParams(vmem_limit_bytes=56 * 2**20),
        cost_estimate=SMALL,
        name=name,
    )(rows_in, *([weights] * len(firsts)), *tiles_in)


def hidden_units(inner, weights):
    units = weights.shape[1] // 2
    return over_units(units_kernel, inner, weights, (0, 1), units, (), 3, "hidden_units")


def back_hidden(grad, down, slope, activated):
    units = down.shape[1]
    return over_units(
        back_hidden_kernel, grad, down, (0,), units, (slope, activated), 2, "back_hidden"
    )


def back_units_kernel(count, *refs):
    *refs, own_ref, other_ref = refs
    contract = (((1,), (1,)), ((), ()))
    total = None
    for units_ref, weight_ref in zip(refs[:count], refs[count:]):
        term = lax.dot_general(
            units_ref[...], weight_ref[...], contract, preferred_element_type=F32
        )
        total = term if total is None else total + term
    half = own_ref.shape[0]
    own_ref[...] = total[:half].astype(BF16)
    other_ref[...] = total[half:].astype(BF16)


def back_units(tree, tokens, units, weights, places):
    width, size = weights.shape[0], units[0].shape[1]
    columns = math.gcd(width, 512)
    tall = pl.BlockSpec((tokens, size), lambda j: (tree, 0))
    made = jax.ShapeDtypeStruct((tokens // 2, width), BF16)
    return pl.pallas_call(
        functools.partial(back_units_kernel, len(units)),
        grid=(width // columns,),
        in_specs=[tall] * len(units)
        + [pl.BlockSpec((columns, size), lambda j, at=at: (j, at)) for at in places],
        out_specs=[pl.BlockSpec((tokens // 2, columns), lambda j: (0, j))] * 2,
        out_shape=[made, made],
        compiler_params=pltpu.CompilerParams(vmem_limit_bytes=56 * 2**20),
        cost_estimate=SMALL,
        name="back_units",
    )(*units, *([weights] * len(units)))


def unit_grads_kernel(tiles, rows_ref, *refs):
    *grad_refs, out_ref, turned = refs
    at = pl.program_id(1)

    @pl.when(at == 0)
    def _():
        turned[...] = rows_ref[...].T

    for i, grad_ref in enumerate(grad_refs):

        @pl.when((at >= i * tiles) & (at < (i + 1) * tiles))
        def _():
            out_ref[...] = jnp.dot(
                turned[...], grad_ref[...], preferred_element_type=F32
            ).astype(BF16)


def unit_grads(rows_in, *grads):
    tokens, width = rows_in.shape
    units = grads[0].shape[1]
    rows, columns = math.gcd(width, 1024), math.gcd(units, 1024 // len(grads))
    tiles = units // columns

    def place(i):
        return lambda at, j: (0, jnp.clip(j - i * tiles, 0, tiles - 1))

    return pl.pallas_call(
        functools.partial(unit_grads_kernel, tiles),
        grid=(width // rows, tiles * len(grads)),
        in_specs=[pl.BlockSpec((tokens, rows), lambda i, j: (0, i))]
        + [pl.BlockSpec((tokens, columns), place(i)) for i in range(len(grads))],
        out_specs=pl.BlockSpec((rows, columns), lambda i, j: (i, j)),
        out_shape=jax.ShapeDtypeStruct((width, units * len(grads)), BF16),
        scratch_shapes=[pltpu.VMEM((rows, tokens), BF16)],
        compiler_params=pltpu.CompilerParams(vmem_limit_bytes=56 * 2**20),
        cost_estimate=SMALL,
        name="unit_grads",
    )(rows_in, *grads)


def ring_place(spot, count):
    spot = lax.rem(spot + count, count)
    return jnp.where(spot < count // 2, 2 * spot, 2 * (count - 1 - spot) + 1)


def ring_sum_kernel(count, arrays, swaps, *refs):
    terms_refs, refs = refs[:arrays], refs[arrays:]
    if swaps:
        swap_ref, *refs, swap_send, swap_receive = refs
    out_refs, refs = refs[:arrays], refs[arrays:]
    if swaps:
        theirs_ref, *refs = refs
    helds, from_lefts, from_rights = (refs[i * arrays : (i + 1) * arrays] for i in range(3))
    load_sems, send_sems, receive_sems = refs[3 * arrays :]
    half = count // 2
    me = lax.axis_index("zy")
    spot = jnp.where(lax.rem(me, 2) == 0, lax.div(me, 2), count - 1 - lax.div(me, 2))
    right, left = ring_place(spot + 1, count), ring_place(spot - 1, count)

    barrier = pltpu.get_barrier_semaphore()
    for neighbour in (right, left):
        pl.semaphore_signal(
            barrier, inc=1, device_id={"zy": neighbour}, device_id_type=pl.DeviceIdType.MESH
        )
    other = {"tp": 1 - lax.axis_index("tp")}
    if swaps:
        pl.semaphore_signal(
            barrier, inc=1, device_id=other, device_id_type=pl.DeviceIdType.MESH
        )
    order = [half]
    for step in range(half - 1, 0, -1):
        order += [step, count - step]
    order.append(0)
    loads = {}
    for k in order:
        for i in range(arrays):
            loads[i, k] = pltpu.make_async_copy(
                terms_refs[i].at[ring_place(spot + k, count)], helds[i].at[k], load_sems.at[i, k]
            )
            loads[i, k].start()
    pl.semaphore_wait(barrier, 3 if swaps else 2)
    if swaps:
        swap = pltpu.make_async_remote_copy(
            src_ref=swap_ref,
            dst_ref=theirs_ref,
            send_sem=swap_send,
            recv_sem=swap_receive,
            device_id=other,
            device_id_type=pl.DeviceIdType.MESH,
        )
        swap.start()

    copies = {}

    def send(i, hop, way, source, target):
        copies[i, hop, way] = pltpu.make_async_remote_copy(
            src_ref=source,
            dst_ref=target,
            send_sem=send_sems.at[i, way, hop],
            recv_sem=receive_sems.at[i, way, hop],
            device_id={"zy": (right, left)[way]},
            device_id_type=pl.DeviceIdType.MESH,
        )
        copies[i, hop, way].start()

    def halves(i):
        cut = helds[i].shape[1] // 2
        return pl.ds(0, cut), pl.ds(cut, cut)

    for i in range(arrays):
        loads[i, half].wait()
        for way, arrived in enumerate((from_lefts[i], from_rights[i])):
            at = halves(i)[way]
            send(i, 0, way, helds[i].at[half, at], arrived.at[0, at])
    for hop in range(1, half):
        step = half - hop
        for i in range(arrays):
            for way, k in enumerate((step, count - step)):
                held, arrived = helds[i], (from_lefts[i], from_rights[i])[way]
                loads[i, k].wait()
                copies[i, hop - 1, way].wait_recv()
                at = halves(i)[way] if hop == 1 else slice(None)
                held[k, at, :] = (
                    held[k, at, :].astype(F32) + arrived[hop - 1, at, :].astype(F32)
                ).astype(BF16)
                send(i, hop, way, held.at[k], arrived.at[hop])
    for i in range(arrays):
        loads[i, 0].wait()
        for way in range(2):
            copies[i, half - 1, way].wait_recv()
        out_refs[i][...] = (
            helds[i][0].astype(F32)
            + from_lefts[i][half - 1].astype(F32)
            + from_rights[i][half - 1].astype(F32)
        )
    for copy in copies.values():
        copy.wait_send()
    if swaps:
        swap.wait()


def ring_sum(terms, collective_id, swap=None):
    arrays, count = len(terms), terms[0].shape[0]
    half = count // 2
    swaps = swap is not None
    anywhere = pl.BlockSpec(memory_space=pl.ANY)
    shapes = [term.shape[1:] for term in terms]
    return pl.pallas_call(
        functools.partial(ring_sum_kernel, count, arrays, swaps),
        in_specs=[anywhere] * (arrays + swaps),
        out_specs=[pl.BlockSpec(memory_space=pltpu.VMEM)] * arrays + [anywhere] * swaps,
        out_shape=[jax.ShapeDtypeStruct(shape, F32) for shape in shapes]
        + ([jax.ShapeDtypeStruct(swap.shape, swap.dtype)] if swaps else []),
        scratch_shapes=[pltpu.VMEM((count, *shape), BF16) for shape in shapes]
        + [pltpu.VMEM((half, *shape), BF16) for shape in shapes + shapes]
        + [
            pltpu.SemaphoreType.DMA((arrays, count)),
            pltpu.SemaphoreType.DMA((arrays, 2, half)),
            pltpu.SemaphoreType.DMA((arrays, 2, half)),
        ]
        + [pltpu.SemaphoreType.DMA] * (2 * swaps),
        compiler_params=pltpu.CompilerParams(
            collective_id=collective_id, has_side_effects=True, vmem_limit_bytes=48 * 2**20
        ),
        cost_estimate=SMALL,
        name="ring_sum",
    )(*terms, *([swap] if swaps else []))


def shards(
    layer_in,
    out_grad,
    parents,
    seg_len,
    attn_gain,
    w_query,
    key_weight,
    value_weight,
    w_out,
    ffn_gain,
    w_gate,
    w_up,
    w_down,
):
    trees, rows, width = layer_in.shape
    ring = Ring()
    chips = ring.count
    here, core = lax.axis_index("zy"), lax.axis_index("core")
    chip_rows = 2 * rows
    keys = chips * chip_rows
    groups = KEY_VALUE_HEADS // (2 * lax.axis_size("tp"))
    rep = QUERY_HEADS // KEY_VALUE_HEADS
    heads = groups * rep
    head_cols, kv_cols = heads * HEAD_SIZE, groups * HEAD_SIZE
    block = math.gcd(rows, 256)
    per_half = rows // block
    query_blocks, key_blocks = chip_rows // block, keys // block

    def column_piece(weight):
        keep, give = split_by_core(weight, 1)
        return by_core(keep, other_core(give), 0)

    def row_piece(weight):
        keep, give = split_by_core(weight, 0)
        return by_core(keep.T, other_core(give).T, 0)

    def column_grad(total):
        keep, give = split_by_core(total, 0)
        return by_core(keep, other_core(give), 1)

    def row_grad(total):
        keep, give = split_by_core(total, 0)
        return by_core(keep, other_core(give), 1).T

    def interleave(keys, values):
        parts = []
        for group in range(groups):
            at = slice(group * HEAD_SIZE, (group + 1) * HEAD_SIZE)
            parts += [keys[:, at], values[:, at]]
        return parts

    kv_pieces = interleave(column_piece(key_weight), column_piece(value_weight))
    gains = jnp.pad(jnp.stack([attn_gain, ffn_gain], axis=1), ((0, 0), (0, 126)))
    gain_piece = by_core(gains, other_core(gains), 0)
    qkv_piece = jnp.concatenate(
        [column_piece(w_query)] + kv_pieces + [gain_piece, row_piece(w_out)], axis=1
    )
    qkv_ring = Gather(ring, [qkv_piece], True)
    (first_in,) = after_all((layer_in,), (qkv_piece,))
    other_in = other_core(first_in)
    hops = [qkv_ring.hop()]
    w_gate, w_up, w_down = after_all((w_gate, w_up, w_down), hops[0])
    down_piece = row_piece(w_down)
    units_piece = unwritten(w_gate, (width // chips, w_gate.shape[1]))
    for at, piece in enumerate((column_piece(w_gate), column_piece(w_up))):
        units_piece = lax.dynamic_update_slice(units_piece, piece, (0, at * piece.shape[1]))
    while qkv_ring.step < chips // 2 - 1:
        hops.append(qkv_ring.hop())
    down_ring = Gather(ring, [down_piece])
    hops.append(qkv_ring.hop(down_piece))
    down_hop = down_ring.hop(*hops[-1])
    (w_attn,) = qkv_ring.finish()
    w_attn = w_attn.reshape(width, -1)
    w_qkv, gain_all, w_o = jnp.split(
        w_attn, [head_cols + 2 * kv_cols, head_cols + 2 * kv_cols + 128], axis=1
    )
    gain_all = gain_all.T[:2].astype(F32)
    gain_a, gain_f = gain_all[0], gain_all[1]

    def token_order(chip):
        first = (chip * 2 + core) * rows
        second = (chip * 2 + 1 - core) * rows
        steps = jnp.arange(rows, dtype=jnp.int32)
        return jnp.concatenate(
            [first[..., None] + steps, second[..., None] + steps], axis=-1
        ).reshape(-1)

    own_tokens = token_order(here)
    key_tokens = token_order(jnp.arange(chips, dtype=jnp.int32))
    own_block = own_tokens[::block] // block
    key_block = key_tokens[::block] // block
    diagonals = here * query_blocks + jnp.arange(query_blocks, dtype=jnp.int32)
    labels = jnp.arange(16, dtype=jnp.int32)
    tables, positions, masks, seens = [], [], [], []
    for tree in range(trees):
        row = after_all((parents[tree], seg_len[tree]), hops[min(tree, len(hops) - 1)])
        reaches, starts_at, ends_at, before = tree_tables(*row)
        seg_count = ends_at.shape[0]
        extra = 16 - seg_count
        reach16 = jnp.pad(reaches, ((0, extra), (0, extra)))
        starts16 = jnp.pad(starts_at, (0, extra))
        before16 = jnp.pad(before, (0, extra))
        ends16 = jnp.pad(ends_at, (0, extra), constant_values=2**30)
        own_seg = jnp.sum((own_tokens[:, None] >= ends_at[None, :]).astype(jnp.int32), axis=1)
        key_seg = jnp.sum((key_tokens[:, None] >= ends_at[None, :]).astype(jnp.int32), axis=1)
        member = own_seg[None, :] == labels[:, None]
        positions.append(
            own_tokens + jnp.sum(jnp.where(member, (before16 - starts16)[:, None], 0), axis=0)
        )
        seen_by = jnp.sum(
            jnp.where(member[:, None, :], reach16.astype(jnp.int32)[:, :, None], 0), axis=0
        )
        masks.append(jnp.where(seen_by > 0, 0.0, NEG).astype(BF16))
        lanes = jnp.arange(128, dtype=jnp.int32)
        key_seg_all = jnp.concatenate([key_seg, jnp.full((block,), seg_count, jnp.int32)])
        hot = (lanes[None, :] == key_seg_all[:, None]) | ((lanes >= 16) & (lanes < 19))[None, :]
        hot = hot.astype(BF16)

        def holds(blocks):
            low = blocks[:, None] * block
            return ((starts_at[None, :] < low + block) & (ends_at[None, :] > low)).astype(F32)

        linked = dot(dot(holds(own_block), reaches.astype(F32)), holds(key_block), 1, 1) > 0.5
        seen = linked & (key_block[None, :] < own_block[:, None])
        rank = jnp.cumsum(seen.astype(jnp.int32), axis=1) - 1
        slots = jnp.arange(key_blocks + 2, dtype=jnp.int32)
        index = jnp.arange(key_blocks, dtype=jnp.int32)
        chosen = seen[:, :, None] & (rank[:, :, None] == slots[None, None, :])
        lists = key_blocks + jnp.sum(
            jnp.where(chosen, index[None, :, None] - key_blocks, 0), axis=1
        )
        counts = jnp.sum(seen.astype(jnp.int32), axis=1)
        tables.append((counts, lists, diagonals, hot))
        on_diagonal = index[None, :] == diagonals[:, None]
        seens.append(jnp.where(on_diagonal, 2, seen.astype(jnp.int32)))
    position = jnp.concatenate(positions)
    (position,) = after_all((position,), hops[-2])
    angles = rope_angles(position, HEAD_SIZE)
    cosine, sine = jnp.cos(angles), jnp.sin(angles)

    inner_a, query, key_value = project(
        first_in, other_in, gain_a[None], w_attn, cosine, sine, head_cols, 2 * kv_cols,
        math.gcd(rows, 256),
    )
    query, key_value = after_all((query, key_value), down_hop)
    kv_rings = [
        Gather(ring, [key_value[tree * chip_rows : (tree + 1) * chip_rows]], True)
        for tree in range(trees)
    ]
    (out_grad,) = after_all((out_grad,), (key_value,))
    other_grad = other_core(out_grad)
    while kv_rings[0].step < chips // 2:
        mark, kv_hop = kv_hop if kv_rings[0].step else None, kv_rings[0].hop()
    kv_hop = kv_rings[1].hop(*mark)
    units_ring = Gather(ring, [units_piece])
    units_hop = units_ring.hop(*kv_rings[0].rightward, *kv_rings[0].leftward) + kv_hop
    kvs = [kv_rings[0].finish()[0].reshape(chips, 1, chip_rows, 2 * kv_cols)]

    def core_sum(own, other):
        return own.astype(F32) + other_core(other.astype(BF16)).astype(F32)

    def laid(buffer, value, tree):
        return lax.dynamic_update_slice(buffer, value[None], (tree, 0, 0))

    mixes, lses, middles, inners, normeds_f, scales_f, lows = [], [], [], [], [], [], []
    for tree in range(trees):
        mixed, lse = attend(tree, tables[tree], query, masks[tree], kvs[tree], rep, block)
        (mixed,) = after_all((mixed,), units_hop)
        part_hop = ()
        if tree == 0:
            while kv_rings[1].step < chips // 2 - 1:
                kv_hop = kv_rings[1].hop(mixed)
            last_hop = kv_rings[1].hop()
            down_hop = down_ring.hop(*kv_hop)
            units_hop = units_ring.hop(*last_hop)
        else:
            units_ring.hop(mixed)
            part_hop = down_hop
        mixes.append(mixed)
        lses.append(lse)
        (part,) = after_all((dot(mixed, w_o, 0, 1),), part_hop)
        lows.append(core_sum(part[:rows], part[rows:]).astype(BF16))
        if tree == 0:
            arrived = other_half(lows[0])
            units_hop += (arrived,)
            (query,) = after_all((query,), lows)
            kvs.append(kv_rings[1].finish()[0].reshape(chips, 1, chip_rows, 2 * kv_cols))
    arrived = [after_all((arrived,), lows[1:])[0]] + [other_half(low) for low in lows[1:]]
    layer_in, out_grad, *turns = after_all((layer_in, out_grad, cosine, sine), lows)
    scale_a = row_scale_of(layer_in.astype(F32))
    grad_low = jnp.concatenate([out_grad, other_grad], axis=1).reshape(trees * chip_rows, width)
    cosine_rows, sine_rows = (table.T[:, None, :] for table in turns)
    for tree in range(trees):
        rows_in = layer_in[tree].astype(F32)
        middle = rows_in + (lows[tree].astype(F32) + arrived[tree].astype(F32))
        scale_f = row_scale_of(middle)
        normed_f = middle * scale_f
        inner = (normed_f * gain_f).astype(BF16)
        inners += [inner, other_core(inner)]
        middles.append(middle)
        scales_f.append(scale_f)
        normeds_f.append(normed_f)
    inner_f = jnp.concatenate(inners, axis=0)

    (w_units,) = units_ring.finish(*arrived[1:], grad_low, cosine_rows, sine_rows, scale_a)
    w_units = w_units.reshape(width, -1)
    down_hop = ()
    while down_ring.step < chips // 2 - 1:
        down_hop += down_ring.hop(*arrived[1:])
    hidden, gate_slope, activated = after_all(hidden_units(inner_f, w_units), down_hop)
    down_hop = down_ring.hop(hidden)
    down_terms, grad_low = after_all((unit_grads(grad_low, hidden), grad_low), down_hop)
    (w_d,) = down_ring.finish()
    w_d = w_d.reshape(width, -1)
    (grad_low,) = after_all((grad_low,), (down_terms,))
    grad_gate, grad_up = back_hidden(grad_low, w_d, gate_slope, activated)

    def pieces(term):
        return term.astype(BF16).reshape(chips, width // chips, -1)

    spans = [slice(tree * chip_rows, (tree + 1) * chip_rows) for tree in range(trees)]
    down_ring = Reduce(ring, [pieces(down_terms)])
    down_hop = down_ring.hop()
    core_sums = []
    (grad_gate,) = after_all((grad_gate,), (down_ring.terms[0],))
    for tree in range(trees):
        part = back_units(tree, chip_rows, [grad_gate, grad_up], w_units, [0, 1])
        part = after_all(part, down_hop)
        down_hop = down_ring.hop(part[0])
        (grad_gate,) = after_all((grad_gate,), part)
        core_sums.append(core_sum(*part))
    lows = unit_lows = [own.astype(BF16) for own in core_sums]
    arrived = [other_half(lows[0])]
    inner_f, hidden = after_all((inner_f, hidden), lows)
    units_terms = unit_grads(inner_f, grad_gate, grad_up)
    units_terms, arrived[0] = after_all((units_terms, arrived[0]), down_hop)
    arrived.append(other_half(after_all(lows[1:], arrived)[0]))
    units_ring = Reduce(ring, [pieces(units_terms)])
    units_hop = units_ring.hop() + down_ring.hop(units_terms)
    arrived[0] = after_all(arrived[:1], (units_terms,))[0]

    grads_middle, grads_low = [], []

    def backward_norm(tree):
        grad_inner = lows[tree].astype(F32) + arrived[tree].astype(F32)
        grad_middle = out_grad[tree].astype(F32) + norm_back(
            grad_inner * gain_f, normeds_f[tree], scales_f[tree]
        )
        low = grad_middle.astype(BF16)
        grads_middle.append(grad_middle)
        grads_low.append(low)
        return jnp.concatenate([low, other_core(low)], axis=0)

    mid_lows, out_lows, out_arrived = [backward_norm(0)], [], []
    grads_qkv = []

    def back_part(tree, kv_sums):
        rows_of = (cosine_rows[spans[tree]], -sine_rows[spans[tree]])
        parts = grad_queries[groups * tree : groups * (tree + 1)]
        for group in range(groups):
            kv_sum = kv_sums[:, 128 * group : 128 * (group + 1)]
            grad_k = kv_sum[:, None, :HEAD_SIZE]
            half = HEAD_SIZE // 2
            first, second = turn(grad_k[..., :half], grad_k[..., half:], *rows_of)
            kv_parts = [first[:, 0], second[:, 0], kv_sum[:, HEAD_SIZE:]]
            parts.append(jnp.concatenate(kv_parts, axis=1).astype(BF16))
        grad_qkv = jnp.concatenate(parts, axis=1)
        grads_qkv.append(grad_qkv)
        part = dot(grad_qkv, w_qkv, 1, 1)
        return core_sum(part[:rows], part[rows:]).astype(BF16)

    grad_queries, grad_kvs = [], []
    for tree in range(trees):
        grad_mixed = dot(w_o, mid_lows[tree], 0, 1).astype(BF16)
        for group in range(groups):
            grad_query, grad_kv = attend_back(
                tree,
                group,
                seens[tree],
                tables[tree][3],
                query,
                masks[tree],
                mixes[tree],
                grad_mixed,
                lses[tree],
                kvs[tree],
                cosine,
                sine,
                rep,
                block,
                grad_kvs[-1] if group else None,
            )
            grad_query, grad_kv = after_all((grad_query, grad_kv), units_hop)
            grad_queries.append(grad_query)
            grad_kvs.append(grad_kv)
            units_hop = ()
            if units_ring.left > 0 and group < groups - 1:
                units_hop = units_ring.hop(grad_query)
            (grad_mixed,) = after_all((grad_mixed,), (grad_query,))
            if tree == 0 and group == 0:
                (hidden,) = after_all((hidden,), (grad_query,))
                out_parts = [
                    back_units(tree, chip_rows, [hidden], w_d, [0]) for tree in range(trees)
                ]
                out_parts[0] = after_all(out_parts[0], arrived[1:])
                out_lows = [core_sum(*part).astype(BF16) for part in out_parts]
                (grad_mixed,) = after_all((grad_mixed,), out_lows)
                out_arrived.append(other_half(out_lows[0]))
                units_hop += tuple(out_arrived)
            elif tree and group < groups - 1:
                while kv_ring.left > 0:
                    units_hop += kv_ring.hop(grad_query)
        if tree == 0:
            kv_ring = Reduce(ring, grad_kvs[-1:])
            kv_ring.hop()
            arrived[-1] = after_all(arrived[-1:], (grad_query,))[0]
            mid_lows.append(backward_norm(1))
            kv_hop = kv_ring.hop()
            out_terms = pieces(
                dot(jnp.concatenate(mid_lows, axis=0), jnp.concatenate(mixes, axis=1), 0, 1)
            )
            mid_lows[1] = after_all(mid_lows[1:], (out_terms, *kv_hop))[0]
            out_arrived.append(other_half(after_all(out_lows[1:], (grad_query,))[0]))
            units_hop += units_ring.hop(*kv_hop) + kv_ring.hop(out_terms)
            units_hop += tuple(out_arrived[1:])
    out_arrived = after_all(out_arrived, (grad_queries[-1],))
    (down_sum,), (units_sum,) = down_ring.finish(), units_ring.finish()
    outputs = unwritten(out_terms, (trees, rows, width))
    out_arrived = after_all(out_arrived, (grad_queries[-1],))
    for tree in range(trees):
        summed = out_lows[tree].astype(F32) + out_arrived[tree].astype(F32)
        outputs = laid(outputs, (middles[tree] + summed).astype(BF16), tree)

    (layer_in,) = after_all((layer_in,), (grad_queries[-1],))

    def normed_rows(tree, *others):
        return after_all((layer_in,), others)[0][tree].astype(F32) * scale_a[tree]

    down_grad = row_grad(down_sum)
    lows = [back_part(0, kv_ring.finish()[0])]
    arrived = [other_half(lows[0])]
    (kv_terms,) = after_all(grad_kvs[-1:], lows)
    (kv_sums,) = after_all(ring_sum([kv_terms], 1), arrived)
    lows.append(back_part(1, kv_sums))
    (inner_a,) = after_all((inner_a,), (grads_qkv[-1],))
    gate_grad, up_grad = (
        column_grad(part) for part in jnp.split(units_sum, 2, axis=1)
    )
    gain_terms = jnp.stack(
        [
            sum(jnp.sum(low * normed_rows(i, lows[0]), axis=0) for i, low in enumerate(lows)),
            sum(jnp.sum(low * normeds_f[i], axis=0) for i, low in enumerate(unit_lows)),
        ]
    )
    gain_terms = jnp.moveaxis(gain_terms.astype(BF16).reshape(2, chips, width // chips), 1, 0)
    gain_terms = jnp.pad(gain_terms, ((0, 0), (0, 30), (0, 0)))
    term_qkv = unit_grads(inner_a, jnp.concatenate(grads_qkv, axis=0))
    qkv_sum, out_sum, gain_sums, theirs = ring_sum(
        [pieces(term_qkv), out_terms, gain_terms], 2, lows[1]
    )
    arrived.append(theirs)
    out_proj_grad = row_grad(out_sum)
    kv_parts = qkv_sum[:, head_cols:].reshape(-1, groups, 2, HEAD_SIZE)
    key_sum, value_sum = (kv_parts[:, :, i].reshape(-1, kv_cols) for i in range(2))

    keep, give = split_by_core(gain_sums[:8], 1)
    gain_sums = keep + other_core(give)
    gain_sums = gain_sums + other_half(gain_sums)
    gain_a_grad, gain_f_grad = gain_sums[0], gain_sums[1]
    input_grad = unwritten(scale_a, (trees, rows, width))
    for tree in range(trees):
        grad_inner = lows[tree].astype(F32) + arrived[tree].astype(F32)
        normed_a = normed_rows(tree, arrived[1])
        input_grad = laid(
            input_grad,
            grads_middle[tree] + norm_back(grad_inner * gain_a, normed_a, scale_a[tree]),
            tree,
        )

    return (
        outputs,
        input_grad,
        gain_a_grad,
        column_grad(qkv_sum[:, :head_cols]),
        column_grad(key_sum),
        column_grad(value_sum),
        out_proj_grad,
        gain_f_grad,
        gate_grad,
        up_grad,
        down_grad,
    )


def solution(mesh):
    devices = mesh.devices
    mesh = Mesh(devices.reshape(-1, 2, devices.shape[1]), ("zy", "core", "tp"))
    fsdp = ("zy", "core")
    specs = (
        P(fsdp),
        P(fsdp, "tp"),
        P(fsdp, "tp"),
        P(fsdp, "tp"),
        P("tp", fsdp),
        P(fsdp),
        P(fsdp, "tp"),
        P(fsdp, "tp"),
        P("tp", fsdp),
    )
    tokens = P(None, fsdp, None)
    return jax.shard_map(
        shards,
        mesh=mesh,
        in_specs=(tokens, tokens, P(), P()) + specs,
        out_specs=(tokens, tokens) + specs,
        check_vma=False,
    )
```
